32 devices in a mesh: groups: 2 (over y), seq: 4 (over z), fsdp: 4 (over x, core).
Axes of the slice: x: 2, y: 2, z: 4, core: 2. Of those that a mesh axis runs over, the one named last changes fastest.
Arguments:
- normed_layer_input: bfloat16 [1024, 8192], P(('groups', 'seq'), 'fsdp'), parts along dimension 0, may hold values from -6 to 6
- frozen_query_rows: bfloat16 [1024, 4096], P(('groups', 'seq'), 'fsdp'), parts along dimension 0, may hold values from -16 to 16
- frozen_key_rows: bfloat16 [1024, 512], P(('groups', 'seq'), 'fsdp'), parts along dimension 0, may hold values from -16 to 16
- frozen_value_rows: bfloat16 [1024, 512], P(('groups', 'seq'), 'fsdp'), parts along dimension 0, may hold values from -6 to 6
- output_gradient: bfloat16 [1024, 4096], P(('groups', 'seq'), 'fsdp'), parts along dimension 0, may hold values from -0.059814453 to 0.059814453
- segment: int32 [1024], P(('groups', 'seq')), parts along dimension 0, may hold values from 0 to 15, never falling along the last dimension, each value on 1 to 64 neighbouring positions
- adapter_down_weight: bfloat16 [8192, 32], P('fsdp'), may hold values from -0.0625 to 0.0625
- query_up_weight: bfloat16 [16, 4096], P(None, 'fsdp'), may hold values from -0.375 to 0.375
- value_up_weight: bfloat16 [16, 512], P(None, 'fsdp'), may hold values from -0.75 to 0.75
Outputs:
- grad_down: float32 [16384, 32], P(('groups', 'fsdp')), parts along dimension 0
- query_up_gradient: float32 [32, 4096], P('groups', 'fsdp'), parts along dimension 0
- value_up_gradient: float32 [32, 512], P('groups', 'fsdp'), parts along dimension 0
The draws below stay inside these ranges and needn't reach their ends.
There are 2 independent parts, one for each index of `groups`. The reference program is written for one: setup_inputs(seed, part) draws one part's arguments, and reference() takes and returns one part's arrays. A program takes and returns all parts, laid end to end along the dimension named above; an argument that names none is the same for every part. Nothing has to cross between parts.
Inputs may be any that keep to these rules, and one draw needn't show every extreme that they name: `segment`: document numbers never fall along the window; each document spans 1 to 64 consecutive tokens, and one spans exactly 64.
All inputs are finite; a program needn't handle non-finite values.
Results may differ from the reference program's by a relative error of at most 0.012.
The reference program's roundings to bfloat16 on the way count: a program that leaves them out, or rounds other values in their place, can miss the bound.
Values may be sent and summed in bfloat16 or wider, within the bound.
No kernel may reach another device: no remote copies, remote signals or barrier semaphores. Data moves between devices by JAX's collectives and lax.ppermute only.
A program may use at most 64 MiB of HBM per device.

```python
import math
import jax
import jax.numpy as jnp
import numpy as np
from jax import lax

MODEL_WIDTH = 8192
QUERY_HEADS = 32
KEY_VALUE_HEADS = 4
HEAD_SIZE = 128
ADAPTER_RANK = 16
WINDOW_TOKENS = 512


def draw_frozen_query_rows(key, part):
    rotary_base = jnp.clip(jax.random.normal(key, (WINDOW_TOKENS, QUERY_HEADS * HEAD_SIZE), jnp.float32), -6.0, 6.0)
    return rotary_base.astype(jnp.bfloat16)


def draw_frozen_key_rows(key, part):
    rotary_base = jnp.clip(jax.random.normal(key, (WINDOW_TOKENS, KEY_VALUE_HEADS * HEAD_SIZE), jnp.float32), -6.0, 6.0)
    return rotary_base.astype(jnp.bfloat16)


def steps_of(own_key, extent, split, smallest, largest):
    def one(position, parts):
        heights = jax.random.uniform(jax.random.fold_in(jax.random.fold_in(own_key, 6), position), (parts,), jnp.float32, smallest / len(split), largest / len(split))
        return jnp.repeat(jnp.exp(heights), extent[position] // parts).reshape((-1,) + (1,) * (len(extent) - position - 1))

    gain = one(*split[0])
    for cut in split[1:]:
        gain = gain * one(*cut)
    return gain


def split_up(amount, total, limit, slope):
    loads = [(1 << 20) // math.isqrt(standing ** slope) + 1 for standing in range(2, amount + 1)]
    spare, counts = total - limit - (amount - 1), [1] * (amount - 1)
    while spare > 0:
        movable = [i for i in range(amount - 1) if counts[i] < limit]
        mass, left = sum([loads[i] for i in movable]), spare
        for i in movable:
            addition = min(limit - counts[i], max(1, left * loads[i] // mass), spare)
            counts[i] = counts[i] + addition
            spare = spare - addition
    return np.array([limit] + counts)


def ragged_sizes(rng, number_of, total, reach, slope):
    if number_of == 2:
        one = jax.random.randint(rng, (), max(1, total - reach), min(reach, total - 1) + 1)
        return jnp.stack([one, total - one])
    tallies = jnp.asarray(split_up(number_of, total, reach, slope), jnp.int32)
    couples = (number_of - 1) // 2
    donor, receiver = tallies[1:1 + 2 * couples:2], tallies[2:2 + 2 * couples:2]
    slack = jnp.minimum(donor - 1, reach - receiver)
    passed = jax.random.randint(jax.random.fold_in(rng, 1), (couples,), 0, 1 << 20) % (slack + 1)
    tallies = tallies.at[1:1 + 2 * couples:2].set(donor - passed).at[2:2 + 2 * couples:2].set(receiver + passed)
    return tallies[jax.random.permutation(jax.random.fold_in(rng, 2), number_of)]


def gaussian(stream_key, shape, spread, reach, pieces=(), held_as=jnp.bfloat16):
    values = jax.random.normal(stream_key, shape, jnp.float32) * spread
    if len(pieces) > 0:
        values = steps_of(stream_key, shape, pieces, -0.22, 0.18) * values
    return jnp.clip(values, min=-reach, max=reach).astype(held_as)


def setup_inputs(seed: int = 0, part: int = 0) -> dict:
    keys = jax.random.split(jax.random.key(seed), 10)
    part_splits = jax.random.split(jax.random.fold_in(keys[9], part), 10)
    return {
        "normed_layer_input": gaussian(part_splits[0], (WINDOW_TOKENS, MODEL_WIDTH), 1.0, 6.0, ((0, 4), (1, 4))),
        "frozen_query_rows": draw_frozen_query_rows(jax.random.fold_in(jax.random.fold_in(keys[9], part), 71), part),
        "frozen_key_rows": draw_frozen_key_rows(jax.random.fold_in(jax.random.fold_in(keys[9], part), 71), part),
        "frozen_value_rows": gaussian(part_splits[3], (WINDOW_TOKENS, KEY_VALUE_HEADS * HEAD_SIZE), 1.0, 6.0, ((0, 4), (1, 4))),
        "output_gradient": gaussian(part_splits[4], (WINDOW_TOKENS, QUERY_HEADS * HEAD_SIZE), 0.01, 0.059814453, ((0, 4), (1, 4))),
        "segment": jnp.searchsorted(jnp.cumsum(ragged_sizes(part_splits[5], max(16, WINDOW_TOKENS // 128), WINDOW_TOKENS, WINDOW_TOKENS // 8, 1)), jnp.arange(WINDOW_TOKENS), side="right").astype(jnp.int32),
        "adapter_down_weight": gaussian(keys[6], (MODEL_WIDTH, 2 * ADAPTER_RANK), MODEL_WIDTH ** -0.5, 0.0625, ((0, 4),)),
        "query_up_weight": gaussian(keys[7], (ADAPTER_RANK, QUERY_HEADS * HEAD_SIZE), (ADAPTER_RANK * 16) ** -0.5, 0.375, ((1, 4),)),
        "value_up_weight": gaussian(keys[8], (ADAPTER_RANK, KEY_VALUE_HEADS * HEAD_SIZE), (ADAPTER_RANK * 4) ** -0.5, 0.75, ((1, 4),)),
    }


ADAPTER_SCALE = 2.0
ROPE_BASE = 500000.0
NEG_FILL = -1e+30

def apply_rotation(vectors, token_positions, sign):
    half = vectors.shape[-1] // 2
    freqs = ROPE_BASE ** (-(2.0 * jnp.arange(half, dtype=jnp.float32)) / vectors.shape[-1])
    angles = token_positions.astype(jnp.float32)[:, None] * freqs[None, :]
    cosine = jnp.cos(angles)[:, None, :]
    sine = sign * jnp.sin(angles)[:, None, :]
    first = vectors[..., :half]
    second = vectors[..., half:]
    return jnp.concatenate([first * cosine - second * sine, second * cosine + first * sine], axis=-1)

def reference(normed_layer_input, frozen_query_rows, frozen_key_rows, frozen_value_rows, output_gradient, segment, adapter_down_weight, query_up_weight, value_up_weight):
    sequence_length = normed_layer_input.shape[0]
    heads_per_group = QUERY_HEADS // KEY_VALUE_HEADS
    inv_root = 1.0 / math.sqrt(HEAD_SIZE)
    adapter_product = jnp.dot(normed_layer_input, adapter_down_weight, preferred_element_type=jnp.float32).astype(jnp.bfloat16)
    query_adapter_codes = adapter_product[:, :ADAPTER_RANK]
    value_adapter_codes = adapter_product[:, ADAPTER_RANK:]
    token_positions = jnp.arange(sequence_length, dtype=jnp.int32)
    rotated_query = frozen_query_rows.astype(jnp.float32) + ADAPTER_SCALE * jnp.dot(query_adapter_codes, query_up_weight, preferred_element_type=jnp.float32)
    rotated_query = apply_rotation(rotated_query.reshape(sequence_length, QUERY_HEADS, HEAD_SIZE), token_positions, 1.0).astype(jnp.bfloat16)
    rotated_keys = apply_rotation(frozen_key_rows.astype(jnp.float32).reshape(sequence_length, KEY_VALUE_HEADS, HEAD_SIZE), token_positions, 1.0).astype(jnp.bfloat16)
    value_rows = (frozen_value_rows.astype(jnp.float32) + ADAPTER_SCALE * jnp.dot(value_adapter_codes, value_up_weight, preferred_element_type=jnp.float32)).astype(jnp.bfloat16)
    value_rows = value_rows.reshape(sequence_length, KEY_VALUE_HEADS, HEAD_SIZE)
    grads_out = output_gradient.reshape(sequence_length, QUERY_HEADS, HEAD_SIZE)
    block = math.gcd(sequence_length, 512)

    def single_group(index):
        q_group = lax.dynamic_slice_in_dim(rotated_query, index * heads_per_group, heads_per_group, 1)
        o_group = lax.dynamic_slice_in_dim(grads_out, index * heads_per_group, heads_per_group, 1)
        k_one = lax.dynamic_index_in_dim(rotated_keys, index, 1, keepdims=False)
        v_one = lax.dynamic_index_in_dim(value_rows, index, 1, keepdims=False)
        dq_parts = []
        dv_total = jnp.zeros((sequence_length, HEAD_SIZE), jnp.float32)
        for start in range(0, sequence_length, block):
            stop = start + block
            q_blk = q_group[start:stop].astype(jnp.float32)
            o_blk = o_group[start:stop].astype(jnp.float32)
            k_pre = k_one[:stop].astype(jnp.float32)
            v_pre = v_one[:stop].astype(jnp.float32)
            scores = jnp.einsum('qhd,kd->qhk', q_blk, k_pre) * inv_root
            allowed = (token_positions[:stop][None, :] <= token_positions[start:stop][:, None]) & (segment[:stop][None, :] == segment[start:stop][:, None])
            scores = jnp.where(allowed[:, None, :], scores, NEG_FILL)
            top = lax.optimization_barrier(jnp.max(scores, axis=-1, keepdims=True))
            expo = jnp.exp(scores - top)
            weights = expo / lax.optimization_barrier(jnp.sum(expo, axis=-1, keepdims=True))
            weights_b = weights.astype(jnp.bfloat16)
            dprob = jnp.einsum('qhd,kd->qhk', o_blk, v_pre)
            delta = lax.optimization_barrier(jnp.sum(weights * dprob, axis=-1, keepdims=True))
            dscore = (weights * (dprob - delta) * inv_root).astype(jnp.bfloat16)
            dq_parts.append(jnp.einsum('qhk,kd->qhd', dscore.astype(jnp.float32), k_pre))
            dv_total = dv_total.at[:stop].add(jnp.einsum('qhk,qhd->kd', weights_b.astype(jnp.float32), o_blk))
        return (jnp.concatenate(dq_parts, axis=0), dv_total)
    query_gradient_full, value_gradient_full = lax.map(single_group, jnp.arange(KEY_VALUE_HEADS, dtype=jnp.int32))
    dq = jnp.transpose(query_gradient_full, (1, 0, 2, 3)).reshape(sequence_length, QUERY_HEADS, HEAD_SIZE)
    query_gradient_rows = apply_rotation(dq, token_positions, -1.0).astype(jnp.bfloat16).reshape(sequence_length, QUERY_HEADS * HEAD_SIZE)
    value_gradient_rows = jnp.transpose(value_gradient_full, (1, 0, 2)).reshape(sequence_length, KEY_VALUE_HEADS * HEAD_SIZE)
    query_code_gradient = ADAPTER_SCALE * jnp.dot(query_gradient_rows, query_up_weight.T, preferred_element_type=jnp.float32)
    value_code_gradient = ADAPTER_SCALE * jnp.dot(value_gradient_rows, value_up_weight.astype(jnp.float32).T, precision=lax.Precision.HIGHEST)
    dlow = jnp.concatenate([query_code_gradient, value_code_gradient], axis=1).astype(jnp.bfloat16)
    grad_down = jnp.dot(normed_layer_input.T, dlow, preferred_element_type=jnp.float32)
    query_up_gradient = ADAPTER_SCALE * jnp.dot(query_adapter_codes.T, query_gradient_rows, preferred_element_type=jnp.float32)
    value_up_gradient = ADAPTER_SCALE * jnp.dot(value_adapter_codes.astype(jnp.float32).T, value_gradient_rows, precision=lax.Precision.HIGHEST)
    return (grad_down, query_up_gradient, value_up_gradient)
```

```python
import functools
import math

import jax
import jax.numpy as jnp
from jax import lax
from jax.experimental import pallas as pl
from jax.experimental.pallas import tpu as pltpu
from jax.sharding import PartitionSpec as P

HEAD = 128
HALF = HEAD // 2
RANK = 16
SCALE = 2.0
ROPE_BASE = 500000.0
NEG_FILL = -1e30
INV_ROOT = 1.0 / math.sqrt(HEAD)
F32 = jnp.float32
BF16 = jnp.bfloat16
EXACT = lax.Precision.HIGHEST
LIMIT = 50 * 1024 * 1024


def dot(left, right, left_dim, right_dim, precision=None):
    return lax.dot_general(
        left,
        right,
        (((left_dim,), (right_dim,)), ((), ())),
        precision=precision,
        preferred_element_type=F32,
    )


def call(kernel, out_shapes, scratch=(), flops=1 << 20):
    return pl.pallas_call(
        kernel,
        out_shape=[jax.ShapeDtypeStruct(s, d) for s, d in out_shapes],
        scratch_shapes=list(scratch),
        compiler_params=pltpu.CompilerParams(vmem_limit_bytes=LIMIT),
        cost_estimate=pl.CostEstimate(flops=flops, bytes_accessed=1 << 20, transcendentals=0),
    )


def lowrank_kernel(send, x_ref, a_ref, k_ref, v_ref, seg_ref, part_ref, pack_ref):
    part_ref[...] = dot(a_ref[...], x_ref[...], 1, 1)
    tok = k_ref.shape[0]
    pack_ref[0:send] = k_ref[tok - send : tok]
    pack_ref[send : 2 * send] = v_ref[tok - send : tok]
    pack_ref[2 * send :] = jnp.broadcast_to(seg_ref[...].astype(F32), (16, tok)).astype(BF16)


def rotate_rows(u, cos, sin):
    return u * cos + pltpu.roll(u, HALF, 1) * sin


def scores_kernel(
    halo, send, blocks, heads,
    low_ref, q_ref, k_ref, o_ref, seg_ref, pack_ref, base_ref, cos_ref, sin_ref, wq_ref, wv_ref,
    w_ref, kt_ref, dv_ref, code_ref, back_ref, bias_ref, keys_ref,
):
    tok = q_ref.shape[0]
    keys = halo + tok
    low = low_ref[...].astype(BF16)
    cos, sin = cos_ref[...], sin_ref[...]
    cos2 = jnp.concatenate([cos, cos], axis=1)
    sin2 = jnp.concatenate([-sin, sin], axis=1)
    raw = [pack_ref[b, 0:send] for b in range(blocks)] + [k_ref[...]]
    keys_ref[...] = rotate_rows(jnp.concatenate(raw, axis=0).astype(F32), cos2, sin2).astype(BF16)
    key_rows = keys_ref[...]
    kt_ref[...] = key_rows.astype(F32).T.astype(BF16)
    seg_here = seg_ref[...].astype(F32)
    cols = []
    for b in range(blocks):
        row = pack_ref[b, 2 * send : 2 * send + 16].astype(F32)[0:1]
        cols.append(jnp.broadcast_to(row, (tok, tok)).T[tok - send :])
    cols.append(jnp.broadcast_to(seg_here, (tok, tok)).T)
    seg_col = jnp.concatenate(cols, axis=0)
    offset = lax.broadcasted_iota(jnp.int32, (keys, tok), 0) - halo
    query = lax.broadcasted_iota(jnp.int32, (keys, tok), 1)
    allowed = (offset <= query) & (offset + base_ref[0] >= 0) & (seg_col == seg_here)
    bias_ref[...] = jnp.where(allowed, 0.0, NEG_FILL)
    q0 = q_ref[...].astype(F32) + SCALE * dot(low[:RANK], wq_ref[...], 0, 0)
    cos_here, sin_here = cos2[halo:], sin2[halo:]
    dv = jnp.zeros((keys, HEAD), F32)
    for h in range(heads):
        cut = slice(h * HEAD, (h + 1) * HEAD)
        qr = rotate_rows(q0[:, cut], cos_here, sin_here).astype(BF16)
        s = dot(key_rows, qr, 1, 1) * INV_ROOT + bias_ref[...]
        e = jnp.exp(s - jnp.max(s, axis=0, keepdims=True))
        w = e * (1.0 / jnp.sum(e, axis=0, keepdims=True))
        w_ref[h] = w
        dv = dv + dot(w.astype(BF16), o_ref[:, cut], 1, 0)
    dv_ref[...] = dv
    wv = wv_ref[...].astype(F32)
    code_ref[...] = SCALE * dot(wv, dv[halo:], 1, 1, EXACT)
    for b in range(blocks):
        part = dv[b * send : (b + 1) * send]
        if send < tok:
            part = jnp.concatenate([jnp.zeros((tok - send, HEAD), F32), part], axis=0)
        back_ref[b] = SCALE * dot(wv, part, 1, 1, EXACT)


def grads_kernel(
    halo, send, blocks, heads,
    low_ref, lowv_ref, v_ref, pack_ref, o_ref, w_ref, kt_ref, dv_ref, cost_ref, sint_ref, wq_ref, wv_ref,
    code_ref, up_ref, vals_ref, qg_ref,
):
    tok = o_ref.shape[0]
    low = low_ref[...].astype(BF16)
    wv = wv_ref[...]

    def values(rows, codes):
        return (rows.astype(F32) + SCALE * dot(codes, wv, 0, 0)[tok - rows.shape[0] :]).astype(BF16)

    for b in range(blocks):
        vals_ref[b * send : (b + 1) * send] = values(pack_ref[b, send : 2 * send], lowv_ref[b])
    vals_ref[halo:] = values(v_ref[...], low[RANK:])
    vals = vals_ref[...]
    kt = kt_ref[...]
    cos, sin = cost_ref[...], sint_ref[...]
    for h in range(heads):
        cut = slice(h * HEAD, (h + 1) * HEAD)
        dp = dot(vals, o_ref[:, cut], 1, 1)
        w = w_ref[h]
        delta = jnp.sum(w * dp, axis=0, keepdims=True)
        ds = (w * (dp - delta) * INV_ROOT).astype(BF16)
        dq = dot(kt, ds, 1, 0)
        first, second = dq[:HALF], dq[HALF:]
        qg_ref[h * HEAD : h * HEAD + HALF] = (first * cos + second * sin).astype(BF16)
        qg_ref[h * HEAD + HALF : (h + 1) * HEAD] = (second * cos - first * sin).astype(BF16)
    qg = qg_ref[...]
    code_ref[...] = SCALE * dot(wq_ref[...], qg, 1, 0)
    up_q = SCALE * dot(low[:RANK], qg, 1, 1)
    dv = dv_ref[...]
    up_v = dot(low[RANK:].astype(F32), dv[halo:], 1, 0, EXACT)
    for b in range(blocks):
        codes = lowv_ref[b].astype(F32)
        part = dv[b * send : (b + 1) * send]
        if send < tok:
            part = jnp.concatenate([jnp.zeros((tok - send, HEAD), F32), part], axis=0)
        up_v = up_v + dot(codes, part, 1, 0, EXACT)
    up_ref[:, : heads * HEAD] = up_q.astype(up_ref.dtype)
    up_ref[:, heads * HEAD :] = (SCALE * up_v).astype(up_ref.dtype)


def down_kernel(dl_ref, x_ref, part_ref):
    part_ref[...] = dot(dl_ref[...], x_ref[...], 1, 0)


def pair_kernel(split, dl_ref, dlp_ref, x_ref, xp_ref, up_ref, upp_ref, send_ref):
    rows, wide = dl_ref.shape[0], x_ref.shape[1]
    part = dot(dl_ref[...], x_ref[...], 1, 0) + dot(dlp_ref[...], xp_ref[...], 1, 0)
    send_ref[:, :wide] = part.astype(BF16)
    up = (up_ref[...].astype(F32) + upp_ref[...].astype(F32)).astype(BF16)
    size = up.shape[1]
    send_ref[0:RANK, wide:] = up[:, :split]
    send_ref[RANK:rows, wide : wide + size - split] = up[:, split:]
    if 2 * split > size:
        send_ref[RANK:rows, wide + size - split :] = jnp.zeros((rows - RANK, 2 * split - size), BF16)


def final_kernel(split, mine_ref, other_ref, down_ref, upq_ref, upv_ref):
    wide = down_ref.shape[1]
    total = mine_ref[...].astype(F32) + other_ref[...].astype(F32)
    down_ref[...] = total[:, :wide]
    size = upq_ref.shape[1]
    upq_ref[:, :split] = total[:RANK, wide:]
    upq_ref[:, split:] = total[RANK:, wide : wide + size - split]
    upv_ref[...] = total[RANK:, wide + size - split : wide + size - split + HEAD]


def body(x, q, k, v, o, segment, a, wq, wv):
    tok, wide = x.shape
    seq_count = lax.axis_size("seq")
    fsdp_count = lax.axis_size("fsdp")
    seq_index = lax.axis_index("seq")
    heads = q.shape[1] // HEAD
    longest = tok * seq_count // 8
    blocks = -(-longest // tok)
    send = longest if blocks == 1 else tok
    halo = blocks * send
    keys = halo + tok
    paired = seq_count == 4 and fsdp_count == 4

    def swap(array, axis, bit):
        size = lax.axis_size(axis)
        return lax.ppermute(array, axis, [(i, i ^ bit) for i in range(size)])

    def shift(array, by):
        moves = [(i, i + by) for i in range(seq_count) if 0 <= i + by < seq_count]
        return lax.ppermute(array, "seq", moves)

    def cross(array):
        moves = [
            (s * fsdp_count + f, (s ^ 1) * fsdp_count + (f ^ 2))
            for s in range(seq_count)
            for f in range(fsdp_count)
        ]
        return lax.ppermute(array, ("seq", "fsdp"), moves)

    def sum_fsdp(array):
        if fsdp_count & (fsdp_count - 1):
            return lax.psum(array, "fsdp")
        bit = 1
        while bit < fsdp_count:
            array = array + swap(array, "fsdp", bit)
            bit *= 2
        return array

    seg_row = segment.reshape(1, tok)
    part, pack = call(
        functools.partial(lowrank_kernel, send),
        [((2 * RANK, tok), F32), ((2 * send + 16, tok), BF16)],
    )(x, a.T, k, v, seg_row)
    part, pack, x = lax.optimization_barrier((part, pack, x))
    if paired:
        x_pair = swap(x, "seq", 1)
    packs = jnp.stack([shift(pack, d) for d in range(blocks, 0, -1)])
    start = seq_index * tok
    base = start.reshape(1).astype(jnp.int32)
    freqs = ROPE_BASE ** (-(2.0 * jnp.arange(HALF, dtype=F32)) / HEAD)
    positions = (start - halo + jnp.arange(keys, dtype=jnp.int32)).astype(F32)
    angles = positions[:, None] * freqs[None, :]
    cos, sin = jnp.cos(angles), jnp.sin(angles)
    here = (start + jnp.arange(tok, dtype=jnp.int32)).astype(F32)
    angles_t = freqs[:, None] * here[None, :]
    cos_t, sin_t = jnp.cos(angles_t), jnp.sin(angles_t)

    low = sum_fsdp(part)
    low_v = low[RANK:].astype(BF16)
    lows = jnp.stack([shift(low_v, d) for d in range(blocks, 0, -1)])

    specs = [pl.BlockSpec(memory_space=pltpu.VMEM)] * 11
    specs[6] = pl.BlockSpec(memory_space=pltpu.SMEM)
    w, kt, dv, code_v, back = pl.pallas_call(
        functools.partial(scores_kernel, halo, send, blocks, heads),
        out_shape=[
            jax.ShapeDtypeStruct((heads, keys, tok), F32),
            jax.ShapeDtypeStruct((HEAD, keys), BF16),
            jax.ShapeDtypeStruct((keys, HEAD), F32),
            jax.ShapeDtypeStruct((RANK, tok), F32),
            jax.ShapeDtypeStruct((blocks, RANK, tok), F32),
        ],
        in_specs=specs,
        scratch_shapes=[pltpu.VMEM((keys, tok), F32), pltpu.VMEM((keys, HEAD), BF16)],
        compiler_params=pltpu.CompilerParams(vmem_limit_bytes=LIMIT),
    )(low, q, k, o, seg_row, packs, base, cos, sin, wq, wv)

    for b, d in enumerate(range(blocks, 0, -1)):
        code_v = code_v + shift(back[b], -d)
    code_q, up = call(
        functools.partial(grads_kernel, halo, send, blocks, heads),
        [((RANK, tok), F32), ((RANK, (heads + 1) * HEAD), BF16 if paired else F32)],
        [pltpu.VMEM((keys, HEAD), BF16), pltpu.VMEM((heads * HEAD, tok), BF16)],
    )(low, lows, v, packs, o, w, kt, dv, cos_t, sin_t, wq, wv)
    codes = jnp.concatenate([code_q, code_v], axis=0)

    if not paired:
        dlow = sum_fsdp(codes).astype(BF16)
        (down,) = call(down_kernel, [((2 * RANK, wide), F32)])(dlow, x)
        down, up = lax.psum((down, up), "seq")
        return down.T, up[:, : heads * HEAD], up[:, heads * HEAD :]

    up_pair = swap(up, "seq", 1)
    codes = codes + swap(codes, "fsdp", 1)
    dlow = (codes + swap(codes, "fsdp", 2)).astype(BF16)
    dlow_pair = (swap(codes, "seq", 1) + cross(codes)).astype(BF16)
    split = -(-(heads + 1) // 2) * HEAD
    (mine,) = call(functools.partial(pair_kernel, split), [((2 * RANK, wide + split), BF16)])(
        dlow, dlow_pair, x, x_pair, up, up_pair
    )
    other = swap(mine, "seq", 2)
    down, up_q, up_v = call(
        functools.partial(final_kernel, split),
        [((2 * RANK, wide), F32), ((RANK, heads * HEAD), F32), ((RANK, HEAD), F32)],
    )(mine, other)
    return down.T, up_q, up_v


def solution(mesh):
    rows = ("groups", "seq")
    in_specs = (
        P(rows, "fsdp"),
        P(rows, "fsdp"),
        P(rows, "fsdp"),
        P(rows, "fsdp"),
        P(rows, "fsdp"),
        P(rows),
        P("fsdp", None),
        P(None, "fsdp"),
        P(None, "fsdp"),
    )
    out_specs = (P(("groups", "fsdp"), None), P("groups", "fsdp"), P("groups", "fsdp"))
    return jax.shard_map(body, mesh=mesh, in_specs=in_specs, out_specs=out_specs, check_vma=False)
```

```python
import functools
import math

import jax
import jax.numpy as jnp
from jax import lax
from jax.experimental import pallas as pl
from jax.experimental.pallas import tpu as pltpu
from jax.sharding import PartitionSpec as P

HEAD = 128
HALF = HEAD // 2
RANK = 16
SCALE = 2.0
ROPE_BASE = 500000.0
NEG_FILL = -1e30
INV_ROOT = 1.0 / math.sqrt(HEAD)
F32 = jnp.float32
BF16 = jnp.bfloat16
EXACT = lax.Precision.HIGHEST
LIMIT = 40 * 1024 * 1024
FULL = 63 * 1024 * 1024


def dot(left, right, left_dim, right_dim, precision=None):
    return lax.dot_general(
        left,
        right,
        (((left_dim,), (right_dim,)), ((), ())),
        precision=precision,
        preferred_element_type=F32,
    )


def call(kernel, out_shapes, scratch=(), limit=LIMIT, cost=1, **specs):
    return pl.pallas_call(
        kernel,
        out_shape=[jax.ShapeDtypeStruct(s, d) for s, d in out_shapes],
        **specs,
        scratch_shapes=list(scratch),
        compiler_params=pltpu.CompilerParams(vmem_limit_bytes=limit),
        cost_estimate=pl.CostEstimate(flops=cost, bytes_accessed=cost, transcendentals=0),
    )


def lowrank_kernel(x_hbm, a_hbm, part_ref, x_ref, a_ref, sems):
    copies = [
        pltpu.make_async_copy(x_hbm, x_ref, sems.at[0]),
        pltpu.make_async_copy(a_hbm, a_ref, sems.at[1]),
    ]
    for copy in copies:
        copy.start()
    for copy in copies:
        copy.wait()
    part_ref[...] = dot(a_ref[...], x_ref[...], 1, 1)


def rotate_rows(u, cos, sin):
    return u * cos + pltpu.roll(u, HALF, 1) * sin


def wide_tables(cos, sin):
    return jnp.concatenate([cos, cos], axis=1), jnp.concatenate([-sin, sin], axis=1)


def column(row, tok):
    return jnp.broadcast_to(row, (tok, tok)).T


def project_kernel(
    heads,
    low_ref, q_ref, k_ref, v_ref, o_ref, seg_ref, cos_ref, sin_ref, wq_ref, wv_ref,
    qr_ref, kt_ref, s_ref, dp_ref, bias_ref,
):
    tok = q_ref.shape[0]
    low = low_ref[...].astype(BF16)
    cos, sin = wide_tables(cos_ref[...], sin_ref[...])
    keys = rotate_rows(k_ref[...].astype(F32), cos, sin)
    kt_ref[...] = keys.T.astype(BF16)
    keys = keys.astype(BF16)
    vals = (v_ref[...].astype(F32) + SCALE * dot(low[RANK:], wv_ref[...], 0, 0)).astype(BF16)
    seg_here = seg_ref[...].astype(F32)
    key = lax.broadcasted_iota(jnp.int32, (tok, tok), 0)
    query = lax.broadcasted_iota(jnp.int32, (tok, tok), 1)
    allowed = (key <= query) & (column(seg_here, tok) == seg_here)
    bias_ref[...] = jnp.where(allowed, 0.0, NEG_FILL)
    q0 = q_ref[...].astype(F32) + SCALE * dot(low[:RANK], wq_ref[...], 0, 0)
    for h in range(heads):
        cut = slice(h * HEAD, (h + 1) * HEAD)
        qr = rotate_rows(q0[:, cut], cos, sin).astype(BF16)
        qr_ref[h] = qr
        s_ref[h] = dot(keys, qr, 1, 1) * INV_ROOT + bias_ref[...]
        dp_ref[h] = dot(vals, o_ref[:, cut], 1, 1)


def softmax_kernel(
    send, blocks, heads,
    qr_ref, s_ref, o_ref, seg_ref, pack_ref, base_ref, cos_ref, sin_ref, wv_ref,
    w_ref, kt_ref, dv_ref, code_ref, back_ref, bias_ref, keys_ref,
):
    tok = qr_ref.shape[1]
    halo = send * blocks
    cos, sin = wide_tables(cos_ref[...], sin_ref[...])
    keys = jnp.concatenate([pack_ref[b, 0:send] for b in range(blocks)], axis=0)
    keys = rotate_rows(keys.astype(F32), cos, sin)
    kt_ref[...] = keys.T.astype(BF16)
    keys_ref[...] = keys.astype(BF16)
    seg_here = seg_ref[...].astype(F32)
    cols = []
    for b in range(blocks):
        row = pack_ref[b, 2 * send + RANK :].astype(F32)[0:1]
        cols.append(column(row, tok)[tok - send :])
    seg_col = jnp.concatenate(cols, axis=0)
    offset = lax.broadcasted_iota(jnp.int32, (halo, tok), 0)
    allowed = (offset + base_ref[0] >= halo) & (seg_col == seg_here)
    bias_ref[...] = jnp.where(allowed, 0.0, NEG_FILL)
    dv = jnp.zeros((halo + tok, HEAD), F32)
    for h in range(heads):
        far = dot(keys_ref[...], qr_ref[h], 1, 1) * INV_ROOT + bias_ref[...]
        s = jnp.concatenate([far, s_ref[h]], axis=0)
        e = jnp.exp(s - jnp.max(s, axis=0, keepdims=True))
        w = e * (1.0 / jnp.sum(e, axis=0, keepdims=True))
        w_ref[h] = w
        dv = dv + dot(w.astype(BF16), o_ref[:, h * HEAD : (h + 1) * HEAD], 1, 0)
    dv_ref[...] = dv
    wv = wv_ref[...].astype(F32)
    code_ref[...] = SCALE * dot(wv, dv[halo:], 1, 1, EXACT)
    for b in range(blocks):
        part = dv[b * send : (b + 1) * send]
        if send < tok:
            part = jnp.concatenate([jnp.zeros((tok - send, HEAD), F32), part], axis=0)
        back_ref[b] = SCALE * dot(wv, part, 1, 1, EXACT)


def grads_kernel(
    send, blocks, heads,
    low_ref, pack_ref, o_ref, w_ref, dp_ref, kt_ref, kth_ref, dv_ref, cost_ref, sint_ref, wq_ref, wv_ref,
    code_ref, up_ref, vals_ref, qg_ref,
):
    tok = o_ref.shape[0]
    halo = send * blocks
    low = low_ref[...].astype(BF16)
    wv = wv_ref[...]
    codes = [pack_ref[b, 2 * send : 2 * send + RANK] for b in range(blocks)]
    for b in range(blocks):
        rows = pack_ref[b, send : 2 * send].astype(F32)
        add = SCALE * dot(codes[b], wv, 0, 0)[tok - send :]
        vals_ref[b * send : (b + 1) * send] = (rows + add).astype(BF16)
    kt = jnp.concatenate([kth_ref[...], kt_ref[...]], axis=1)
    cos, sin = cost_ref[...], sint_ref[...]
    for h in range(heads):
        far = dot(vals_ref[...], o_ref[:, h * HEAD : (h + 1) * HEAD], 1, 1)
        dp = jnp.concatenate([far, dp_ref[h]], axis=0)
        w = w_ref[h]
        delta = jnp.sum(w * dp, axis=0, keepdims=True)
        ds = (w * (dp - delta) * INV_ROOT).astype(BF16)
        dq = dot(kt, ds, 1, 0)
        first, second = dq[:HALF], dq[HALF:]
        qg_ref[h * HEAD : h * HEAD + HALF] = (first * cos + second * sin).astype(BF16)
        qg_ref[h * HEAD + HALF : (h + 1) * HEAD] = (second * cos - first * sin).astype(BF16)
    qg = qg_ref[...]
    code_ref[...] = SCALE * dot(wq_ref[...], qg, 1, 0)
    up_q = SCALE * dot(low[:RANK], qg, 1, 1)
    dv = dv_ref[...]
    up_v = dot(low[RANK:].astype(F32), dv[halo:], 1, 0, EXACT)
    for b in range(blocks):
        part = dv[b * send : (b + 1) * send]
        if send < tok:
            part = jnp.concatenate([jnp.zeros((tok - send, HEAD), F32), part], axis=0)
        up_v = up_v + dot(codes[b].astype(F32), part, 1, 0, EXACT)
    up_ref[:, : heads * HEAD] = up_q.astype(up_ref.dtype)
    up_ref[:, heads * HEAD :] = (SCALE * up_v).astype(up_ref.dtype)


def down_kernel(dl_ref, x_ref, part_ref):
    part_ref[...] = dot(dl_ref[...], x_ref[...], 1, 0)


def pair_kernel(split, dl_ref, dlp_ref, x_ref, xp_ref, up_ref, upp_ref, send_ref):
    rows, wide = dl_ref.shape[0], x_ref.shape[1]
    part = dot(dl_ref[...], x_ref[...], 1, 0) + dot(dlp_ref[...], xp_ref[...], 1, 0)
    send_ref[:, :wide] = part.astype(BF16)
    up = (up_ref[...].astype(F32) + upp_ref[...].astype(F32)).astype(BF16)
    size = up.shape[1]
    send_ref[0:RANK, wide:] = up[:, :split]
    send_ref[RANK:rows, wide : wide + size - split] = up[:, split:]
    if 2 * split > size:
        send_ref[RANK:rows, wide + size - split :] = jnp.zeros((rows - RANK, 2 * split - size), BF16)


def final_kernel(split, mine_ref, other_ref, down_ref, upq_ref, upv_ref):
    wide = down_ref.shape[1]
    total = mine_ref[...].astype(F32) + other_ref[...].astype(F32)
    down_ref[...] = total[:, :wide]
    size = upq_ref.shape[1]
    upq_ref[:, :split] = total[:RANK, wide:]
    upq_ref[:, split:] = total[RANK:, wide : wide + size - split]
    upv_ref[...] = total[RANK:, wide + size - split : wide + size - split + HEAD]


def body(x, q, k, v, o, segment, a, wq, wv):
    tok, wide = x.shape
    seq_count = lax.axis_size("seq")
    fsdp_count = lax.axis_size("fsdp")
    seq_index = lax.axis_index("seq")
    heads = q.shape[1] // HEAD
    longest = tok * seq_count // 8
    blocks = -(-longest // tok)
    send = longest if blocks == 1 else tok
    halo = blocks * send
    keys = halo + tok
    paired = seq_count == 4 and fsdp_count == 4

    def swap(array, axis, bit):
        size = lax.axis_size(axis)
        return lax.ppermute(array, axis, [(i, i ^ bit) for i in range(size)])

    def shift(array, by):
        moves = [(i, (i + by) % seq_count) for i in range(seq_count)]
        return lax.ppermute(array, "seq", moves)

    def cross(array):
        moves = [
            (s * fsdp_count + f, (s ^ 1) * fsdp_count + (f ^ 2))
            for s in range(seq_count)
            for f in range(fsdp_count)
        ]
        return lax.ppermute(array, ("seq", "fsdp"), moves)

    def sum_fsdp(array):
        if fsdp_count & (fsdp_count - 1):
            return lax.psum(array, "fsdp")
        bit = 1
        while bit < fsdp_count:
            array = array + swap(array, "fsdp", bit)
            bit *= 2
        return array

    seg_row = segment.reshape(1, tok)
    hbm = pl.BlockSpec(memory_space=pltpu.HBM)
    (part,) = call(
        lowrank_kernel,
        [((2 * RANK, tok), F32)],
        [
            pltpu.VMEM((tok, wide), BF16),
            pltpu.VMEM((2 * RANK, wide), BF16),
            pltpu.SemaphoreType.DMA((2,)),
        ],
        limit=FULL,
        in_specs=[hbm, hbm],
    )(x, a.T)
    if paired:
        part, x = lax.optimization_barrier((part, x))
        x_pair = swap(x, "seq", 1)
    start = seq_index * tok
    base = start.reshape(1).astype(jnp.int32)
    freqs = ROPE_BASE ** (-(2.0 * jnp.arange(HALF, dtype=F32)) / HEAD)
    positions = (start - halo + jnp.arange(keys, dtype=jnp.int32)).astype(F32)
    angles = positions[:, None] * freqs[None, :]
    cos, sin = jnp.cos(angles), jnp.sin(angles)
    here = (start + jnp.arange(tok, dtype=jnp.int32)).astype(F32)
    angles_t = freqs[:, None] * here[None, :]
    cos_t, sin_t = jnp.cos(angles_t), jnp.sin(angles_t)

    low = sum_fsdp(part)
    seg_rows = jnp.broadcast_to(seg_row, (16, tok)).astype(BF16)
    pack = jnp.concatenate(
        [k[tok - send :], v[tok - send :], low[RANK:].astype(BF16), seg_rows], axis=0
    )
    packs = jnp.stack([shift(pack, d) for d in range(blocks, 0, -1)])
    qr, kt, s, dp = call(
        functools.partial(project_kernel, heads),
        [
            ((heads, tok, HEAD), BF16),
            ((HEAD, tok), BF16),
            ((heads, tok, tok), F32),
            ((heads, tok, tok), F32),
        ],
        [pltpu.VMEM((tok, tok), F32)],
    )(low, q, k, v, o, seg_row, cos[halo:], sin[halo:], wq, wv)
    specs = [pl.BlockSpec(memory_space=pltpu.VMEM)] * 9
    specs[5] = pl.BlockSpec(memory_space=pltpu.SMEM)
    w, kt_far, dv, code_v, back = call(
        functools.partial(softmax_kernel, send, blocks, heads),
        [
            ((heads, keys, tok), F32),
            ((HEAD, halo), BF16),
            ((keys, HEAD), F32),
            ((RANK, tok), F32),
            ((blocks, RANK, tok), F32),
        ],
        [pltpu.VMEM((halo, tok), F32), pltpu.VMEM((halo, HEAD), BF16)],
        in_specs=specs,
    )(qr, s, o, seg_row, packs, base, cos[:halo], sin[:halo], wv)
    for b, d in enumerate(range(blocks, 0, -1)):
        code_v = code_v + shift(back[b], -d)
    code_q, up = call(
        functools.partial(grads_kernel, send, blocks, heads),
        [((RANK, tok), F32), ((RANK, (heads + 1) * HEAD), BF16 if paired else F32)],
        [pltpu.VMEM((halo, HEAD), BF16), pltpu.VMEM((heads * HEAD, tok), BF16)],
        cost=6 << 20,
    )(low, packs, o, w, dp, kt, kt_far, dv, cos_t, sin_t, wq, wv)
    codes = jnp.concatenate([code_q, code_v], axis=0)

    if not paired:
        dlow = sum_fsdp(codes).astype(BF16)
        (down,) = call(down_kernel, [((2 * RANK, wide), F32)])(dlow, x)
        down, up = lax.psum((down, up), "seq")
        return down.T, up[:, : heads * HEAD], up[:, heads * HEAD :]

    up_pair = swap(up, "seq", 1)
    codes, x_pair = lax.optimization_barrier((codes, x_pair))
    codes = codes + swap(codes, "fsdp", 1)
    dlow = (codes + swap(codes, "fsdp", 2)).astype(BF16)
    dlow_pair = (swap(codes, "seq", 1) + cross(codes)).astype(BF16)
    split = -(-(heads + 1) // 2) * HEAD
    (mine,) = call(functools.partial(pair_kernel, split), [((2 * RANK, wide + split), BF16)])(
        dlow, dlow_pair, x, x_pair, up, up_pair
    )
    other = swap(mine, "seq", 2)
    down, up_q, up_v = call(
        functools.partial(final_kernel, split),
        [((2 * RANK, wide), F32), ((RANK, heads * HEAD), F32), ((RANK, HEAD), F32)],
    )(mine, other)
    return down.T, up_q, up_v


def solution(mesh):
    rows = ("groups", "seq")
    in_specs = (
        P(rows, "fsdp"),
        P(rows, "fsdp"),
        P(rows, "fsdp"),
        P(rows, "fsdp"),
        P(rows, "fsdp"),
        P(rows),
        P("fsdp", None),
        P(None, "fsdp"),
        P(None, "fsdp"),
    )
    out_specs = (P(("groups", "fsdp"), None), P("groups", "fsdp"), P("groups", "fsdp"))
    return jax.shard_map(body, mesh=mesh, in_specs=in_specs, out_specs=out_specs, check_vma=False)
```

```python
import functools
import math

import jax
import jax.numpy as jnp
from jax import lax
from jax.experimental import pallas as pl
from jax.experimental.pallas import tpu as pltpu
from jax.sharding import PartitionSpec as P

HEAD = 128
HALF = HEAD // 2
RANK = 16
SCALE = 2.0
ROPE_BASE = 500000.0
NEG_FILL = -1e30
INV_ROOT = 1.0 / math.sqrt(HEAD)
F32 = jnp.float32
BF16 = jnp.bfloat16
EXACT = lax.Precision.HIGHEST
LIMIT = 40 * 1024 * 1024
FULL = 55168 * 1024


def dot(left, right, left_dim, right_dim, precision=None):
    return lax.dot_general(
        left,
        right,
        (((left_dim,), (right_dim,)), ((), ())),
        precision=precision,
        preferred_element_type=F32,
    )


def call(kernel, out_shapes, scratch=(), limit=LIMIT, cost=1, **specs):
    return pl.pallas_call(
        kernel,
        out_shape=[jax.ShapeDtypeStruct(s, d) for s, d in out_shapes],
        **specs,
        scratch_shapes=list(scratch),
        compiler_params=pltpu.CompilerParams(vmem_limit_bytes=limit),
        cost_estimate=pl.CostEstimate(flops=cost, bytes_accessed=cost, transcendentals=0),
    )


def lowrank_kernel(x_hbm, a_hbm, part_ref, x_ref, a_ref, sems):
    pairs = [(x_hbm, x_ref), (a_hbm, a_ref)]
    copies = [pltpu.make_async_copy(src, dst, sems.at[i]) for i, (src, dst) in enumerate(pairs)]
    for copy in copies:
        copy.start()
    for copy in copies:
        copy.wait()
    part_ref[...] = dot(a_ref[...], x_ref[...], 1, 1)


def rotate_rows(u, cos, sin):
    return u * cos + pltpu.roll(u, HALF, 1) * sin


def wide_tables(cos, sin):
    return jnp.concatenate([cos, cos], axis=1), jnp.concatenate([-sin, sin], axis=1)


def column(row, tok):
    return jnp.broadcast_to(row, (tok, tok)).T


def project_kernel(
    heads,
    low_ref, q_ref, k_ref, v_ref, o_ref, seg_ref, cos_ref, sin_ref, wq_ref, wv_ref,
    qr_ref, kt_ref, s_ref, dp_ref, cost_ref, sint_ref, bias_ref,
):
    tok = q_ref.shape[0]
    low = low_ref[...].astype(BF16)
    cost_ref[...] = cos_ref[...].T
    sint_ref[...] = sin_ref[...].T
    cos, sin = wide_tables(cos_ref[...], sin_ref[...])
    keys = rotate_rows(k_ref[...].astype(F32), cos, sin)
    kt_ref[...] = keys.T.astype(BF16)
    keys = keys.astype(BF16)
    vals = (v_ref[...].astype(F32) + SCALE * dot(low[RANK:], wv_ref[...], 0, 0)).astype(BF16)
    seg_here = seg_ref[...].astype(F32)[0:1]
    key = lax.broadcasted_iota(jnp.int32, (tok, tok), 0)
    query = lax.broadcasted_iota(jnp.int32, (tok, tok), 1)
    allowed = (key <= query) & (column(seg_here, tok) == seg_here)
    bias_ref[...] = jnp.where(allowed, 0.0, NEG_FILL)
    q0 = q_ref[...].astype(F32) + SCALE * dot(low[:RANK], wq_ref[...], 0, 0)
    for h in range(heads):
        cut = slice(h * HEAD, (h + 1) * HEAD)
        qr = rotate_rows(q0[:, cut], cos, sin).astype(BF16)
        qr_ref[h] = qr
        s_ref[h] = dot(keys, qr, 1, 1) * INV_ROOT + bias_ref[...]
        dp_ref[h] = dot(vals, o_ref[:, cut], 1, 1)


def softmax_kernel(
    send, blocks, heads,
    qr_ref, s_ref, o_ref, seg_ref, pack_ref, base_ref, cos_ref, sin_ref, wv_ref,
    w_ref, kt_ref, dv_ref, code_ref, back_ref, bias_ref, keys_ref,
):
    tok = qr_ref.shape[1]
    halo = send * blocks
    cos, sin = wide_tables(cos_ref[...], sin_ref[...])
    keys = jnp.concatenate([pack_ref[b, 0:send] for b in range(blocks)], axis=0)
    keys = rotate_rows(keys.astype(F32), cos, sin)
    kt_ref[...] = keys.T.astype(BF16)
    keys_ref[...] = keys.astype(BF16)
    seg_here = seg_ref[...].astype(F32)[0:1]
    cols = []
    for b in range(blocks):
        row = pack_ref[b, 2 * send + RANK :].astype(F32)[0:1]
        cols.append(column(row, tok)[tok - send :])
    seg_col = jnp.concatenate(cols, axis=0)
    offset = lax.broadcasted_iota(jnp.int32, (halo, tok), 0)
    allowed = (offset + base_ref[0] >= halo) & (seg_col == seg_here)
    bias_ref[...] = jnp.where(allowed, 0.0, NEG_FILL)
    dv = jnp.zeros((halo + tok, HEAD), F32)
    for h in range(heads):
        far = dot(keys_ref[...], qr_ref[h], 1, 1) * INV_ROOT + bias_ref[...]
        s = jnp.concatenate([far, s_ref[h]], axis=0)
        e = jnp.exp(s - jnp.max(s, axis=0, keepdims=True))
        w = e * (1.0 / jnp.sum(e, axis=0, keepdims=True))
        w_ref[h] = w
        dv = dv + dot(w.astype(BF16), o_ref[:, h * HEAD : (h + 1) * HEAD], 1, 0)
    dv_ref[...] = dv
    wv = wv_ref[...].astype(F32)
    code_ref[...] = SCALE * dot(wv, dv[halo:], 1, 1, EXACT)
    for b in range(blocks):
        part = dv[b * send : (b + 1) * send]
        if send < tok:
            part = jnp.concatenate([jnp.zeros((tok - send, HEAD), F32), part], axis=0)
        back_ref[b] = SCALE * dot(wv, part, 1, 1, EXACT)


def grads_kernel(
    send, blocks, heads,
    low_ref, pack_ref, o_ref, w_ref, dp_ref, kt_ref, kth_ref, dv_ref, cost_ref, sint_ref, wq_ref, wv_ref,
    code_ref, up_ref, vals_ref, qg_ref,
):
    tok = o_ref.shape[0]
    halo = send * blocks
    low = low_ref[...].astype(BF16)
    wv = wv_ref[...]
    codes = [pack_ref[b, 2 * send : 2 * send + RANK] for b in range(blocks)]
    for b in range(blocks):
        rows = pack_ref[b, send : 2 * send].astype(F32)
        add = SCALE * dot(codes[b], wv, 0, 0)[tok - send :]
        vals_ref[b * send : (b + 1) * send] = (rows + add).astype(BF16)
    kt = jnp.concatenate([kth_ref[...], kt_ref[...]], axis=1)
    cos, sin = cost_ref[...], sint_ref[...]
    for h in range(heads):
        far = dot(vals_ref[...], o_ref[:, h * HEAD : (h + 1) * HEAD], 1, 1)
        dp = jnp.concatenate([far, dp_ref[h]], axis=0)
        w = w_ref[h]
        delta = jnp.sum(w * dp, axis=0, keepdims=True)
        ds = (w * (dp - delta) * INV_ROOT).astype(BF16)
        dq = dot(kt, ds, 1, 0)
        first, second = dq[:HALF], dq[HALF:]
        qg_ref[h * HEAD : h * HEAD + HALF] = (first * cos + second * sin).astype(BF16)
        qg_ref[h * HEAD + HALF : (h + 1) * HEAD] = (second * cos - first * sin).astype(BF16)
    qg = qg_ref[...]
    code_ref[...] = SCALE * dot(wq_ref[...], qg, 1, 0)
    up_q = SCALE * dot(low[:RANK], qg, 1, 1)
    dv = dv_ref[...]
    up_v = dot(low[RANK:].astype(F32), dv[halo:], 1, 0, EXACT)
    for b in range(blocks):
        part = dv[b * send : (b + 1) * send]
        if send < tok:
            part = jnp.concatenate([jnp.zeros((tok - send, HEAD), F32), part], axis=0)
        up_v = up_v + dot(codes[b].astype(F32), part, 1, 0, EXACT)
    up_ref[:, : heads * HEAD] = up_q.astype(up_ref.dtype)
    up_ref[:, heads * HEAD :] = (SCALE * up_v).astype(up_ref.dtype)


def down_kernel(dl_ref, x_ref, part_ref):
    part_ref[...] = dot(dl_ref[...], x_ref[...], 1, 0)


def partial_kernel(split, dl_ref, x_ref, up_ref, send_ref):
    rows, wide = dl_ref.shape[0], x_ref.shape[1]
    send_ref[:, :wide] = dot(dl_ref[...], x_ref[...], 1, 0).astype(BF16)
    up = up_ref[...]
    size = up.shape[1]
    send_ref[0:RANK, wide:] = up[:, :split]
    send_ref[RANK:rows, wide : wide + size - split] = up[:, split:]
    if 2 * split > size:
        send_ref[RANK:rows, wide + size - split :] = jnp.zeros((rows - RANK, 2 * split - size), BF16)


def final_kernel(split, mine_ref, one_ref, two_ref, three_ref, down_ref, upq_ref, upv_ref):
    wide = down_ref.shape[1]
    near = mine_ref[...].astype(F32) + one_ref[...].astype(F32)
    far = two_ref[...].astype(F32) + three_ref[...].astype(F32)
    total = near + far
    down_ref[...] = total[:, :wide]
    size = upq_ref.shape[1]
    upq_ref[:, :split] = total[:RANK, wide:]
    upq_ref[:, split:] = total[RANK:, wide : wide + size - split]
    upv_ref[...] = total[RANK:, wide + size - split : wide + size - split + HEAD]


def body(x, q, k, v, o, segment, a, wq, wv):
    tok, wide = x.shape
    seq_count = lax.axis_size("seq")
    fsdp_count = lax.axis_size("fsdp")
    seq_index = lax.axis_index("seq")
    heads = q.shape[1] // HEAD
    longest = tok * seq_count // 8
    blocks = -(-longest // tok)
    send = longest if blocks == 1 else tok
    halo = blocks * send
    keys = halo + tok
    direct = seq_count == 4

    def swap(array, axis, bit):
        size = lax.axis_size(axis)
        return lax.ppermute(array, axis, [(i, i ^ bit) for i in range(size)])

    def shift(array, by):
        moves = [(i, (i + by) % seq_count) for i in range(seq_count)]
        return lax.ppermute(array, "seq", moves)

    def sum_fsdp(array):
        if fsdp_count & (fsdp_count - 1):
            return lax.psum(array, "fsdp")
        bit = 1
        while bit < fsdp_count:
            array = array + swap(array, "fsdp", bit)
            bit *= 2
        return array

    seg_row = segment.reshape(1, tok)
    (part,) = call(
        lowrank_kernel,
        [((2 * RANK, tok), F32)],
        [
            pltpu.VMEM((tok, wide), BF16),
            pltpu.VMEM((2 * RANK, wide), BF16),
            pltpu.SemaphoreType.DMA((2,)),
        ],
        limit=FULL,
        in_specs=[pl.BlockSpec(memory_space=pltpu.HBM)] * 2,
    )(x, a.T)
    seg_rows = jnp.broadcast_to(seg_row, (16, tok)).astype(BF16)
    start = seq_index * tok
    base = start.reshape(1).astype(jnp.int32)
    freqs = ROPE_BASE ** (-(2.0 * jnp.arange(HALF, dtype=F32)) / HEAD)
    positions = (start - halo + jnp.arange(keys, dtype=jnp.int32)).astype(F32)
    angles = positions[:, None] * freqs[None, :]
    cos, sin = jnp.cos(angles), jnp.sin(angles)
    low = sum_fsdp(part)
    pack = jnp.concatenate(
        [k[tok - send :], v[tok - send :], low[RANK:].astype(BF16), seg_rows], axis=0
    )
    packs = jnp.stack([shift(pack, d) for d in range(blocks, 0, -1)])
    qr, kt, s, dp, cos_t, sin_t = call(
        functools.partial(project_kernel, heads),
        [
            ((heads, tok, HEAD), BF16),
            ((HEAD, tok), BF16),
            ((heads, tok, tok), F32),
            ((heads, tok, tok), F32),
            ((HALF, tok), F32),
            ((HALF, tok), F32),
        ],
        [pltpu.VMEM((tok, tok), F32)],
    )(low, q, k, v, o, seg_rows, cos[halo:], sin[halo:], wq, wv)
    specs = [pl.BlockSpec(memory_space=pltpu.VMEM)] * 9
    specs[5] = pl.BlockSpec(memory_space=pltpu.SMEM)
    w, kt_far, dv, code_v, back = call(
        functools.partial(softmax_kernel, send, blocks, heads),
        [
            ((heads, keys, tok), F32),
            ((HEAD, halo), BF16),
            ((keys, HEAD), F32),
            ((RANK, tok), F32),
            ((blocks, RANK, tok), F32),
        ],
        [pltpu.VMEM((halo, tok), F32), pltpu.VMEM((halo, HEAD), BF16)],
        in_specs=specs,
    )(qr, s, o, seg_rows, packs, base, cos[:halo], sin[:halo], wv)
    for b, d in enumerate(range(blocks, 0, -1)):
        code_v = code_v + shift(back[b], -d)
    code_q, up = call(
        functools.partial(grads_kernel, send, blocks, heads),
        [((RANK, tok), F32), ((RANK, (heads + 1) * HEAD), BF16 if direct else F32)],
        [pltpu.VMEM((halo, HEAD), BF16), pltpu.VMEM((heads * HEAD, tok), BF16)],
        cost=6 << 20,
    )(low, packs, o, w, dp, kt, kt_far, dv, cos_t, sin_t, wq, wv)
    codes = jnp.concatenate([code_q, code_v], axis=0)

    dlow = sum_fsdp(codes).astype(BF16)
    if not direct:
        (down,) = call(down_kernel, [((2 * RANK, wide), F32)])(dlow, x)
        down, up = lax.psum((down, up), "seq")
        return down.T, up[:, : heads * HEAD], up[:, heads * HEAD :]

    split = -(-(heads + 1) // 2) * HEAD
    (mine,) = call(functools.partial(partial_kernel, split), [((2 * RANK, wide + split), BF16)])(
        dlow, x, up
    )
    down, up_q, up_v = call(
        functools.partial(final_kernel, split),
        [((2 * RANK, wide), F32), ((RANK, heads * HEAD), F32), ((RANK, HEAD), F32)],
    )(mine, *[swap(mine, "seq", bit) for bit in (1, 2, 3)])
    return down.T, up_q, up_v


def solution(mesh):
    rows = ("groups", "seq")
    in_specs = (
        P(rows, "fsdp"),
        P(rows, "fsdp"),
        P(rows, "fsdp"),
        P(rows, "fsdp"),
        P(rows, "fsdp"),
        P(rows),
        P("fsdp", None),
        P(None, "fsdp"),
        P(None, "fsdp"),
    )
    out_specs = (P(("groups", "fsdp"), None), P("groups", "fsdp"), P("groups", "fsdp"))
    return jax.shard_map(body, mesh=mesh, in_specs=in_specs, out_specs=out_specs, check_vma=False)
```

```python
import functools
import math

import jax
import jax.numpy as jnp
from jax import lax
from jax.experimental import pallas as pl
from jax.experimental.pallas import tpu as pltpu
from jax.sharding import PartitionSpec as P

HEAD = 128
HALF = HEAD // 2
RANK = 16
SCALE = 2.0
ROPE_BASE = 500000.0
NEG_FILL = -1e30
INV_ROOT = 1.0 / math.sqrt(HEAD)
F32 = jnp.float32
BF16 = jnp.bfloat16
EXACT = lax.Precision.HIGHEST
LIMIT = 40 * 1024 * 1024
FULL = 55168 * 1024


def dot(left, right, left_dim, right_dim, precision=None):
    return lax.dot_general(
        left,
        right,
        (((left_dim,), (right_dim,)), ((), ())),
        precision=precision,
        preferred_element_type=F32,
    )


def call(kernel, out_shapes, scratch=(), limit=LIMIT, cost=1, **specs):
    return pl.pallas_call(
        kernel,
        out_shape=[jax.ShapeDtypeStruct(s, d) for s, d in out_shapes],
        **specs,
        scratch_shapes=list(scratch),
        compiler_params=pltpu.CompilerParams(vmem_limit_bytes=limit),
        cost_estimate=pl.CostEstimate(flops=cost, bytes_accessed=cost, transcendentals=0),
    )


def lowrank_kernel(x_hbm, a_hbm, part_ref, x_ref, a_ref, sems):
    pairs = [(x_hbm, x_ref), (a_hbm, a_ref)]
    copies = [pltpu.make_async_copy(src, dst, sems.at[i]) for i, (src, dst) in enumerate(pairs)]
    for copy in copies:
        copy.start()
    for copy in copies:
        copy.wait()
    part_ref[...] = dot(a_ref[...], x_ref[...], 1, 1)


def rotate_rows(u, cos, sin):
    return u * cos + pltpu.roll(u, HALF, 1) * sin


def wide_tables(cos, sin):
    return jnp.concatenate([cos, cos], axis=1), jnp.concatenate([-sin, sin], axis=1)


def column(row, tok):
    return jnp.broadcast_to(row, (tok, tok)).T


def project_kernel(
    heads,
    low_ref, q_ref, k_ref, v_ref, o_ref, seg_ref, cos_ref, sin_ref, wq_ref, wv_ref,
    qr_ref, kt_ref, s_ref, dp_ref, cost_ref, sint_ref, bias_ref,
):
    tok = q_ref.shape[0]
    low = low_ref[...].astype(BF16)
    cost_ref[...] = cos_ref[...].T
    sint_ref[...] = sin_ref[...].T
    cos, sin = wide_tables(cos_ref[...], sin_ref[...])
    keys = rotate_rows(k_ref[...].astype(F32), cos, sin)
    kt_ref[...] = keys.T.astype(BF16)
    keys = keys.astype(BF16)
    vals = (v_ref[...].astype(F32) + SCALE * dot(low[RANK:], wv_ref[...], 0, 0)).astype(BF16)
    seg_here = seg_ref[...].astype(F32)[0:1]
    key = lax.broadcasted_iota(jnp.int32, (tok, tok), 0)
    query = lax.broadcasted_iota(jnp.int32, (tok, tok), 1)
    allowed = (key <= query) & (column(seg_here, tok) == seg_here)
    bias_ref[...] = jnp.where(allowed, 0.0, NEG_FILL)
    q0 = q_ref[...].astype(F32) + SCALE * dot(low[:RANK], wq_ref[...], 0, 0)
    for h in range(heads):
        cut = slice(h * HEAD, (h + 1) * HEAD)
        qr = rotate_rows(q0[:, cut], cos, sin).astype(BF16)
        qr_ref[h] = qr
        s_ref[h] = dot(keys, qr, 1, 1) * INV_ROOT + bias_ref[...]
        dp_ref[h] = dot(vals, o_ref[:, cut], 1, 1)


def softmax_kernel(
    send, blocks, heads,
    qr_ref, s_ref, o_ref, seg_ref, pack_ref, base_ref, cos_ref, sin_ref, wv_ref,
    w_ref, kt_ref, dv_ref, code_ref, bias_ref, keys_ref,
):
    tok = qr_ref.shape[1]
    halo = send * blocks
    cos, sin = wide_tables(cos_ref[...], sin_ref[...])
    keys = jnp.concatenate([pack_ref[b, 0:send] for b in range(blocks)], axis=0)
    keys = rotate_rows(keys.astype(F32), cos, sin)
    kt_ref[...] = keys.T.astype(BF16)
    keys_ref[...] = keys.astype(BF16)
    seg_here = seg_ref[...].astype(F32)[0:1]
    cols = []
    for b in range(blocks):
        row = pack_ref[b, 2 * send :].astype(F32)[0:1]
        cols.append(column(row, tok)[tok - send :])
    seg_col = jnp.concatenate(cols, axis=0)
    offset = lax.broadcasted_iota(jnp.int32, (halo, tok), 0)
    allowed = (offset + base_ref[0] >= halo) & (seg_col == seg_here)
    bias_ref[...] = jnp.where(allowed, 0.0, NEG_FILL)
    dv = jnp.zeros((halo + tok, HEAD), F32)
    for h in range(heads):
        far = dot(keys_ref[...], qr_ref[h], 1, 1) * INV_ROOT + bias_ref[...]
        s = jnp.concatenate([far, s_ref[h]], axis=0)
        e = jnp.exp(s - jnp.max(s, axis=0, keepdims=True))
        w = e * (1.0 / jnp.sum(e, axis=0, keepdims=True))
        w_ref[h] = w
        dv = dv + dot(w.astype(BF16), o_ref[:, h * HEAD : (h + 1) * HEAD], 1, 0)
    dv_ref[...] = dv
    wv = wv_ref[...].astype(F32)
    code_ref[0:RANK] = SCALE * dot(wv, dv[halo:], 1, 1, EXACT)
    for b in range(blocks):
        part = dv[b * send : (b + 1) * send]
        if send < tok:
            part = jnp.concatenate([jnp.zeros((tok - send, HEAD), F32), part], axis=0)
        code_ref[(b + 1) * RANK : (b + 2) * RANK] = SCALE * dot(wv, part, 1, 1, EXACT)


def grads_kernel(
    send, blocks, heads,
    low_ref, far_ref, pack_ref, o_ref, w_ref, dp_ref, kt_ref, kth_ref, dv_ref, cost_ref, sint_ref, wq_ref, wv_ref,
    code_ref, up_ref, vals_ref, qg_ref,
):
    tok = o_ref.shape[0]
    halo = send * blocks
    low = low_ref[...].astype(BF16)
    wv = wv_ref[...]
    codes = [far_ref[b] for b in range(blocks)]
    for b in range(blocks):
        rows = pack_ref[b, send : 2 * send].astype(F32)
        add = SCALE * dot(codes[b], wv, 0, 0)[tok - send :]
        vals_ref[b * send : (b + 1) * send] = (rows + add).astype(BF16)
    kt = jnp.concatenate([kth_ref[...], kt_ref[...]], axis=1)
    cos, sin = cost_ref[...], sint_ref[...]
    for h in range(heads):
        far = dot(vals_ref[...], o_ref[:, h * HEAD : (h + 1) * HEAD], 1, 1)
        dp = jnp.concatenate([far, dp_ref[h]], axis=0)
        w = w_ref[h]
        delta = jnp.sum(w * dp, axis=0, keepdims=True)
        ds = (w * (dp - delta) * INV_ROOT).astype(BF16)
        dq = dot(kt, ds, 1, 0)
        first, second = dq[:HALF], dq[HALF:]
        qg_ref[h * HEAD : h * HEAD + HALF] = (first * cos + second * sin).astype(BF16)
        qg_ref[h * HEAD + HALF : (h + 1) * HEAD] = (second * cos - first * sin).astype(BF16)
    qg = qg_ref[...]
    code_ref[...] = SCALE * dot(wq_ref[...], qg, 1, 0)
    up_q = SCALE * dot(low[:RANK], qg, 1, 1)
    dv = dv_ref[...]
    up_v = dot(low[RANK:].astype(F32), dv[halo:], 1, 0, EXACT)
    for b in range(blocks):
        part = dv[b * send : (b + 1) * send]
        if send < tok:
            part = jnp.concatenate([jnp.zeros((tok - send, HEAD), F32), part], axis=0)
        up_v = up_v + dot(codes[b].astype(F32), part, 1, 0, EXACT)
    up_ref[:, : heads * HEAD] = up_q.astype(up_ref.dtype)
    up_ref[:, heads * HEAD :] = (SCALE * up_v).astype(up_ref.dtype)


def down_kernel(dl_ref, x_ref, part_ref):
    part_ref[...] = dot(dl_ref[...], x_ref[...], 1, 0)


def partial_kernel(own_ref, x_ref, up_ref, near_ref, part_ref, both_ref):
    part = dot(own_ref[...], x_ref[...], 1, 0).astype(BF16)
    wide, size = part.shape[1], up_ref.shape[1]
    half = both_ref.shape[1] - wide
    part_ref[...] = part
    both_ref[:, :wide] = part
    up = (up_ref[...].astype(F32) + near_ref[...].astype(F32)).astype(BF16)
    both_ref[:RANK, wide:] = up[:, :half]
    both_ref[RANK:, wide : wide + size - half] = up[:, half:]
    if 2 * half > size:
        both_ref[RANK:, wide + size - half :] = jnp.zeros((RANK, 2 * half - size), BF16)


def final_kernel(mine_ref, one_ref, two_ref, three_ref, down_ref, upq_ref, upv_ref):
    wide = one_ref.shape[1]
    near = mine_ref[:, :wide].astype(F32) + one_ref[...].astype(F32)
    far = two_ref[:, :wide].astype(F32) + three_ref[...].astype(F32)
    down_ref[...] = near + far
    up = mine_ref[:, wide:].astype(F32) + two_ref[:, wide:].astype(F32)
    half, size = up.shape[1], upq_ref.shape[1]
    upq_ref[:, :half] = up[:RANK]
    upq_ref[:, half:] = up[RANK:, : size - half]
    upv_ref[...] = up[RANK:, size - half : size - half + HEAD]


def body(x, q, k, v, o, segment, a, wq, wv):
    tok, wide = x.shape
    seq_count = lax.axis_size("seq")
    fsdp_count = lax.axis_size("fsdp")
    seq_index = lax.axis_index("seq")
    heads = q.shape[1] // HEAD
    longest = tok * seq_count // 8
    blocks = -(-longest // tok)
    send = longest if blocks == 1 else tok
    halo = blocks * send
    keys = halo + tok
    direct = seq_count == 4

    def swap(array, axis, bit):
        size = lax.axis_size(axis)
        return lax.ppermute(array, axis, [(i, i ^ bit) for i in range(size)])

    def shift(array, by):
        moves = [(i, (i + by) % seq_count) for i in range(seq_count)]
        return lax.ppermute(array, "seq", moves)

    def sum_four(array):
        if fsdp_count != 4:
            return sum_fsdp(array)
        one, two, three = [swap(array, "fsdp", bit) for bit in (1, 2, 3)]
        return (array + one) + (two + three)

    def sum_fsdp(array):
        if fsdp_count & (fsdp_count - 1):
            return lax.psum(array, "fsdp")
        bit = 1
        while bit < fsdp_count:
            array = array + swap(array, "fsdp", bit)
            bit *= 2
        return array

    seg_row = segment.reshape(1, tok)
    (part,) = call(
        lowrank_kernel,
        [((2 * RANK, tok), F32)],
        [
            pltpu.VMEM((tok, wide), BF16),
            pltpu.VMEM((2 * RANK, wide), BF16),
            pltpu.SemaphoreType.DMA((2,)),
        ],
        limit=FULL,
        in_specs=[pl.BlockSpec(memory_space=pltpu.HBM)] * 2,
    )(x, a.T)
    seg_rows = jnp.broadcast_to(seg_row, (16, tok)).astype(BF16)
    start = seq_index * tok
    base = start.reshape(1).astype(jnp.int32)
    freqs = ROPE_BASE ** (-(2.0 * jnp.arange(HALF, dtype=F32)) / HEAD)
    positions = (start - halo + jnp.arange(keys, dtype=jnp.int32)).astype(F32)
    angles = positions[:, None] * freqs[None, :]
    cos, sin = jnp.cos(angles), jnp.sin(angles)
    pack = jnp.concatenate([k[tok - send :], v[tok - send :], seg_rows], axis=0)
    packs = jnp.stack([shift(pack, d) for d in range(blocks, 0, -1)])
    low = sum_fsdp(part)
    lows = jnp.stack([shift(low[RANK:].astype(BF16), d) for d in range(blocks, 0, -1)])
    qr, kt, s, dp, cos_t, sin_t = call(
        functools.partial(project_kernel, heads),
        [
            ((heads, tok, HEAD), BF16),
            ((HEAD, tok), BF16),
            ((heads, tok, tok), F32),
            ((heads, tok, tok), F32),
            ((HALF, tok), F32),
            ((HALF, tok), F32),
        ],
        [pltpu.VMEM((tok, tok), F32)],
        cost=3 << 20,
    )(low, q, k, v, o, seg_rows, cos[halo:], sin[halo:], wq, wv)
    specs = [pl.BlockSpec(memory_space=pltpu.VMEM)] * 9
    specs[5] = pl.BlockSpec(memory_space=pltpu.SMEM)
    w, kt_far, dv, codes_v = call(
        functools.partial(softmax_kernel, send, blocks, heads),
        [
            ((heads, keys, tok), F32),
            ((HEAD, halo), BF16),
            ((keys, HEAD), F32),
            (((blocks + 1) * RANK, tok), F32),
        ],
        [pltpu.VMEM((halo, tok), F32), pltpu.VMEM((halo, HEAD), BF16)],
        in_specs=specs,
        cost=5 << 20,
    )(qr, s, o, seg_rows, packs, base, cos[:halo], sin[:halo], wv)
    codes_v, lows = lax.optimization_barrier((codes_v, lows))
    code_v = codes_v[:RANK]
    for b, d in enumerate(range(blocks, 0, -1)):
        code_v = code_v + shift(codes_v[(b + 1) * RANK : (b + 2) * RANK], -d)
    code_q, up = call(
        functools.partial(grads_kernel, send, blocks, heads),
        [((RANK, tok), F32), ((RANK, (heads + 1) * HEAD), BF16 if direct else F32)],
        [pltpu.VMEM((halo, HEAD), BF16), pltpu.VMEM((heads * HEAD, tok), BF16)],
        cost=6 << 20,
    )(low, lows, packs, o, w, dp, kt, kt_far, dv, cos_t, sin_t, wq, wv)

    codes = jnp.concatenate([code_q, code_v], axis=0)
    if not direct:
        dlow = sum_fsdp(codes).astype(BF16)
        (down,) = call(down_kernel, [((2 * RANK, wide), F32)])(dlow, x)
        down, up = lax.psum((down, up), "seq")
        return down.T, up[:, : heads * HEAD], up[:, heads * HEAD :]

    near_up = swap(up, "seq", 1)
    dlow = sum_fsdp(codes).astype(BF16)
    half = -(-(heads + 1) // 2) * HEAD
    part, both = call(
        partial_kernel, [((2 * RANK, wide), BF16), ((2 * RANK, wide + half), BF16)]
    )(dlow, x, up, near_up)
    down, up_q, up_v = call(
        final_kernel,
        [((2 * RANK, wide), F32), ((RANK, heads * HEAD), F32), ((RANK, HEAD), F32)],
    )(both, swap(part, "seq", 1), swap(both, "seq", 2), swap(part, "seq", 3))
    return down.T, up_q, up_v


def solution(mesh):
    rows = ("groups", "seq")
    in_specs = (
        P(rows, "fsdp"),
        P(rows, "fsdp"),
        P(rows, "fsdp"),
        P(rows, "fsdp"),
        P(rows, "fsdp"),
        P(rows),
        P("fsdp", None),
        P(None, "fsdp"),
        P(None, "fsdp"),
    )
    out_specs = (P(("groups", "fsdp"), None), P("groups", "fsdp"), P("groups", "fsdp"))
    return jax.shard_map(body, mesh=mesh, in_specs=in_specs, out_specs=out_specs, check_vma=False)
```

```python
import functools
import math

import jax
import jax.numpy as jnp
from jax import lax
from jax.experimental import pallas as pl
from jax.experimental.pallas import tpu as pltpu
from jax.sharding import PartitionSpec as P

HEAD = 128
HALF = HEAD // 2
RANK = 16
SCALE = 2.0
ROPE_BASE = 500000.0
NEG_FILL = -1e30
INV_ROOT = 1.0 / math.sqrt(HEAD)
F32 = jnp.float32
BF16 = jnp.bfloat16
LIMIT = 40 * 1024 * 1024
FULL = 55168 * 1024


def dot(left, right, left_dim, right_dim):
    return lax.dot_general(
        left,
        right,
        (((left_dim,), (right_dim,)), ((), ())),
        preferred_element_type=F32,
    )


def call(kernel, out_shapes, scratch=(), limit=LIMIT, cost=1, **specs):
    return pl.pallas_call(
        kernel,
        out_shape=[jax.ShapeDtypeStruct(s, d) for s, d in out_shapes],
        **specs,
        scratch_shapes=list(scratch),
        compiler_params=pltpu.CompilerParams(vmem_limit_bytes=limit),
        cost_estimate=pl.CostEstimate(flops=cost, bytes_accessed=cost, transcendentals=0),
    )


def lowrank_kernel(x_hbm, a_hbm, part_ref, x_ref, a_ref, sems):
    pairs = [(x_hbm, x_ref), (a_hbm, a_ref)]
    copies = [pltpu.make_async_copy(src, dst, sems.at[i]) for i, (src, dst) in enumerate(pairs)]
    for copy in copies:
        copy.start()
    for copy in copies:
        copy.wait()
    part_ref[...] = dot(a_ref[...], x_ref[...], 1, 1)


def rotate_rows(u, cos, sin):
    return u * cos + pltpu.roll(u, HALF, 1) * sin


def wide_tables(cos, sin):
    return jnp.concatenate([cos, cos], axis=1), jnp.concatenate([-sin, sin], axis=1)


def column(row, tok):
    return jnp.broadcast_to(row, (tok, tok)).T


def lanes(array, count):
    return jnp.concatenate([array] * count, axis=1)


def head_rows(ref, first, count):
    parts = [ref[:, h * HEAD : (h + 1) * HEAD] for h in range(first, first + count)]
    return jnp.concatenate(parts, axis=0)


def split_dot(left, right, left_dim, right_dim):
    high = right.astype(BF16)
    rest = (right - high.astype(F32)).astype(BF16)
    return dot(left, high, left_dim, right_dim) + dot(left, rest, left_dim, right_dim)


def by_token(array, send, tok):
    if send == tok:
        return array
    gap = jnp.zeros((tok - send, array.shape[1]), array.dtype)
    return jnp.concatenate([array[:tok], gap, array[tok:]], axis=0)


def project_kernel(
    count, heads,
    low_ref, q_ref, k_ref, v_ref, o_ref, seg_ref, cos_ref, sin_ref, wq_ref, wv_ref,
    qr_ref, kt_ref, s_ref, dp_ref, cost_ref, sint_ref,
):
    tok = q_ref.shape[0]
    low = low_ref[...].astype(BF16)
    cost_ref[...] = cos_ref[...].T
    sint_ref[...] = sin_ref[...].T
    cos, sin = wide_tables(cos_ref[...], sin_ref[...])
    keys = rotate_rows(k_ref[...].astype(F32), cos, sin)
    kt_ref[...] = keys.T.astype(BF16)
    keys = keys.astype(BF16)
    vals = (v_ref[...].astype(F32) + SCALE * dot(low[RANK:], wv_ref[...], 0, 0)).astype(BF16)
    seg_here = seg_ref[...].astype(F32)[0:1]
    key = lax.broadcasted_iota(jnp.int32, (tok, tok), 0)
    query = lax.broadcasted_iota(jnp.int32, (tok, tok), 1)
    allowed = (key <= query) & (column(seg_here, tok) == seg_here)
    bias = lanes(jnp.where(allowed, 0.0, NEG_FILL), count)
    q0 = q_ref[...].astype(F32) + SCALE * dot(low[:RANK], wq_ref[...], 0, 0)
    for g in range(0, heads, count):
        cut = slice(g * tok, (g + count) * tok)
        parts = [q0[:, h * HEAD : (h + 1) * HEAD] for h in range(g, g + count)]
        qr = jnp.concatenate([rotate_rows(u, cos, sin).astype(BF16) for u in parts], axis=0)
        qr_ref[cut] = qr
        s_ref[:, cut] = dot(keys, qr, 1, 1) * INV_ROOT + bias
        dp_ref[:, cut] = dot(vals, head_rows(o_ref, g, count), 1, 1)


def softmax_kernel(
    count, send, blocks, heads,
    qr_ref, s_ref, o_ref, seg_ref, pack_ref, base_ref, cos_ref, sin_ref, wv_ref,
    w_ref, kt_ref, dv_ref, code_ref,
):
    tok = o_ref.shape[0]
    halo = send * blocks
    cos, sin = wide_tables(cos_ref[...], sin_ref[...])
    keys = jnp.concatenate([pack_ref[b, 0:send] for b in range(blocks)], axis=0)
    keys = rotate_rows(keys.astype(F32), cos, sin)
    kt_ref[...] = keys.T.astype(BF16)
    keys = keys.astype(BF16)
    seg_here = seg_ref[...].astype(F32)[0:1]
    cols = []
    for b in range(blocks):
        row = pack_ref[b, 2 * send :].astype(F32)[0:1]
        cols.append(column(row, tok)[tok - send :])
    seg_col = jnp.concatenate(cols, axis=0)
    offset = lax.broadcasted_iota(jnp.int32, (halo, tok), 0)
    allowed = (offset + base_ref[0] >= halo) & (seg_col == seg_here)
    bias = lanes(jnp.where(allowed, 0.0, NEG_FILL), count)
    dv = jnp.zeros((tok + halo, HEAD), F32)
    for g in range(0, heads, count):
        cut = slice(g * tok, (g + count) * tok)
        far = dot(keys, qr_ref[cut], 1, 1) * INV_ROOT + bias
        s = jnp.concatenate([s_ref[:, cut], far], axis=0)
        e = jnp.exp(s - jnp.max(s, axis=0, keepdims=True))
        w = e * (1.0 / jnp.sum(e, axis=0, keepdims=True))
        w_ref[:, cut] = w
        dv = dv + dot(w.astype(BF16), head_rows(o_ref, g, count), 1, 0)
    dv_ref[...] = dv
    codes = SCALE * split_dot(wv_ref[...], by_token(dv, send, tok), 1, 1)
    for b in range(blocks + 1):
        code_ref[b * RANK : (b + 1) * RANK] = codes[:, b * tok : (b + 1) * tok]


def grads_kernel(
    count, send, blocks, heads,
    low_ref, far_ref, pack_ref, o_ref, w_ref, dp_ref, kt_ref, kth_ref, dv_ref, cost_ref, sint_ref, wq_ref, wv_ref,
    code_ref, up_ref, qg_ref,
):
    tok = o_ref.shape[0]
    low = low_ref[...].astype(BF16)
    wv = wv_ref[...]
    vals = []
    for b in range(blocks):
        rows = pack_ref[b, send : 2 * send].astype(F32)
        add = SCALE * dot(far_ref[b], wv, 0, 0)[tok - send :]
        vals.append((rows + add).astype(BF16))
    vals = jnp.concatenate(vals, axis=0)
    kt = jnp.concatenate([kt_ref[...], kth_ref[...]], axis=1)
    cos, sin = lanes(cost_ref[...], count), lanes(sint_ref[...], count)
    for g in range(0, heads, count):
        cut = slice(g * tok, (g + count) * tok)
        far = dot(vals, head_rows(o_ref, g, count), 1, 1)
        dp = jnp.concatenate([dp_ref[:, cut], far], axis=0)
        w = w_ref[:, cut]
        delta = jnp.sum(w * dp, axis=0, keepdims=True)
        ds = (w * (dp - delta) * INV_ROOT).astype(BF16)
        dq = dot(kt, ds, 1, 0)
        first, second = dq[:HALF], dq[HALF:]
        first, second = first * cos + second * sin, second * cos - first * sin
        turned = jnp.concatenate([first.astype(BF16), second.astype(BF16)], axis=0)
        for h in range(count):
            qg_ref[(g + h) * HEAD : (g + h + 1) * HEAD] = turned[:, h * tok : (h + 1) * tok]
    qg = qg_ref[...]
    code_ref[...] = SCALE * dot(wq_ref[...], qg, 1, 0)
    up_ref[:, : heads * HEAD] = (SCALE * dot(low[:RANK], qg, 1, 1)).astype(up_ref.dtype)
    codes = jnp.concatenate([low[RANK:]] + [far_ref[b] for b in range(blocks)], axis=1)
    up_v = SCALE * split_dot(codes, by_token(dv_ref[...], send, tok), 1, 0)
    up_ref[:, heads * HEAD :] = up_v.astype(up_ref.dtype)


def down_kernel(dl_ref, x_ref, part_ref):
    part_ref[...] = dot(dl_ref[...], x_ref[...], 1, 0)


def partial_kernel(own_ref, x_ref, up_ref, send_ref):
    part = dot(own_ref[...], x_ref[...], 1, 0).astype(BF16)
    wide, size = part.shape[1], up_ref.shape[1]
    half = send_ref.shape[1] - wide
    send_ref[:, :wide] = part
    send_ref[:RANK, wide:] = up_ref[:, :half]
    send_ref[RANK:, wide : wide + size - half] = up_ref[:, half:]
    if 2 * half > size:
        send_ref[RANK:, wide + size - half :] = jnp.zeros((RANK, 2 * half - size), BF16)


def final_kernel(mine_ref, one_ref, two_ref, three_ref, down_ref, upq_ref, upv_ref):
    near = mine_ref[...].astype(F32) + one_ref[...].astype(F32)
    far = two_ref[...].astype(F32) + three_ref[...].astype(F32)
    total = near + far
    wide, size = down_ref.shape[1], upq_ref.shape[1]
    half = total.shape[1] - wide
    down_ref[...] = total[:, :wide]
    upq_ref[:, :half] = total[:RANK, wide:]
    upq_ref[:, half:] = total[RANK:, wide : wide + size - half]
    upv_ref[...] = total[RANK:, wide + size - half : wide + size - half + HEAD]


def body(x, q, k, v, o, segment, a, wq, wv):
    tok, wide = x.shape
    seq_count = lax.axis_size("seq")
    fsdp_count = lax.axis_size("fsdp")
    seq_index = lax.axis_index("seq")
    heads = q.shape[1] // HEAD
    longest = tok * seq_count // 8
    blocks = -(-longest // tok)
    send = longest if blocks == 1 else tok
    halo = blocks * send
    keys = halo + tok
    direct = seq_count == 4

    def swap(array, axis, bit):
        size = lax.axis_size(axis)
        return lax.ppermute(array, axis, [(i, i ^ bit) for i in range(size)])

    def shift(array, by):
        moves = [(i, (i + by) % seq_count) for i in range(seq_count)]
        return lax.ppermute(array, "seq", moves)

    def sum_fsdp(array):
        if fsdp_count & (fsdp_count - 1):
            return lax.psum(array, "fsdp")
        bit = 1
        while bit < fsdp_count:
            array = array + swap(array, "fsdp", bit)
            bit *= 2
        return array

    seg_row = segment.reshape(1, tok)
    (part,) = call(
        lowrank_kernel,
        [((2 * RANK, tok), F32)],
        [
            pltpu.VMEM((tok, wide), BF16),
            pltpu.VMEM((2 * RANK, wide), BF16),
            pltpu.SemaphoreType.DMA((2,)),
        ],
        limit=FULL,
        in_specs=[pl.BlockSpec(memory_space=pltpu.HBM)] * 2,
    )(x, a.T)
    seg_rows = jnp.broadcast_to(seg_row, (16, tok)).astype(BF16)
    start = seq_index * tok
    base = start.reshape(1).astype(jnp.int32)
    freqs = ROPE_BASE ** (-(2.0 * jnp.arange(HALF, dtype=F32)) / HEAD)
    positions = (start - halo + jnp.arange(keys, dtype=jnp.int32)).astype(F32)
    angles = positions[:, None] * freqs[None, :]
    cos, sin = jnp.cos(angles), jnp.sin(angles)
    pack = jnp.concatenate([k[tok - send :], v[tok - send :], seg_rows], axis=0)
    packs = jnp.stack([shift(pack, d) for d in range(blocks, 0, -1)])
    low = sum_fsdp(part)
    low, cos, sin = lax.optimization_barrier((low, cos, sin))
    lows = jnp.stack([shift(low[RANK:].astype(BF16), d) for d in range(blocks, 0, -1)])
    count = heads if blocks == 1 else 1
    qr, kt, s, dp, cos_t, sin_t = call(
        functools.partial(project_kernel, count, heads),
        [
            ((heads * tok, HEAD), BF16),
            ((HEAD, tok), BF16),
            ((tok, heads * tok), F32),
            ((tok, heads * tok), F32),
            ((HALF, tok), F32),
            ((HALF, tok), F32),
        ],
        cost=3 << 20,
    )(low, q, k, v, o, seg_rows, cos[halo:], sin[halo:], wq, wv)
    specs = [pl.BlockSpec(memory_space=pltpu.VMEM)] * 9
    specs[5] = pl.BlockSpec(memory_space=pltpu.SMEM)
    w, kt_far, dv, codes_v = call(
        functools.partial(softmax_kernel, count, send, blocks, heads),
        [
            ((keys, heads * tok), F32),
            ((HEAD, halo), BF16),
            ((keys, HEAD), F32),
            (((blocks + 1) * RANK, tok), F32),
        ],
        in_specs=specs,
        cost=5 << 20,
    )(qr, s, o, seg_rows, packs, base, cos[:halo], sin[:halo], wv)
    codes_v, lows = lax.optimization_barrier((codes_v, lows))
    code_v = codes_v[:RANK]
    for b, d in enumerate(range(blocks, 0, -1)):
        code_v = code_v + shift(codes_v[(b + 1) * RANK : (b + 2) * RANK], -d)
    code_q, up = call(
        functools.partial(grads_kernel, count, send, blocks, heads),
        [((RANK, tok), F32), ((RANK, (heads + 1) * HEAD), BF16 if direct else F32)],
        [pltpu.VMEM((heads * HEAD, tok), BF16)],
        cost=6 << 20,
    )(low, lows, packs, o, w, dp, kt, kt_far, dv, cos_t, sin_t, wq, wv)
    codes = jnp.concatenate([code_q, code_v], axis=0)
    if not direct:
        dlow = sum_fsdp(codes).astype(BF16)
        (down,) = call(down_kernel, [((2 * RANK, wide), F32)])(dlow, x)
        down, up = lax.psum((down, up), "seq")
        return down.T, up[:, : heads * HEAD], up[:, heads * HEAD :]

    dlow = sum_fsdp(codes).astype(BF16)
    half = -(-(heads + 1) // 2) * HEAD
    (mine,) = call(partial_kernel, [((2 * RANK, wide + half), BF16)])(dlow, x, up)
    down, up_q, up_v = call(
        final_kernel,
        [((2 * RANK, wide), F32), ((RANK, heads * HEAD), F32), ((RANK, HEAD), F32)],
    )(mine, *[swap(mine, "seq", bit) for bit in (1, 2, 3)])
    return down.T, up_q, up_v


def solution(mesh):
    rows = ("groups", "seq")
    in_specs = (
        P(rows, "fsdp"),
        P(rows, "fsdp"),
        P(rows, "fsdp"),
        P(rows, "fsdp"),
        P(rows, "fsdp"),
        P(rows),
        P("fsdp", None),
        P(None, "fsdp"),
        P(None, "fsdp"),
    )
    out_specs = (P(("groups", "fsdp"), None), P("groups", "fsdp"), P("groups", "fsdp"))
    return jax.shard_map(body, mesh=mesh, in_specs=in_specs, out_specs=out_specs, check_vma=False)
```

```python
import functools
import math

import jax
import jax.numpy as jnp
from jax import lax
from jax.experimental import pallas as pl
from jax.experimental.pallas import tpu as pltpu
from jax.sharding import PartitionSpec as P

HEAD = 128
HALF = HEAD // 2
RANK = 16
SCALE = 2.0
ROPE_BASE = 500000.0
NEG_FILL = -1e30
INV_ROOT = 1.0 / math.sqrt(HEAD)
F32 = jnp.float32
BF16 = jnp.bfloat16
LIMIT = 40 * 1024 * 1024
FULL = 55136 * 1024


def dot(left, right, left_dim, right_dim):
    return lax.dot_general(
        left,
        right,
        (((left_dim,), (right_dim,)), ((), ())),
        preferred_element_type=F32,
    )


def call(kernel, out_shapes, scratch=(), limit=LIMIT, cost=1, **specs):
    return pl.pallas_call(
        kernel,
        out_shape=[jax.ShapeDtypeStruct(s, d) for s, d in out_shapes],
        **specs,
        scratch_shapes=list(scratch),
        compiler_params=pltpu.CompilerParams(vmem_limit_bytes=limit),
        cost_estimate=pl.CostEstimate(flops=cost, bytes_accessed=cost, transcendentals=0),
    )


def lowrank_kernel(send, *refs):
    sources, (part_ref, tails_ref, k_ref, v_ref, wq_ref) = refs[:5], refs[5:10]
    x_ref, a_ref, sems = refs[10:]
    targets = (x_ref, a_ref, k_ref, v_ref, wq_ref)
    copies = []
    for i, (source, target) in enumerate(zip(sources, targets)):
        copies.append(pltpu.make_async_copy(source, target, sems.at[i]))
        copies[-1].start()
    for copy in copies:
        copy.wait()
    part_ref[...] = dot(a_ref[...], x_ref[...], 1, 1)
    tok = k_ref.shape[0]
    tails_ref[0:send] = k_ref[tok - send :]
    tails_ref[send:] = v_ref[tok - send :]


def rotate_rows(u, cos, sin):
    return u * cos + pltpu.roll(u, HALF, 1) * sin


def wide_tables(cos, sin):
    return jnp.concatenate([cos, cos], axis=1), jnp.concatenate([-sin, sin], axis=1)


def column(row, tok):
    return jnp.broadcast_to(row, (tok, tok)).T


def lanes(array, count):
    return jnp.concatenate([array] * count, axis=1)


def head_rows(ref, first, count):
    parts = [ref[:, h * HEAD : (h + 1) * HEAD] for h in range(first, first + count)]
    return jnp.concatenate(parts, axis=0)


def split_dot(left, right, left_dim, right_dim):
    high = right.astype(BF16)
    rest = (right - high.astype(F32)).astype(BF16)
    return dot(left, high, left_dim, right_dim) + dot(left, rest, left_dim, right_dim)


def by_token(array, send, tok):
    if send == tok:
        return array
    gap = jnp.zeros((tok - send, array.shape[1]), array.dtype)
    return jnp.concatenate([array[:tok], gap, array[tok:]], axis=0)


def project_kernel(
    count, heads,
    low_ref, q_ref, k_ref, v_ref, o_ref, seg_ref, cos_ref, sin_ref, wq_ref, wv_ref,
    qr_ref, kt_ref, s_ref, dp_ref, cost_ref, sint_ref,
):
    tok = q_ref.shape[0]
    low = low_ref[...].astype(BF16)
    cost_ref[...] = cos_ref[...].T
    sint_ref[...] = sin_ref[...].T
    cos, sin = wide_tables(cos_ref[...], sin_ref[...])
    keys = rotate_rows(k_ref[...].astype(F32), cos, sin)
    kt_ref[...] = keys.T.astype(BF16)
    keys = keys.astype(BF16)
    vals = (v_ref[...].astype(F32) + dot(low[RANK:], wv_ref[...], 0, 0)).astype(BF16)
    seg_here = seg_ref[...].astype(F32)[0:1]
    key = lax.broadcasted_iota(jnp.int32, (tok, tok), 0)
    query = lax.broadcasted_iota(jnp.int32, (tok, tok), 1)
    allowed = (key <= query) & (column(seg_here, tok) == seg_here)
    bias = lanes(jnp.where(allowed, 0.0, NEG_FILL), count)
    q0 = q_ref[...].astype(F32) + SCALE * dot(low[:RANK], wq_ref[...], 0, 0)
    for g in range(0, heads, count):
        cut = slice(g * tok, (g + count) * tok)
        parts = [q0[:, h * HEAD : (h + 1) * HEAD] for h in range(g, g + count)]
        qr = jnp.concatenate([rotate_rows(u, cos, sin).astype(BF16) for u in parts], axis=0)
        qr_ref[cut] = qr
        s_ref[:, cut] = dot(keys, qr, 1, 1) * INV_ROOT + bias
        dp_ref[:, cut] = dot(vals, head_rows(o_ref, g, count), 1, 1)


def softmax_kernel(
    count, send, blocks, heads,
    qr_ref, s_ref, o_ref, seg_ref, pack_ref, base_ref, cos_ref, sin_ref, wv_ref,
    w_ref, kt_ref, dv_ref, code_ref,
):
    tok = o_ref.shape[0]
    halo = send * blocks
    cos, sin = wide_tables(cos_ref[...], sin_ref[...])
    keys = jnp.concatenate([pack_ref[b, 0:send] for b in range(blocks)], axis=0)
    keys = rotate_rows(keys.astype(F32), cos, sin)
    kt_ref[...] = keys.T.astype(BF16)
    keys = keys.astype(BF16)
    seg_here = seg_ref[...].astype(F32)[0:1]
    cols = []
    for b in range(blocks):
        row = pack_ref[b, 2 * send :].astype(F32)[0:1]
        cols.append(column(row, tok)[tok - send :])
    seg_col = jnp.concatenate(cols, axis=0)
    offset = lax.broadcasted_iota(jnp.int32, (halo, tok), 0)
    allowed = (offset + base_ref[0] >= halo) & (seg_col == seg_here)
    bias = lanes(jnp.where(allowed, 0.0, NEG_FILL), count)
    dv = jnp.zeros((tok + halo, HEAD), F32)
    for g in range(0, heads, count):
        cut = slice(g * tok, (g + count) * tok)
        far = dot(keys, qr_ref[cut], 1, 1) * INV_ROOT + bias
        s = jnp.concatenate([s_ref[:, cut], far], axis=0)
        e = jnp.exp(s - jnp.max(s, axis=0, keepdims=True))
        w = e * (1.0 / jnp.sum(e, axis=0, keepdims=True))
        w_ref[:, cut] = w
        dv = dv + dot(w.astype(BF16), head_rows(o_ref, g, count), 1, 0)
    dv_ref[...] = dv
    codes = split_dot(wv_ref[...], by_token(dv, send, tok), 1, 1)
    for b in range(blocks + 1):
        code_ref[b * RANK : (b + 1) * RANK] = codes[:, b * tok : (b + 1) * tok]


def grads_kernel(
    count, send, blocks, heads,
    low_ref, far_ref, pack_ref, o_ref, w_ref, dp_ref, kt_ref, kth_ref, dv_ref, cost_ref, sint_ref, wq_ref, wv_ref,
    code_ref, up_ref, qg_ref,
):
    tok = o_ref.shape[0]
    low = low_ref[...].astype(BF16)
    wv = wv_ref[...]
    vals = []
    for b in range(blocks):
        rows = pack_ref[b, send : 2 * send].astype(F32)
        add = dot(far_ref[b], wv, 0, 0)[tok - send :]
        vals.append((rows + add).astype(BF16))
    vals = jnp.concatenate(vals, axis=0)
    kt = jnp.concatenate([kt_ref[...], kth_ref[...]], axis=1)
    cos, sin = lanes(cost_ref[...], count), lanes(sint_ref[...], count)
    for g in range(0, heads, count):
        cut = slice(g * tok, (g + count) * tok)
        far = dot(vals, head_rows(o_ref, g, count), 1, 1)
        dp = jnp.concatenate([dp_ref[:, cut], far], axis=0)
        w = w_ref[:, cut]
        delta = jnp.sum(w * dp, axis=0, keepdims=True)
        ds = (w * (dp - delta) * INV_ROOT).astype(BF16)
        dq = dot(kt, ds, 1, 0)
        first, second = dq[:HALF], dq[HALF:]
        first, second = first * cos + second * sin, second * cos - first * sin
        turned = jnp.concatenate([first.astype(BF16), second.astype(BF16)], axis=0)
        for h in range(count):
            qg_ref[(g + h) * HEAD : (g + h + 1) * HEAD] = turned[:, h * tok : (h + 1) * tok]
    qg = qg_ref[...]
    code_ref[...] = SCALE * dot(wq_ref[...], qg, 1, 0)
    up_ref[:, : heads * HEAD] = (SCALE * dot(low[:RANK], qg, 1, 1)).astype(up_ref.dtype)
    codes = jnp.concatenate([low[RANK:]] + [far_ref[b] for b in range(blocks)], axis=1)
    up_v = SCALE * split_dot(codes, by_token(dv_ref[...], send, tok), 1, 0)
    up_ref[:, heads * HEAD :] = up_v.astype(up_ref.dtype)


def down_kernel(dl_ref, x_ref, part_ref):
    part_ref[...] = dot(dl_ref[...], x_ref[...], 1, 0)


def partial_kernel(own_ref, x_ref, up_ref, send_ref):
    part = dot(own_ref[...], x_ref[...], 1, 0).astype(BF16)
    wide, size = part.shape[1], up_ref.shape[1]
    half = send_ref.shape[1] - wide
    send_ref[:, :wide] = part
    send_ref[:RANK, wide:] = up_ref[:, :half]
    send_ref[RANK:, wide : wide + size - half] = up_ref[:, half:]
    if 2 * half > size:
        send_ref[RANK:, wide + size - half :] = jnp.zeros((RANK, 2 * half - size), BF16)


def final_kernel(mine_ref, one_ref, two_ref, three_ref, down_ref, upq_ref, upv_ref):
    near = mine_ref[...].astype(F32) + one_ref[...].astype(F32)
    far = two_ref[...].astype(F32) + three_ref[...].astype(F32)
    total = near + far
    wide, size = down_ref.shape[1], upq_ref.shape[1]
    half = total.shape[1] - wide
    down_ref[...] = total[:, :wide]
    upq_ref[:, :half] = total[:RANK, wide:]
    upq_ref[:, half:] = total[RANK:, wide : wide + size - half]
    upv_ref[...] = total[RANK:, wide + size - half : wide + size - half + HEAD]


def body(x, q, k, v, o, segment, a, wq, wv):
    tok, wide = x.shape
    seq_count = lax.axis_size("seq")
    fsdp_count = lax.axis_size("fsdp")
    seq_index = lax.axis_index("seq")
    heads = q.shape[1] // HEAD
    longest = tok * seq_count // 8
    blocks = -(-longest // tok)
    send = longest if blocks == 1 else tok
    halo = blocks * send
    keys = halo + tok
    direct = seq_count == 4 and fsdp_count == 4

    def swap(array, axis, bit):
        size = lax.axis_size(axis)
        return lax.ppermute(array, axis, [(i, i ^ bit) for i in range(size)])

    def shift(array, by):
        moves = [(i, (i + by) % seq_count) for i in range(seq_count)]
        return lax.ppermute(array, "seq", moves)

    def near(array, bit):
        moves = []
        for i in range(seq_count):
            for f in range(fsdp_count):
                if f % 2 == 0:
                    to, flip = i ^ 1, bit
                elif i in (1, 2):
                    to, flip = 3 - i, bit
                else:
                    to, flip = i, 2
                moves.append((i * fsdp_count + f, to * fsdp_count + (f ^ flip)))
        return lax.ppermute(array, ("seq", "fsdp"), moves)

    def sum_fsdp(array):
        if fsdp_count & (fsdp_count - 1):
            return lax.psum(array, "fsdp")
        bit = 1
        while bit < fsdp_count:
            array = array + swap(array, "fsdp", bit)
            bit *= 2
        return array

    seg_row = segment.reshape(1, tok)
    part, tails, k, v, wq = call(
        functools.partial(lowrank_kernel, send),
        [
            ((2 * RANK, tok), F32),
            ((2 * send, HEAD), BF16),
            ((tok, HEAD), BF16),
            ((tok, HEAD), BF16),
            (wq.shape, BF16),
        ],
        [
            pltpu.VMEM((tok, wide), BF16),
            pltpu.VMEM((2 * RANK, wide), BF16),
            pltpu.SemaphoreType.DMA((5,)),
        ],
        limit=FULL,
        in_specs=[pl.BlockSpec(memory_space=pltpu.HBM)] * 5,
    )(x, a.T, k, v, wq)
    seg_rows = jnp.broadcast_to(seg_row, (16, tok)).astype(BF16)
    pack = jnp.concatenate([tails, seg_rows], axis=0)
    wv = wv * SCALE
    start = seq_index * tok
    base = start.reshape(1).astype(jnp.int32)
    freqs = ROPE_BASE ** (-(2.0 * jnp.arange(HALF, dtype=F32)) / HEAD)
    positions = (start - halo + jnp.arange(keys, dtype=jnp.int32)).astype(F32)
    angles = positions[:, None] * freqs[None, :]
    cos, sin = jnp.cos(angles), jnp.sin(angles)
    packs = jnp.stack([shift(pack, d) for d in range(blocks, 0, -1)])
    if direct:
        part = part + swap(part, "fsdp", 1)
        low = part + swap(part, "fsdp", 2)
        far = (near(part[RANK:], 0) + near(part[RANK:], 2)).astype(BF16)
        early = (low, cos, sin, far, packs, wv)
        low, cos, sin, far, packs, wv = lax.optimization_barrier(early)
        mine = (seq_index == 2) == (lax.axis_index("fsdp") % 2 == 1)
        lows = jnp.where(mine, far, swap(far, "fsdp", 1))[None]
    else:
        low = sum_fsdp(part)
        lows = jnp.stack([shift(low[RANK:].astype(BF16), d) for d in range(blocks, 0, -1)])
    count = heads if blocks == 1 else 1
    qr, kt, s, dp, cos_t, sin_t = call(
        functools.partial(project_kernel, count, heads),
        [
            ((heads * tok, HEAD), BF16),
            ((HEAD, tok), BF16),
            ((tok, heads * tok), F32),
            ((tok, heads * tok), F32),
            ((HALF, tok), F32),
            ((HALF, tok), F32),
        ],
        cost=3 << 20,
    )(low, q, k, v, o, seg_rows, cos[halo:], sin[halo:], wq, wv)
    specs = [pl.BlockSpec(memory_space=pltpu.VMEM)] * 9
    specs[5] = pl.BlockSpec(memory_space=pltpu.SMEM)
    w, kt_far, dv, codes_v = call(
        functools.partial(softmax_kernel, count, send, blocks, heads),
        [
            ((keys, heads * tok), F32),
            ((HEAD, halo), BF16),
            ((keys, HEAD), F32),
            (((blocks + 1) * RANK, tok), F32),
        ],
        in_specs=specs,
        cost=5 << 20,
    )(qr, s, o, seg_rows, packs, base, cos[:halo], sin[:halo], wv)
    codes_v, lows = lax.optimization_barrier((codes_v, lows))
    code_v = codes_v[:RANK]
    for b, d in enumerate(range(blocks, 0, -1)):
        code_v = code_v + shift(codes_v[(b + 1) * RANK : (b + 2) * RANK], -d)
    code_q, up = call(
        functools.partial(grads_kernel, count, send, blocks, heads),
        [((RANK, tok), F32), ((RANK, (heads + 1) * HEAD), BF16 if direct else F32)],
        [pltpu.VMEM((heads * HEAD, tok), BF16)],
        cost=6 << 20,
    )(low, lows, packs, o, w, dp, kt, kt_far, dv, cos_t, sin_t, wq, wv)
    codes = jnp.concatenate([code_q, code_v], axis=0)
    if not direct:
        dlow = sum_fsdp(codes).astype(BF16)
        (down,) = call(down_kernel, [((2 * RANK, wide), F32)])(dlow, x)
        down, up = lax.psum((down, up), "seq")
        return down.T, up[:, : heads * HEAD], up[:, heads * HEAD :]

    dlow = sum_fsdp(codes).astype(BF16)
    half = -(-(heads + 1) // 2) * HEAD
    (mine,) = call(partial_kernel, [((2 * RANK, wide + half), BF16)])(dlow, x, up)
    down, up_q, up_v = call(
        final_kernel,
        [((2 * RANK, wide), F32), ((RANK, heads * HEAD), F32), ((RANK, HEAD), F32)],
    )(mine, *[swap(mine, "seq", bit) for bit in (1, 2, 3)])
    return down.T, up_q, up_v


def solution(mesh):
    rows = ("groups", "seq")
    in_specs = (
        P(rows, "fsdp"),
        P(rows, "fsdp"),
        P(rows, "fsdp"),
        P(rows, "fsdp"),
        P(rows, "fsdp"),
        P(rows),
        P("fsdp", None),
        P(None, "fsdp"),
        P(None, "fsdp"),
    )
    out_specs = (P(("groups", "fsdp"), None), P("groups", "fsdp"), P("groups", "fsdp"))
    return jax.shard_map(body, mesh=mesh, in_specs=in_specs, out_specs=out_specs, check_vma=False)
```

```python
import functools
import math

import jax
import jax.numpy as jnp
from jax import lax
from jax.experimental import pallas as pl
from jax.experimental.pallas import tpu as pltpu
from jax.sharding import PartitionSpec as P

HEAD = 128
HALF = HEAD // 2
RANK = 16
SCALE = 2.0
ROPE_BASE = 500000.0
NEG_FILL = -1e30
INV_ROOT = 1.0 / math.sqrt(HEAD)
F32 = jnp.float32
BF16 = jnp.bfloat16
LIMIT = 40 * 1024 * 1024
FULL = 55080 * 1024


def dot(left, right, left_dim, right_dim):
    return lax.dot_general(
        left,
        right,
        (((left_dim,), (right_dim,)), ((), ())),
        preferred_element_type=F32,
    )


def call(kernel, out_shapes, scratch=(), limit=LIMIT, cost=1, **specs):
    return pl.pallas_call(
        kernel,
        out_shape=[jax.ShapeDtypeStruct(s, d) for s, d in out_shapes],
        **specs,
        scratch_shapes=list(scratch),
        compiler_params=pltpu.CompilerParams(vmem_limit_bytes=limit),
        cost_estimate=pl.CostEstimate(flops=cost, bytes_accessed=cost, transcendentals=0),
    )


def lowrank_kernel(send, *refs):
    sources, (part_ref, tails_ref, k_ref, v_ref, wq_ref) = refs[:5], refs[5:10]
    x_ref, a_ref, sems = refs[10:]
    targets = (x_ref, a_ref, k_ref, v_ref, wq_ref)
    copies = []
    for i, (source, target) in enumerate(zip(sources, targets)):
        copies.append(pltpu.make_async_copy(source, target, sems.at[i]))
        copies[-1].start()
    for copy in copies:
        copy.wait()
    part_ref[...] = dot(a_ref[...], x_ref[...], 1, 1)
    tok = k_ref.shape[0]
    tails_ref[0:send] = k_ref[tok - send :]
    tails_ref[send:] = v_ref[tok - send :]


def rotate_rows(u, cos, sin):
    return u * cos + pltpu.roll(u, HALF, 1) * sin


def wide_tables(cos, sin):
    return jnp.concatenate([cos, cos], axis=1), jnp.concatenate([-sin, sin], axis=1)


def column(row, tok):
    return jnp.broadcast_to(row, (tok, tok)).T


def lanes(array, count):
    return jnp.concatenate([array] * count, axis=1)


def head_rows(ref, first, count):
    parts = [ref[:, h * HEAD : (h + 1) * HEAD] for h in range(first, first + count)]
    return jnp.concatenate(parts, axis=0)


def split_dot(left, right, left_dim, right_dim):
    high = right.astype(BF16)
    rest = (right - high.astype(F32)).astype(BF16)
    return dot(left, high, left_dim, right_dim) + dot(left, rest, left_dim, right_dim)


def by_token(array, send, tok):
    if send == tok:
        return array
    gap = jnp.zeros((tok - send, array.shape[1]), array.dtype)
    return jnp.concatenate([array[:tok], gap, array[tok:]], axis=0)


def project_kernel(
    count, heads,
    low_ref, q_ref, k_ref, v_ref, o_ref, seg_ref, cos_ref, sin_ref, wq_ref, wv_ref,
    qr_ref, kt_ref, s_ref, dp_ref, cost_ref, sint_ref,
):
    tok = q_ref.shape[0]
    low = low_ref[...].astype(BF16)
    cost_ref[...] = cos_ref[...].T
    sint_ref[...] = sin_ref[...].T
    cos, sin = wide_tables(cos_ref[...], sin_ref[...])
    keys = rotate_rows(k_ref[...].astype(F32), cos, sin)
    kt_ref[...] = keys.T.astype(BF16)
    keys = keys.astype(BF16)
    vals = (v_ref[...].astype(F32) + dot(low[RANK:], wv_ref[...], 0, 0)).astype(BF16)
    seg_here = seg_ref[...].astype(F32)[0:1]
    key = lax.broadcasted_iota(jnp.int32, (tok, tok), 0)
    query = lax.broadcasted_iota(jnp.int32, (tok, tok), 1)
    allowed = (key <= query) & (column(seg_here, tok) == seg_here)
    bias = lanes(jnp.where(allowed, 0.0, NEG_FILL), count)
    q0 = q_ref[...].astype(F32) + SCALE * dot(low[:RANK], wq_ref[...], 0, 0)
    for g in range(0, heads, count):
        cut = slice(g * tok, (g + count) * tok)
        parts = [q0[:, h * HEAD : (h + 1) * HEAD] for h in range(g, g + count)]
        qr = jnp.concatenate([rotate_rows(u, cos, sin).astype(BF16) for u in parts], axis=0)
        qr_ref[cut] = qr
        s_ref[:, cut] = dot(keys, qr, 1, 1) * INV_ROOT + bias
        dp_ref[:, cut] = dot(vals, head_rows(o_ref, g, count), 1, 1)


def softmax_kernel(
    count, send, blocks, heads,
    qr_ref, s_ref, o_ref, seg_ref, pack_ref, base_ref, cos_ref, sin_ref, wv_ref,
    w_ref, kt_ref, dv_ref, code_ref,
):
    tok = o_ref.shape[0]
    halo = send * blocks
    cos, sin = wide_tables(cos_ref[...], sin_ref[...])
    keys = jnp.concatenate([pack_ref[b, 0:send] for b in range(blocks)], axis=0)
    keys = rotate_rows(keys.astype(F32), cos, sin)
    kt_ref[...] = keys.T.astype(BF16)
    keys = keys.astype(BF16)
    seg_here = seg_ref[...].astype(F32)[0:1]
    cols = []
    for b in range(blocks):
        row = pack_ref[b, 2 * send :].astype(F32)[0:1]
        cols.append(column(row, tok)[tok - send :])
    seg_col = jnp.concatenate(cols, axis=0)
    offset = lax.broadcasted_iota(jnp.int32, (halo, tok), 0)
    allowed = (offset + base_ref[0] >= halo) & (seg_col == seg_here)
    bias = lanes(jnp.where(allowed, 0.0, NEG_FILL), count)
    dv = jnp.zeros((tok + halo, HEAD), F32)
    for g in range(0, heads, count):
        cut = slice(g * tok, (g + count) * tok)
        far = dot(keys, qr_ref[cut], 1, 1) * INV_ROOT + bias
        s = jnp.concatenate([s_ref[:, cut], far], axis=0)
        e = jnp.exp(s - jnp.max(s, axis=0, keepdims=True))
        w = e * (1.0 / jnp.sum(e, axis=0, keepdims=True))
        w_ref[:, cut] = w
        dv = dv + dot(w.astype(BF16), head_rows(o_ref, g, count), 1, 0)
    dv_ref[...] = dv
    codes = split_dot(wv_ref[...], by_token(dv, send, tok), 1, 1)
    for b in range(blocks + 1):
        code_ref[b * RANK : (b + 1) * RANK] = codes[:, b * tok : (b + 1) * tok]


def grads_kernel(
    count, send, blocks, heads,
    low_ref, far_ref, pack_ref, o_ref, w_ref, dp_ref, kt_ref, kth_ref, dv_ref, cost_ref, sint_ref, wq_ref, wv_ref,
    code_ref, up_ref, qg_ref,
):
    tok = o_ref.shape[0]
    low = low_ref[...].astype(BF16)
    wv = wv_ref[...]
    vals = []
    for b in range(blocks):
        rows = pack_ref[b, send : 2 * send].astype(F32)
        add = dot(far_ref[b], wv, 0, 0)[tok - send :]
        vals.append((rows + add).astype(BF16))
    vals = jnp.concatenate(vals, axis=0)
    kt = jnp.concatenate([kt_ref[...], kth_ref[...]], axis=1)
    cos, sin = lanes(cost_ref[...], count), lanes(sint_ref[...], count)
    for g in range(0, heads, count):
        cut = slice(g * tok, (g + count) * tok)
        far = dot(vals, head_rows(o_ref, g, count), 1, 1)
        dp = jnp.concatenate([dp_ref[:, cut], far], axis=0)
        w = w_ref[:, cut]
        delta = jnp.sum(w * dp, axis=0, keepdims=True)
        ds = (w * (dp - delta) * INV_ROOT).astype(BF16)
        dq = dot(kt, ds, 1, 0)
        first, second = dq[:HALF], dq[HALF:]
        first, second = first * cos + second * sin, second * cos - first * sin
        turned = jnp.concatenate([first.astype(BF16), second.astype(BF16)], axis=0)
        for h in range(count):
            qg_ref[(g + h) * HEAD : (g + h + 1) * HEAD] = turned[:, h * tok : (h + 1) * tok]
    qg = qg_ref[...]
    code_ref[...] = SCALE * dot(wq_ref[...], qg, 1, 0)
    up_ref[:, : heads * HEAD] = (SCALE * dot(low[:RANK], qg, 1, 1)).astype(up_ref.dtype)
    codes = jnp.concatenate([low[RANK:]] + [far_ref[b] for b in range(blocks)], axis=1)
    up_v = SCALE * split_dot(codes, by_token(dv_ref[...], send, tok), 1, 0)
    up_ref[:, heads * HEAD :] = up_v.astype(up_ref.dtype)


def down_kernel(dl_ref, x_ref, part_ref):
    part_ref[...] = dot(dl_ref[...], x_ref[...], 1, 0)


def partial_kernel(own_ref, x_ref, *refs):
    send_ref = refs[-1]
    wide = x_ref.shape[1]
    send_ref[:, :wide] = dot(own_ref[...], x_ref[...], 1, 0).astype(BF16)
    if len(refs) == 2:
        send_ref[:, wide:] = refs[0][...]


def add_four(refs):
    first, second, third, fourth = [ref[...].astype(F32) for ref in refs]
    return (first + second) + (third + fourth)


def queries_kernel(*refs):
    down_ref, upq_ref, upv_ref = refs[4:]
    total = add_four(refs[:4])
    wide, size = down_ref.shape[1], upq_ref.shape[1]
    down_ref[...] = total[:, :wide]
    upq_ref[...] = total[:, wide : wide + size]
    upv_ref[...] = total[:, wide + size :]


def values_kernel(*refs):
    down_ref = refs[5]
    down_ref[:RANK] = refs[4][...]
    down_ref[RANK:] = add_four(refs[:4])


def body(x, q, k, v, o, segment, a, wq, wv):
    tok, wide = x.shape
    seq_count = lax.axis_size("seq")
    fsdp_count = lax.axis_size("fsdp")
    seq_index = lax.axis_index("seq")
    heads = q.shape[1] // HEAD
    longest = tok * seq_count // 8
    blocks = -(-longest // tok)
    send = longest if blocks == 1 else tok
    halo = blocks * send
    keys = halo + tok
    direct = seq_count == 4 and fsdp_count == 4

    def swap(array, axis, bit):
        size = lax.axis_size(axis)
        return lax.ppermute(array, axis, [(i, i ^ bit) for i in range(size)])

    def shift(array, by):
        moves = [(i, (i + by) % seq_count) for i in range(seq_count)]
        return lax.ppermute(array, "seq", moves)

    def sum_fsdp(array):
        if fsdp_count & (fsdp_count - 1):
            return lax.psum(array, "fsdp")
        bit = 1
        while bit < fsdp_count:
            array = array + swap(array, "fsdp", bit)
            bit *= 2
        return array

    seg_row = segment.reshape(1, tok)
    part, tails, k, v, wq = call(
        functools.partial(lowrank_kernel, send),
        [
            ((2 * RANK, tok), F32),
            ((2 * send, HEAD), BF16),
            ((tok, HEAD), BF16),
            ((tok, HEAD), BF16),
            (wq.shape, BF16),
        ],
        [
            pltpu.VMEM((tok, wide), BF16),
            pltpu.VMEM((2 * RANK, wide), BF16),
            pltpu.SemaphoreType.DMA((5,)),
        ],
        limit=FULL,
        in_specs=[pl.BlockSpec(memory_space=pltpu.HBM)] * 5,
    )(x, a.T, k, v, wq)
    seg_rows = jnp.broadcast_to(seg_row, (16, tok)).astype(BF16)
    pack = jnp.concatenate([tails, seg_rows], axis=0)
    wv = wv * SCALE
    start = seq_index * tok
    base = start.reshape(1).astype(jnp.int32)
    freqs = ROPE_BASE ** (-(2.0 * jnp.arange(HALF, dtype=F32)) / HEAD)
    positions = (start - halo + jnp.arange(keys, dtype=jnp.int32)).astype(F32)
    angles = positions[:, None] * freqs[None, :]
    cos, sin = jnp.cos(angles), jnp.sin(angles)
    packs = jnp.stack([shift(pack, d) for d in range(blocks, 0, -1)])
    low = sum_fsdp(part)
    low, cos, sin, wv = lax.optimization_barrier((low, cos, sin, wv))
    lows = jnp.stack([shift(low[RANK:].astype(BF16), d) for d in range(blocks, 0, -1)])
    count = heads if blocks == 1 else 1
    qr, kt, s, dp, cos_t, sin_t = call(
        functools.partial(project_kernel, count, heads),
        [
            ((heads * tok, HEAD), BF16),
            ((HEAD, tok), BF16),
            ((tok, heads * tok), F32),
            ((tok, heads * tok), F32),
            ((HALF, tok), F32),
            ((HALF, tok), F32),
        ],
        cost=3 << 20,
    )(low, q, k, v, o, seg_rows, cos[halo:], sin[halo:], wq, wv)
    specs = [pl.BlockSpec(memory_space=pltpu.VMEM)] * 9
    specs[5] = pl.BlockSpec(memory_space=pltpu.SMEM)
    w, kt_far, dv, codes_v = call(
        functools.partial(softmax_kernel, count, send, blocks, heads),
        [
            ((keys, heads * tok), F32),
            ((HEAD, halo), BF16),
            ((keys, HEAD), F32),
            (((blocks + 1) * RANK, tok), F32),
        ],
        in_specs=specs,
        cost=5 << 20,
    )(qr, s, o, seg_rows, packs, base, cos[:halo], sin[:halo], wv)
    codes_v, lows = lax.optimization_barrier((codes_v, lows))
    code_v = codes_v[:RANK]
    backs = []
    for b, d in enumerate(range(blocks, 0, -1)):
        backs.append(shift(codes_v[(b + 1) * RANK : (b + 2) * RANK], -d))
    code_q, up = call(
        functools.partial(grads_kernel, count, send, blocks, heads),
        [((RANK, tok), F32), ((RANK, (heads + 1) * HEAD), BF16 if direct else F32)],
        [pltpu.VMEM((heads * HEAD, tok), BF16)],
        cost=6 << 20,
    )(low, lows, packs, o, w, dp, kt, kt_far, dv, cos_t, sin_t, wq, wv)
    if not direct:
        code_v = sum(backs, code_v)
        dlow = sum_fsdp(jnp.concatenate([code_q, code_v], axis=0)).astype(BF16)
        (down,) = call(down_kernel, [((2 * RANK, wide), F32)])(dlow, x)
        down, up = lax.psum((down, up), "seq")
        return down.T, up[:, : heads * HEAD], up[:, heads * HEAD :]

    up_size = (heads + 1) * HEAD
    dlow_q = sum_fsdp(code_q).astype(BF16)
    (mine_q,) = call(partial_kernel, [((RANK, wide + up_size), BF16)])(dlow_q, x, up)
    all_q = [mine_q] + [swap(mine_q, "seq", bit) for bit in (1, 2, 3)]
    code_v, mine_q = lax.optimization_barrier((code_v, mine_q))
    dlow_v = sum_fsdp(code_v + backs[0]).astype(BF16)
    (mine_v,) = call(partial_kernel, [((RANK, wide), BF16)])(dlow_v, x)
    all_v = [mine_v] + [swap(mine_v, "seq", bit) for bit in (1, 2, 3)]
    down_q, up_q, up_v = call(
        queries_kernel,
        [((RANK, wide), F32), ((RANK, heads * HEAD), F32), ((RANK, HEAD), F32)],
        cost=64 << 20,
    )(*all_q)
    (down,) = call(values_kernel, [((2 * RANK, wide), F32)])(*all_v, down_q)
    return down.T, up_q, up_v


def solution(mesh):
    rows = ("groups", "seq")
    in_specs = (
        P(rows, "fsdp"),
        P(rows, "fsdp"),
        P(rows, "fsdp"),
        P(rows, "fsdp"),
        P(rows, "fsdp"),
        P(rows),
        P("fsdp", None),
        P(None, "fsdp"),
        P(None, "fsdp"),
    )
    out_specs = (P(("groups", "fsdp"), None), P("groups", "fsdp"), P("groups", "fsdp"))
    return jax.shard_map(body, mesh=mesh, in_specs=in_specs, out_specs=out_specs, check_vma=False)
```

```python
import functools
import math

import jax
import jax.numpy as jnp
from jax import lax
from jax.experimental import pallas as pl
from jax.experimental.pallas import tpu as pltpu
from jax.sharding import PartitionSpec as P

HEAD = 128
HALF = HEAD // 2
RANK = 16
SCALE = 2.0
ROPE_BASE = 500000.0
NEG_FILL = -1e30
INV_ROOT = 1.0 / math.sqrt(HEAD)
F32 = jnp.float32
BF16 = jnp.bfloat16
LIMIT = 40 * 1024 * 1024
FULL = 55080 * 1024


def dot(left, right, left_dim, right_dim):
    return lax.dot_general(
        left,
        right,
        (((left_dim,), (right_dim,)), ((), ())),
        preferred_element_type=F32,
    )


def call(kernel, out_shapes, scratch=(), limit=LIMIT, cost=1, **specs):
    return pl.pallas_call(
        kernel,
        out_shape=[jax.ShapeDtypeStruct(s, d) for s, d in out_shapes],
        **specs,
        scratch_shapes=list(scratch),
        compiler_params=pltpu.CompilerParams(vmem_limit_bytes=limit),
        cost_estimate=pl.CostEstimate(flops=cost, bytes_accessed=cost, transcendentals=0),
    )


def lowrank_kernel(send, *refs):
    sources, (part_ref, tails_ref, k_ref, v_ref, wq_ref) = refs[:5], refs[5:10]
    x_ref, a_ref, sems = refs[10:]
    targets = (x_ref, a_ref, k_ref, v_ref, wq_ref)
    copies = []
    for i, (source, target) in enumerate(zip(sources, targets)):
        copies.append(pltpu.make_async_copy(source, target, sems.at[i]))
        copies[-1].start()
    for copy in copies:
        copy.wait()
    part_ref[...] = dot(a_ref[...], x_ref[...], 1, 1)
    tok = k_ref.shape[0]
    tails_ref[0:send] = k_ref[tok - send :]
    tails_ref[send:] = v_ref[tok - send :]


def rotate_rows(u, cos, sin):
    return u * cos + pltpu.roll(u, HALF, 1) * sin


def wide_tables(cos, sin):
    return jnp.concatenate([cos, cos], axis=1), jnp.concatenate([-sin, sin], axis=1)


def column(row, tok):
    return jnp.broadcast_to(row, (tok, tok)).T


def lanes(array, count):
    return jnp.concatenate([array] * count, axis=1)


def head_rows(ref, first, count):
    parts = [ref[:, h * HEAD : (h + 1) * HEAD] for h in range(first, first + count)]
    return jnp.concatenate(parts, axis=0)


def split_dot(left, right, left_dim, right_dim):
    high = right.astype(BF16)
    rest = (right - high.astype(F32)).astype(BF16)
    return dot(left, high, left_dim, right_dim) + dot(left, rest, left_dim, right_dim)


def by_token(array, send, tok):
    if send == tok:
        return array
    gap = jnp.zeros((tok - send, array.shape[1]), array.dtype)
    return jnp.concatenate([array[:tok], gap, array[tok:]], axis=0)


def project_kernel(
    count, heads,
    low_ref, q_ref, k_ref, v_ref, o_ref, seg_ref, cos_ref, sin_ref, wq_ref, wv_ref,
    qr_ref, kt_ref, s_ref, dp_ref, cost_ref, sint_ref,
):
    tok = q_ref.shape[0]
    low = low_ref[...].astype(BF16)
    cost_ref[...] = cos_ref[...].T
    sint_ref[...] = sin_ref[...].T
    cos, sin = wide_tables(cos_ref[...], sin_ref[...])
    keys = rotate_rows(k_ref[...].astype(F32), cos, sin)
    kt_ref[...] = keys.T.astype(BF16)
    keys = keys.astype(BF16)
    vals = (v_ref[...].astype(F32) + dot(low[RANK:], wv_ref[...], 0, 0)).astype(BF16)
    seg_here = seg_ref[...].astype(F32)[0:1]
    key = lax.broadcasted_iota(jnp.int32, (tok, tok), 0)
    query = lax.broadcasted_iota(jnp.int32, (tok, tok), 1)
    allowed = (key <= query) & (column(seg_here, tok) == seg_here)
    bias = lanes(jnp.where(allowed, 0.0, NEG_FILL), count)
    q0 = q_ref[...].astype(F32) + SCALE * dot(low[:RANK], wq_ref[...], 0, 0)
    for g in range(0, heads, count):
        cut = slice(g * tok, (g + count) * tok)
        parts = [q0[:, h * HEAD : (h + 1) * HEAD] for h in range(g, g + count)]
        qr = jnp.concatenate([rotate_rows(u, cos, sin).astype(BF16) for u in parts], axis=0)
        qr_ref[cut] = qr
        s_ref[:, cut] = dot(keys, qr, 1, 1) * INV_ROOT + bias
        dp_ref[:, cut] = dot(vals, head_rows(o_ref, g, count), 1, 1)


def softmax_kernel(
    count, send, blocks, heads,
    qr_ref, s_ref, o_ref, seg_ref, pack_ref, base_ref, cos_ref, sin_ref, wv_ref,
    w_ref, kt_ref, dv_ref, code_ref,
):
    tok = o_ref.shape[0]
    halo = send * blocks
    cos, sin = wide_tables(cos_ref[...], sin_ref[...])
    keys = jnp.concatenate([pack_ref[b, 0:send] for b in range(blocks)], axis=0)
    keys = rotate_rows(keys.astype(F32), cos, sin)
    kt_ref[...] = keys.T.astype(BF16)
    keys = keys.astype(BF16)
    seg_here = seg_ref[...].astype(F32)[0:1]
    cols = []
    for b in range(blocks):
        row = pack_ref[b, 2 * send :].astype(F32)[0:1]
        cols.append(column(row, tok)[tok - send :])
    seg_col = jnp.concatenate(cols, axis=0)
    offset = lax.broadcasted_iota(jnp.int32, (halo, tok), 0)
    allowed = (offset + base_ref[0] >= halo) & (seg_col == seg_here)
    bias = lanes(jnp.where(allowed, 0.0, NEG_FILL), count)
    dv = jnp.zeros((tok + halo, HEAD), F32)
    for g in range(0, heads, count):
        cut = slice(g * tok, (g + count) * tok)
        far = dot(keys, qr_ref[cut], 1, 1) * INV_ROOT + bias
        s = jnp.concatenate([s_ref[:, cut], far], axis=0)
        e = jnp.exp(s - jnp.max(s, axis=0, keepdims=True))
        w = e * (1.0 / jnp.sum(e, axis=0, keepdims=True))
        w_ref[:, cut] = w
        dv = dv + dot(w.astype(BF16), head_rows(o_ref, g, count), 1, 0)
    dv_ref[...] = dv
    codes = split_dot(wv_ref[...], by_token(dv, send, tok), 1, 1)
    for b in range(blocks + 1):
        code_ref[b * RANK : (b + 1) * RANK] = codes[:, b * tok : (b + 1) * tok]


def grads_kernel(
    count, send, blocks, heads,
    low_ref, far_ref, pack_ref, o_ref, w_ref, dp_ref, kt_ref, kth_ref, dv_ref, cost_ref, sint_ref, wq_ref, wv_ref,
    code_ref, up_ref, qg_ref,
):
    tok = o_ref.shape[0]
    low = low_ref[...].astype(BF16)
    wv = wv_ref[...]
    vals = []
    for b in range(blocks):
        rows = pack_ref[b, send : 2 * send].astype(F32)
        add = dot(far_ref[b], wv, 0, 0)[tok - send :]
        vals.append((rows + add).astype(BF16))
    vals = jnp.concatenate(vals, axis=0)
    kt = jnp.concatenate([kt_ref[...], kth_ref[...]], axis=1)
    cos, sin = lanes(cost_ref[...], count), lanes(sint_ref[...], count)
    for g in range(0, heads, count):
        cut = slice(g * tok, (g + count) * tok)
        far = dot(vals, head_rows(o_ref, g, count), 1, 1)
        dp = jnp.concatenate([dp_ref[:, cut], far], axis=0)
        w = w_ref[:, cut]
        delta = jnp.sum(w * dp, axis=0, keepdims=True)
        ds = (w * (dp - delta) * INV_ROOT).astype(BF16)
        dq = dot(kt, ds, 1, 0)
        first, second = dq[:HALF], dq[HALF:]
        first, second = first * cos + second * sin, second * cos - first * sin
        turned = jnp.concatenate([first.astype(BF16), second.astype(BF16)], axis=0)
        for h in range(count):
            qg_ref[(g + h) * HEAD : (g + h + 1) * HEAD] = turned[:, h * tok : (h + 1) * tok]
    qg = qg_ref[...]
    code_ref[...] = SCALE * dot(wq_ref[...], qg, 1, 0)
    up_ref[:, : heads * HEAD] = (SCALE * dot(low[:RANK], qg, 1, 1)).astype(up_ref.dtype)
    codes = jnp.concatenate([low[RANK:]] + [far_ref[b] for b in range(blocks)], axis=1)
    up_v = SCALE * split_dot(codes, by_token(dv_ref[...], send, tok), 1, 0)
    up_ref[:, heads * HEAD :] = up_v.astype(up_ref.dtype)


def down_kernel(dl_ref, x_ref, part_ref):
    part_ref[...] = dot(dl_ref[...], x_ref[...], 1, 0)


def partial_kernel(own_ref, x_ref, up_ref, near_ref, part_ref, both_ref):
    part = dot(own_ref[...], x_ref[...], 1, 0).astype(BF16)
    wide, size = part.shape[1], up_ref.shape[1]
    half = both_ref.shape[1] - wide
    part_ref[...] = part
    both_ref[:, :wide] = part
    up = (up_ref[...].astype(F32) + near_ref[...].astype(F32)).astype(BF16)
    both_ref[:RANK, wide:] = up[:, :half]
    both_ref[RANK:, wide : wide + size - half] = up[:, half:]
    if 2 * half > size:
        both_ref[RANK:, wide + size - half :] = jnp.zeros((RANK, 2 * half - size), BF16)


def final_kernel(mine_ref, one_ref, two_ref, three_ref, down_ref, upq_ref, upv_ref):
    wide = one_ref.shape[1]
    near = mine_ref[:, :wide].astype(F32) + one_ref[...].astype(F32)
    far = two_ref[:, :wide].astype(F32) + three_ref[...].astype(F32)
    down_ref[...] = near + far
    up = mine_ref[:, wide:].astype(F32) + two_ref[:, wide:].astype(F32)
    half, size = up.shape[1], upq_ref.shape[1]
    upq_ref[:, :half] = up[:RANK]
    upq_ref[:, half:] = up[RANK:, : size - half]
    upv_ref[...] = up[RANK:, size - half : size - half + HEAD]


def body(x, q, k, v, o, segment, a, wq, wv):
    tok, wide = x.shape
    seq_count = lax.axis_size("seq")
    fsdp_count = lax.axis_size("fsdp")
    seq_index = lax.axis_index("seq")
    heads = q.shape[1] // HEAD
    longest = tok * seq_count // 8
    blocks = -(-longest // tok)
    send = longest if blocks == 1 else tok
    halo = blocks * send
    keys = halo + tok
    direct = seq_count == 4 and fsdp_count == 4

    def swap(array, axis, bit):
        size = lax.axis_size(axis)
        return lax.ppermute(array, axis, [(i, i ^ bit) for i in range(size)])

    def shift(array, by):
        moves = [(i, (i + by) % seq_count) for i in range(seq_count)]
        return lax.ppermute(array, "seq", moves)

    def near(array):
        moves = []
        for i in range(seq_count):
            for f in range(fsdp_count):
                if f % 2 == 0:
                    to, flip = i ^ 1, 0
                elif i in (1, 2):
                    to, flip = 3 - i, 0
                else:
                    to, flip = i, 2
                moves.append((i * fsdp_count + f, to * fsdp_count + (f ^ flip)))
        return lax.ppermute(array, ("seq", "fsdp"), moves)

    def sum_fsdp(array):
        if fsdp_count & (fsdp_count - 1):
            return lax.psum(array, "fsdp")
        bit = 1
        while bit < fsdp_count:
            array = array + swap(array, "fsdp", bit)
            bit *= 2
        return array

    seg_row = segment.reshape(1, tok)
    part, tails, k, v, wq = call(
        functools.partial(lowrank_kernel, send),
        [
            ((2 * RANK, tok), F32),
            ((2 * send, HEAD), BF16),
            ((tok, HEAD), BF16),
            ((tok, HEAD), BF16),
            (wq.shape, BF16),
        ],
        [
            pltpu.VMEM((tok, wide), BF16),
            pltpu.VMEM((2 * RANK, wide), BF16),
            pltpu.SemaphoreType.DMA((5,)),
        ],
        limit=FULL,
        in_specs=[pl.BlockSpec(memory_space=pltpu.HBM)] * 5,
    )(x, a.T, k, v, wq)
    seg_rows = jnp.broadcast_to(seg_row, (16, tok)).astype(BF16)
    pack = jnp.concatenate([tails, seg_rows], axis=0)
    wv = wv * SCALE
    start = seq_index * tok
    base = start.reshape(1).astype(jnp.int32)
    freqs = ROPE_BASE ** (-(2.0 * jnp.arange(HALF, dtype=F32)) / HEAD)
    positions = (start - halo + jnp.arange(keys, dtype=jnp.int32)).astype(F32)
    angles = positions[:, None] * freqs[None, :]
    cos, sin = jnp.cos(angles), jnp.sin(angles)
    packs = jnp.stack([shift(pack, d) for d in range(blocks, 0, -1)])
    low = sum_fsdp(part)
    low, cos, sin, wv = lax.optimization_barrier((low, cos, sin, wv))
    low_v = low[RANK:].astype(BF16)
    if direct:
        far = near(low_v)
    else:
        lows = jnp.stack([shift(low_v, d) for d in range(blocks, 0, -1)])
    count = heads if blocks == 1 else 1
    qr, kt, s, dp, cos_t, sin_t = call(
        functools.partial(project_kernel, count, heads),
        [
            ((heads * tok, HEAD), BF16),
            ((HEAD, tok), BF16),
            ((tok, heads * tok), F32),
            ((tok, heads * tok), F32),
            ((HALF, tok), F32),
            ((HALF, tok), F32),
        ],
        cost=3 << 20,
    )(low, q, k, v, o, seg_rows, cos[halo:], sin[halo:], wq, wv)
    specs = [pl.BlockSpec(memory_space=pltpu.VMEM)] * 9
    specs[5] = pl.BlockSpec(memory_space=pltpu.SMEM)
    w, kt_far, dv, codes_v = call(
        functools.partial(softmax_kernel, count, send, blocks, heads),
        [
            ((keys, heads * tok), F32),
            ((HEAD, halo), BF16),
            ((keys, HEAD), F32),
            (((blocks + 1) * RANK, tok), F32),
        ],
        in_specs=specs,
        cost=5 << 20,
    )(qr, s, o, seg_rows, packs, base, cos[:halo], sin[:halo], wv)
    if direct:
        w, far = lax.optimization_barrier((w, far))
        mine = (seq_index == 2) == (lax.axis_index("fsdp") % 2 == 1)
        lows = jnp.where(mine, far, swap(far, "fsdp", 1))[None]
    code_v = codes_v[:RANK]
    backs = []
    for b, d in enumerate(range(blocks, 0, -1)):
        backs.append(shift(codes_v[(b + 1) * RANK : (b + 2) * RANK], -d))
    code_q, up = call(
        functools.partial(grads_kernel, count, send, blocks, heads),
        [((RANK, tok), F32), ((RANK, (heads + 1) * HEAD), BF16 if direct else F32)],
        [pltpu.VMEM((heads * HEAD, tok), BF16)],
        cost=24 << 20,
    )(low, lows, packs, o, w, dp, kt, kt_far, dv, cos_t, sin_t, wq, wv)
    if not direct:
        code_v = sum(backs, code_v)
        dlow = sum_fsdp(jnp.concatenate([code_q, code_v], axis=0)).astype(BF16)
        (down,) = call(down_kernel, [((2 * RANK, wide), F32)])(dlow, x)
        down, up = lax.psum((down, up), "seq")
        return down.T, up[:, : heads * HEAD], up[:, heads * HEAD :]

    codes = jnp.concatenate([code_q, code_v + backs[0]], axis=0)
    near_up = swap(up, "seq", 1)
    codes = codes + swap(codes, "fsdp", 1)
    codes, near_up = lax.optimization_barrier((codes, near_up))
    dlow = (codes + swap(codes, "fsdp", 2)).astype(BF16)
    half = -(-(heads + 1) // 2) * HEAD
    part, both = call(
        partial_kernel, [((2 * RANK, wide), BF16), ((2 * RANK, wide + half), BF16)]
    )(dlow, x, up, near_up)
    down, up_q, up_v = call(
        final_kernel,
        [((2 * RANK, wide), F32), ((RANK, heads * HEAD), F32), ((RANK, HEAD), F32)],
    )(both, swap(part, "seq", 1), swap(both, "seq", 2), swap(part, "seq", 3))
    return down.T, up_q, up_v


def solution(mesh):
    rows = ("groups", "seq")
    in_specs = (
        P(rows, "fsdp"),
        P(rows, "fsdp"),
        P(rows, "fsdp"),
        P(rows, "fsdp"),
        P(rows, "fsdp"),
        P(rows),
        P("fsdp", None),
        P(None, "fsdp"),
        P(None, "fsdp"),
    )
    out_specs = (P(("groups", "fsdp"), None), P("groups", "fsdp"), P("groups", "fsdp"))
    return jax.shard_map(body, mesh=mesh, in_specs=in_specs, out_specs=out_specs, check_vma=False)
```

```python
import functools
import math

import jax
import jax.numpy as jnp
from jax import lax
from jax.experimental import pallas as pl
from jax.experimental.pallas import tpu as pltpu
from jax.sharding import PartitionSpec as P

HEAD = 128
HALF = HEAD // 2
RANK = 16
SCALE = 2.0
ROPE_BASE = 500000.0
NEG_FILL = -1e30
INV_ROOT = 1.0 / math.sqrt(HEAD)
F32 = jnp.float32
BF16 = jnp.bfloat16
LIMIT = 40 * 1024 * 1024
FULL = 55080 * 1024


def dot(left, right, left_dim, right_dim):
    return lax.dot_general(
        left,
        right,
        (((left_dim,), (right_dim,)), ((), ())),
        preferred_element_type=F32,
    )


def call(kernel, out_shapes, scratch=(), limit=LIMIT, cost=1, **specs):
    return pl.pallas_call(
        kernel,
        out_shape=[jax.ShapeDtypeStruct(s, d) for s, d in out_shapes],
        **specs,
        scratch_shapes=list(scratch),
        compiler_params=pltpu.CompilerParams(vmem_limit_bytes=limit),
        cost_estimate=pl.CostEstimate(flops=cost, bytes_accessed=cost, transcendentals=0),
    )


def lowrank_kernel(send, *refs):
    sources, (part_ref, tails_ref, k_ref, v_ref, wq_ref) = refs[:5], refs[5:10]
    x_ref, a_ref, sems = refs[10:]
    targets = (x_ref, a_ref, k_ref, v_ref, wq_ref)
    copies = []
    for i, (source, target) in enumerate(zip(sources, targets)):
        copies.append(pltpu.make_async_copy(source, target, sems.at[i]))
        copies[-1].start()
    for copy in copies:
        copy.wait()
    part_ref[...] = dot(a_ref[...], x_ref[...], 1, 1)
    tok = k_ref.shape[0]
    tails_ref[0:send] = k_ref[tok - send :]
    tails_ref[send:] = v_ref[tok - send :]


def rotate_rows(u, cos, sin):
    return u * cos + pltpu.roll(u, HALF, 1) * sin


def wide_tables(cos, sin):
    return jnp.concatenate([cos, cos], axis=1), jnp.concatenate([-sin, sin], axis=1)


def column(row, tok):
    return jnp.broadcast_to(row, (tok, tok)).T


def lanes(array, count):
    return jnp.concatenate([array] * count, axis=1)


def head_rows(ref, first, count):
    parts = [ref[:, h * HEAD : (h + 1) * HEAD] for h in range(first, first + count)]
    return jnp.concatenate(parts, axis=0)


def split_dot(left, right, left_dim, right_dim):
    high = right.astype(BF16)
    rest = (right - high.astype(F32)).astype(BF16)
    return dot(left, high, left_dim, right_dim) + dot(left, rest, left_dim, right_dim)


def by_token(array, send, tok):
    if send == tok:
        return array
    gap = jnp.zeros((tok - send, array.shape[1]), array.dtype)
    return jnp.concatenate([array[:tok], gap, array[tok:]], axis=0)


def project_kernel(
    count, heads,
    low_ref, q_ref, k_ref, v_ref, o_ref, seg_ref, cos_ref, sin_ref, wq_ref, wv_ref,
    qr_ref, kt_ref, s_ref, dp_ref, cost_ref, sint_ref,
):
    tok = q_ref.shape[0]
    low = low_ref[...].astype(BF16)
    cost_ref[...] = cos_ref[...].T
    sint_ref[...] = sin_ref[...].T
    cos, sin = wide_tables(cos_ref[...], sin_ref[...])
    keys = rotate_rows(k_ref[...].astype(F32), cos, sin)
    kt_ref[...] = keys.T.astype(BF16)
    keys = keys.astype(BF16)
    vals = (v_ref[...].astype(F32) + dot(low[RANK:], wv_ref[...], 0, 0)).astype(BF16)
    seg_here = seg_ref[...].astype(F32)[0:1]
    key = lax.broadcasted_iota(jnp.int32, (tok, tok), 0)
    query = lax.broadcasted_iota(jnp.int32, (tok, tok), 1)
    allowed = (key <= query) & (column(seg_here, tok) == seg_here)
    bias = lanes(jnp.where(allowed, 0.0, NEG_FILL), count)
    q0 = q_ref[...].astype(F32) + SCALE * dot(low[:RANK], wq_ref[...], 0, 0)
    for g in range(0, heads, count):
        cut = slice(g * tok, (g + count) * tok)
        parts = [q0[:, h * HEAD : (h + 1) * HEAD] for h in range(g, g + count)]
        qr = jnp.concatenate([rotate_rows(u, cos, sin).astype(BF16) for u in parts], axis=0)
        qr_ref[cut] = qr
        s_ref[:, cut] = dot(keys, qr, 1, 1) * INV_ROOT + bias
        dp_ref[:, cut] = dot(vals, head_rows(o_ref, g, count), 1, 1)


def softmax_kernel(
    count, send, blocks, heads,
    qr_ref, s_ref, o_ref, seg_ref, pack_ref, base_ref, cos_ref, sin_ref, wv_ref,
    w_ref, kt_ref, dv_ref, code_ref,
):
    tok = o_ref.shape[0]
    halo = send * blocks
    cos, sin = wide_tables(cos_ref[...], sin_ref[...])
    keys = jnp.concatenate([pack_ref[b, 0:send] for b in range(blocks)], axis=0)
    keys = rotate_rows(keys.astype(F32), cos, sin)
    kt_ref[...] = keys.T.astype(BF16)
    keys = keys.astype(BF16)
    seg_here = seg_ref[...].astype(F32)[0:1]
    cols = []
    for b in range(blocks):
        row = pack_ref[b, 2 * send :].astype(F32)[0:1]
        cols.append(column(row, tok)[tok - send :])
    seg_col = jnp.concatenate(cols, axis=0)
    offset = lax.broadcasted_iota(jnp.int32, (halo, tok), 0)
    allowed = (offset + base_ref[0] >= halo) & (seg_col == seg_here)
    bias = lanes(jnp.where(allowed, 0.0, NEG_FILL), count)
    dv = jnp.zeros((tok + halo, HEAD), F32)
    for g in range(0, heads, count):
        cut = slice(g * tok, (g + count) * tok)
        far = dot(keys, qr_ref[cut], 1, 1) * INV_ROOT + bias
        s = jnp.concatenate([s_ref[:, cut], far], axis=0)
        e = jnp.exp(s - jnp.max(s, axis=0, keepdims=True))
        w = e * (1.0 / jnp.sum(e, axis=0, keepdims=True))
        w_ref[:, cut] = w
        dv = dv + dot(w.astype(BF16), head_rows(o_ref, g, count), 1, 0)
    dv_ref[...] = dv
    codes = split_dot(wv_ref[...], by_token(dv, send, tok), 1, 1)
    for b in range(blocks + 1):
        code_ref[b * RANK : (b + 1) * RANK] = codes[:, b * tok : (b + 1) * tok]


def grads_kernel(
    count, send, blocks, heads,
    low_ref, far_ref, pack_ref, o_ref, w_ref, dp_ref, kt_ref, kth_ref, dv_ref, cost_ref, sint_ref, wq_ref, wv_ref,
    code_ref, up_ref, qg_ref,
):
    tok = o_ref.shape[0]
    low = low_ref[...].astype(BF16)
    wv = wv_ref[...]
    vals = []
    for b in range(blocks):
        rows = pack_ref[b, send : 2 * send].astype(F32)
        add = dot(far_ref[b], wv, 0, 0)[tok - send :]
        vals.append((rows + add).astype(BF16))
    vals = jnp.concatenate(vals, axis=0)
    kt = jnp.concatenate([kt_ref[...], kth_ref[...]], axis=1)
    cos, sin = lanes(cost_ref[...], count), lanes(sint_ref[...], count)
    for g in range(0, heads, count):
        cut = slice(g * tok, (g + count) * tok)
        far = dot(vals, head_rows(o_ref, g, count), 1, 1)
        dp = jnp.concatenate([dp_ref[:, cut], far], axis=0)
        w = w_ref[:, cut]
        delta = jnp.sum(w * dp, axis=0, keepdims=True)
        ds = (w * (dp - delta) * INV_ROOT).astype(BF16)
        dq = dot(kt, ds, 1, 0)
        first, second = dq[:HALF], dq[HALF:]
        first, second = first * cos + second * sin, second * cos - first * sin
        turned = jnp.concatenate([first.astype(BF16), second.astype(BF16)], axis=0)
        for h in range(count):
            qg_ref[(g + h) * HEAD : (g + h + 1) * HEAD] = turned[:, h * tok : (h + 1) * tok]
    qg = qg_ref[...]
    code_ref[...] = SCALE * dot(wq_ref[...], qg, 1, 0)
    up_ref[:, : heads * HEAD] = (SCALE * dot(low[:RANK], qg, 1, 1)).astype(up_ref.dtype)
    codes = jnp.concatenate([low[RANK:]] + [far_ref[b] for b in range(blocks)], axis=1)
    up_v = SCALE * split_dot(codes, by_token(dv_ref[...], send, tok), 1, 0)
    up_ref[:, heads * HEAD :] = up_v.astype(up_ref.dtype)


def down_kernel(dl_ref, x_ref, part_ref):
    part_ref[...] = dot(dl_ref[...], x_ref[...], 1, 0)


def partial_kernel(own_ref, x_ref, up_ref, send_ref):
    part = dot(own_ref[...], x_ref[...], 1, 0).astype(BF16)
    wide, size = part.shape[1], up_ref.shape[1]
    half = send_ref.shape[1] - wide
    send_ref[:, :wide] = part
    send_ref[:RANK, wide:] = up_ref[:, :half]
    send_ref[RANK:, wide : wide + size - half] = up_ref[:, half:]
    if 2 * half > size:
        send_ref[RANK:, wide + size - half :] = jnp.zeros((RANK, 2 * half - size), BF16)


def final_kernel(mine_ref, three_ref, two_ref, one_ref, down_ref, upq_ref, upv_ref):
    near = mine_ref[...].astype(F32) + one_ref[...].astype(F32)
    far = two_ref[...].astype(F32) + three_ref[...].astype(F32)
    total = near + far
    wide, size = down_ref.shape[1], upq_ref.shape[1]
    half = total.shape[1] - wide
    down_ref[...] = total[:, :wide]
    upq_ref[:, :half] = total[:RANK, wide:]
    upq_ref[:, half:] = total[RANK:, wide : wide + size - half]
    upv_ref[...] = total[RANK:, wide + size - half : wide + size - half + HEAD]


def body(x, q, k, v, o, segment, a, wq, wv):
    tok, wide = x.shape
    seq_count = lax.axis_size("seq")
    fsdp_count = lax.axis_size("fsdp")
    seq_index = lax.axis_index("seq")
    heads = q.shape[1] // HEAD
    longest = tok * seq_count // 8
    blocks = -(-longest // tok)
    send = longest if blocks == 1 else tok
    halo = blocks * send
    keys = halo + tok
    direct = seq_count == 4 and fsdp_count == 4

    def swap(array, axis, bit):
        size = lax.axis_size(axis)
        return lax.ppermute(array, axis, [(i, i ^ bit) for i in range(size)])

    def shift(array, by):
        moves = [(i, (i + by) % seq_count) for i in range(seq_count)]
        return lax.ppermute(array, "seq", moves)

    def near(array):
        moves = []
        for i in range(seq_count):
            for f in range(fsdp_count):
                if f % 2 == 0:
                    to, flip = i ^ 1, 0
                elif i in (1, 2):
                    to, flip = 3 - i, 0
                else:
                    to, flip = i, 2
                moves.append((i * fsdp_count + f, to * fsdp_count + (f ^ flip)))
        return lax.ppermute(array, ("seq", "fsdp"), moves)

    def sum_fsdp(array):
        if fsdp_count != 4:
            return lax.psum(array, "fsdp")
        one, two, three = [swap(array, "fsdp", bit) for bit in (1, 2, 3)]
        return (array + one) + (two + three)

    seg_row = segment.reshape(1, tok)
    part, tails, k, v, wq = call(
        functools.partial(lowrank_kernel, send),
        [
            ((2 * RANK, tok), F32),
            ((2 * send, HEAD), BF16),
            ((tok, HEAD), BF16),
            ((tok, HEAD), BF16),
            (wq.shape, BF16),
        ],
        [
            pltpu.VMEM((tok, wide), BF16),
            pltpu.VMEM((2 * RANK, wide), BF16),
            pltpu.SemaphoreType.DMA((5,)),
        ],
        limit=FULL,
        in_specs=[pl.BlockSpec(memory_space=pltpu.HBM)] * 5,
    )(x, a.T, k, v, wq)
    seg_rows = jnp.broadcast_to(seg_row, (16, tok)).astype(BF16)
    pack = jnp.concatenate([tails, seg_rows], axis=0)
    wv = wv * SCALE
    start = seq_index * tok
    base = start.reshape(1).astype(jnp.int32)
    freqs = ROPE_BASE ** (-(2.0 * jnp.arange(HALF, dtype=F32)) / HEAD)
    positions = (start - halo + jnp.arange(keys, dtype=jnp.int32)).astype(F32)
    angles = positions[:, None] * freqs[None, :]
    cos, sin = jnp.cos(angles), jnp.sin(angles)
    packs = jnp.stack([shift(pack, d) for d in range(blocks, 0, -1)])
    low = sum_fsdp(part)
    low, cos, sin, wv = lax.optimization_barrier((low, cos, sin, wv))
    low_v = low[RANK:].astype(BF16)
    if direct:
        far = near(low_v)
    else:
        lows = jnp.stack([shift(low_v, d) for d in range(blocks, 0, -1)])
    count = heads if blocks == 1 else 1
    qr, kt, s, dp, cos_t, sin_t = call(
        functools.partial(project_kernel, count, heads),
        [
            ((heads * tok, HEAD), BF16),
            ((HEAD, tok), BF16),
            ((tok, heads * tok), F32),
            ((tok, heads * tok), F32),
            ((HALF, tok), F32),
            ((HALF, tok), F32),
        ],
        cost=3 << 20,
    )(low, q, k, v, o, seg_rows, cos[halo:], sin[halo:], wq, wv)
    specs = [pl.BlockSpec(memory_space=pltpu.VMEM)] * 9
    specs[5] = pl.BlockSpec(memory_space=pltpu.SMEM)
    w, kt_far, dv, codes_v = call(
        functools.partial(softmax_kernel, count, send, blocks, heads),
        [
            ((keys, heads * tok), F32),
            ((HEAD, halo), BF16),
            ((keys, HEAD), F32),
            (((blocks + 1) * RANK, tok), F32),
        ],
        in_specs=specs,
        cost=5 << 20,
    )(qr, s, o, seg_rows, packs, base, cos[:halo], sin[:halo], wv)
    if direct:
        w, far = lax.optimization_barrier((w, far))
        mine = (seq_index == 2) == (lax.axis_index("fsdp") % 2 == 1)
        lows = jnp.where(mine, far, swap(far, "fsdp", 1))[None]
    code_v = codes_v[:RANK]
    backs = []
    for b, d in enumerate(range(blocks, 0, -1)):
        backs.append(shift(codes_v[(b + 1) * RANK : (b + 2) * RANK], -d))
    code_q, up = call(
        functools.partial(grads_kernel, count, send, blocks, heads),
        [((RANK, tok), F32), ((RANK, (heads + 1) * HEAD), BF16 if direct else F32)],
        [pltpu.VMEM((heads * HEAD, tok), BF16)],
        cost=24 << 20,
    )(low, lows, packs, o, w, dp, kt, kt_far, dv, cos_t, sin_t, wq, wv)
    if not direct:
        code_v = sum(backs, code_v)
        dlow = sum_fsdp(jnp.concatenate([code_q, code_v], axis=0)).astype(BF16)
        (down,) = call(down_kernel, [((2 * RANK, wide), F32)])(dlow, x)
        down, up = lax.psum((down, up), "seq")
        return down.T, up[:, : heads * HEAD], up[:, heads * HEAD :]

    codes = jnp.concatenate([code_q, code_v + backs[0]], axis=0)
    dlow = sum_fsdp(codes).astype(BF16)
    half = -(-(heads + 1) // 2) * HEAD
    (mine,) = call(partial_kernel, [((2 * RANK, wide + half), BF16)])(dlow, x, up)
    three, two, one = [swap(mine, "seq", bit) for bit in (3, 2, 1)]
    down, up_q, up_v = call(
        final_kernel,
        [((2 * RANK, wide), F32), ((RANK, heads * HEAD), F32), ((RANK, HEAD), F32)],
    )(mine, three, two, one)
    return down.T, up_q, up_v


def solution(mesh):
    rows = ("groups", "seq")
    in_specs = (
        P(rows, "fsdp"),
        P(rows, "fsdp"),
        P(rows, "fsdp"),
        P(rows, "fsdp"),
        P(rows, "fsdp"),
        P(rows),
        P("fsdp", None),
        P(None, "fsdp"),
        P(None, "fsdp"),
    )
    out_specs = (P(("groups", "fsdp"), None), P("groups", "fsdp"), P("groups", "fsdp"))
    return jax.shard_map(body, mesh=mesh, in_specs=in_specs, out_specs=out_specs, check_vma=False)
```

```python
import functools
import math

import jax
import jax.numpy as jnp
from jax import lax
from jax.experimental import pallas as pl
from jax.experimental.pallas import tpu as pltpu
from jax.sharding import PartitionSpec as P

HEAD = 128
HALF = HEAD // 2
RANK = 16
SCALE = 2.0
ROPE_BASE = 500000.0
NEG_FILL = -1e30
INV_ROOT = 1.0 / math.sqrt(HEAD)
F32 = jnp.float32
BF16 = jnp.bfloat16
LIMIT = 40 * 1024 * 1024
FULL = 55080 * 1024


def dot(left, right, left_dim, right_dim):
    return lax.dot_general(
        left,
        right,
        (((left_dim,), (right_dim,)), ((), ())),
        preferred_element_type=F32,
    )


def call(kernel, out_shapes, scratch=(), limit=LIMIT, cost=1, **specs):
    return pl.pallas_call(
        kernel,
        out_shape=[jax.ShapeDtypeStruct(s, d) for s, d in out_shapes],
        **specs,
        scratch_shapes=list(scratch),
        compiler_params=pltpu.CompilerParams(vmem_limit_bytes=limit),
        cost_estimate=pl.CostEstimate(flops=cost, bytes_accessed=cost, transcendentals=0),
    )


def lowrank_kernel(send, *refs):
    sources, (part_ref, tails_ref, k_ref, v_ref, wq_ref) = refs[:5], refs[5:10]
    x_ref, a_ref, sems = refs[10:]
    targets = (x_ref, a_ref, k_ref, v_ref, wq_ref)
    copies = []
    for i, (source, target) in enumerate(zip(sources, targets)):
        copies.append(pltpu.make_async_copy(source, target, sems.at[i]))
        copies[-1].start()
    for copy in copies:
        copy.wait()
    part_ref[...] = dot(a_ref[...], x_ref[...], 1, 1)
    tok = k_ref.shape[0]
    tails_ref[0:send] = k_ref[tok - send :]
    tails_ref[send:] = v_ref[tok - send :]


def rotate_rows(u, cos, sin):
    return u * cos + pltpu.roll(u, HALF, 1) * sin


def wide_tables(cos, sin):
    return jnp.concatenate([cos, cos], axis=1), jnp.concatenate([-sin, sin], axis=1)


def column(row, tok):
    return jnp.broadcast_to(row, (tok, tok)).T


def lanes(array, count):
    return jnp.concatenate([array] * count, axis=1)


def head_rows(ref, first, count):
    parts = [ref[:, h * HEAD : (h + 1) * HEAD] for h in range(first, first + count)]
    return jnp.concatenate(parts, axis=0)


def split_dot(left, right, left_dim, right_dim):
    high = right.astype(BF16)
    rest = (right - high.astype(F32)).astype(BF16)
    return dot(left, high, left_dim, right_dim) + dot(left, rest, left_dim, right_dim)


def by_token(array, send, tok):
    if send == tok:
        return array
    gap = jnp.zeros((tok - send, array.shape[1]), array.dtype)
    return jnp.concatenate([array[:tok], gap, array[tok:]], axis=0)


def project_kernel(
    count, heads,
    low_ref, q_ref, k_ref, v_ref, o_ref, seg_ref, cos_ref, sin_ref, wq_ref, wv_ref,
    qr_ref, kt_ref, s_ref, dp_ref, cost_ref, sint_ref,
):
    tok = q_ref.shape[0]
    low = low_ref[...].astype(BF16)
    cost_ref[...] = cos_ref[...].T
    sint_ref[...] = sin_ref[...].T
    cos, sin = wide_tables(cos_ref[...], sin_ref[...])
    keys = rotate_rows(k_ref[...].astype(F32), cos, sin)
    kt_ref[...] = keys.T.astype(BF16)
    keys = keys.astype(BF16)
    vals = (v_ref[...].astype(F32) + dot(low[RANK:], wv_ref[...], 0, 0)).astype(BF16)
    seg_here = seg_ref[...].astype(F32)[0:1]
    key = lax.broadcasted_iota(jnp.int32, (tok, tok), 0)
    query = lax.broadcasted_iota(jnp.int32, (tok, tok), 1)
    allowed = (key <= query) & (column(seg_here, tok) == seg_here)
    bias = lanes(jnp.where(allowed, 0.0, NEG_FILL), count)
    q0 = q_ref[...].astype(F32) + SCALE * dot(low[:RANK], wq_ref[...], 0, 0)
    for g in range(0, heads, count):
        cut = slice(g * tok, (g + count) * tok)
        parts = [q0[:, h * HEAD : (h + 1) * HEAD] for h in range(g, g + count)]
        qr = jnp.concatenate([rotate_rows(u, cos, sin).astype(BF16) for u in parts], axis=0)
        qr_ref[cut] = qr
        s_ref[:, cut] = dot(keys, qr, 1, 1) * INV_ROOT + bias
        dp_ref[:, cut] = dot(vals, head_rows(o_ref, g, count), 1, 1)


def softmax_kernel(
    count, send, blocks, heads,
    qr_ref, s_ref, o_ref, seg_ref, pack_ref, base_ref, cos_ref, sin_ref, wv_ref,
    w_ref, kt_ref, dv_ref, code_ref,
):
    tok = o_ref.shape[0]
    halo = send * blocks
    cos, sin = wide_tables(cos_ref[...], sin_ref[...])
    keys = jnp.concatenate([pack_ref[b, 0:send] for b in range(blocks)], axis=0)
    keys = rotate_rows(keys.astype(F32), cos, sin)
    kt_ref[...] = keys.T.astype(BF16)
    keys = keys.astype(BF16)
    seg_here = seg_ref[...].astype(F32)[0:1]
    cols = []
    for b in range(blocks):
        row = pack_ref[b, 2 * send :].astype(F32)[0:1]
        cols.append(column(row, tok)[tok - send :])
    seg_col = jnp.concatenate(cols, axis=0)
    offset = lax.broadcasted_iota(jnp.int32, (halo, tok), 0)
    allowed = (offset + base_ref[0] >= halo) & (seg_col == seg_here)
    bias = lanes(jnp.where(allowed, 0.0, NEG_FILL), count)
    dv = jnp.zeros((tok + halo, HEAD), F32)
    for g in range(0, heads, count):
        cut = slice(g * tok, (g + count) * tok)
        far = dot(keys, qr_ref[cut], 1, 1) * INV_ROOT + bias
        s = jnp.concatenate([s_ref[:, cut], far], axis=0)
        e = jnp.exp(s - jnp.max(s, axis=0, keepdims=True))
        w = e * (1.0 / jnp.sum(e, axis=0, keepdims=True))
        w_ref[:, cut] = w
        dv = dv + dot(w.astype(BF16), head_rows(o_ref, g, count), 1, 0)
    dv_ref[...] = dv
    codes = split_dot(wv_ref[...], by_token(dv, send, tok), 1, 1)
    for b in range(blocks + 1):
        code_ref[b * RANK : (b + 1) * RANK] = codes[:, b * tok : (b + 1) * tok]


def grads_kernel(
    count, send, blocks, heads,
    low_ref, far_ref, pack_ref, o_ref, w_ref, dp_ref, kt_ref, kth_ref, dv_ref, cost_ref, sint_ref, wq_ref, wv_ref,
    code_ref, up_ref, qg_ref,
):
    tok = o_ref.shape[0]
    low = low_ref[...].astype(BF16)
    wv = wv_ref[...]
    vals = []
    for b in range(blocks):
        rows = pack_ref[b, send : 2 * send].astype(F32)
        add = dot(far_ref[b], wv, 0, 0)[tok - send :]
        vals.append((rows + add).astype(BF16))
    vals = jnp.concatenate(vals, axis=0)
    kt = jnp.concatenate([kt_ref[...], kth_ref[...]], axis=1)
    cos, sin = lanes(cost_ref[...], count), lanes(sint_ref[...], count)
    for g in range(0, heads, count):
        cut = slice(g * tok, (g + count) * tok)
        far = dot(vals, head_rows(o_ref, g, count), 1, 1)
        dp = jnp.concatenate([dp_ref[:, cut], far], axis=0)
        w = w_ref[:, cut]
        delta = jnp.sum(w * dp, axis=0, keepdims=True)
        ds = (w * (dp - delta) * INV_ROOT).astype(BF16)
        dq = dot(kt, ds, 1, 0)
        first, second = dq[:HALF], dq[HALF:]
        first, second = first * cos + second * sin, second * cos - first * sin
        turned = jnp.concatenate([first.astype(BF16), second.astype(BF16)], axis=0)
        for h in range(count):
            qg_ref[(g + h) * HEAD : (g + h + 1) * HEAD] = turned[:, h * tok : (h + 1) * tok]
    qg = qg_ref[...]
    code_ref[...] = SCALE * dot(wq_ref[...], qg, 1, 0)
    up_ref[:, : heads * HEAD] = (SCALE * dot(low[:RANK], qg, 1, 1)).astype(up_ref.dtype)
    codes = jnp.concatenate([low[RANK:]] + [far_ref[b] for b in range(blocks)], axis=1)
    up_v = SCALE * split_dot(codes, by_token(dv_ref[...], send, tok), 1, 0)
    up_ref[:, heads * HEAD :] = up_v.astype(up_ref.dtype)


def down_kernel(dl_ref, x_ref, part_ref):
    part_ref[...] = dot(dl_ref[...], x_ref[...], 1, 0)


def partial_kernel(own_ref, x_ref, up_ref, send_ref):
    part = dot(own_ref[...], x_ref[...], 1, 0).astype(BF16)
    wide, size = part.shape[1], up_ref.shape[1]
    half = send_ref.shape[1] - wide
    send_ref[:, :wide] = part
    send_ref[:RANK, wide:] = up_ref[:, :half]
    send_ref[RANK:, wide : wide + size - half] = up_ref[:, half:]
    if 2 * half > size:
        send_ref[RANK:, wide + size - half :] = jnp.zeros((RANK, 2 * half - size), BF16)


def final_kernel(mine_ref, three_ref, two_ref, one_ref, down_ref, upq_ref, upv_ref):
    near = mine_ref[...].astype(F32) + one_ref[...].astype(F32)
    far = two_ref[...].astype(F32) + three_ref[...].astype(F32)
    total = near + far
    wide, size = down_ref.shape[1], upq_ref.shape[1]
    half = total.shape[1] - wide
    down_ref[...] = total[:, :wide]
    upq_ref[:, :half] = total[:RANK, wide:]
    upq_ref[:, half:] = total[RANK:, wide : wide + size - half]
    upv_ref[...] = total[RANK:, wide + size - half : wide + size - half + HEAD]


def body(x, q, k, v, o, segment, a, wq, wv):
    tok, wide = x.shape
    seq_count = lax.axis_size("seq")
    fsdp_count = lax.axis_size("fsdp")
    seq_index = lax.axis_index("seq")
    heads = q.shape[1] // HEAD
    longest = tok * seq_count // 8
    blocks = -(-longest // tok)
    send = longest if blocks == 1 else tok
    halo = blocks * send
    keys = halo + tok
    direct = seq_count == 4 and fsdp_count == 4

    def swap(array, axis, bit):
        size = lax.axis_size(axis)
        return lax.ppermute(array, axis, [(i, i ^ bit) for i in range(size)])

    def shift(array, by):
        moves = [(i, (i + by) % seq_count) for i in range(seq_count)]
        return lax.ppermute(array, "seq", moves)

    def inner(array, even):
        moves = []
        for i in range(seq_count):
            for f in range(fsdp_count):
                if even and f % 2 == 0:
                    to, flip = i ^ 1, 0
                elif i in (1, 2):
                    to, flip = 3 - i, 0
                else:
                    to, flip = i, 2
                moves.append((i * fsdp_count + f, to * fsdp_count + (f ^ flip)))
        return lax.ppermute(array, ("seq", "fsdp"), moves)

    def sum_fsdp(array):
        if fsdp_count != 4:
            return lax.psum(array, "fsdp")
        one, two, three = [swap(array, "fsdp", bit) for bit in (1, 2, 3)]
        return (array + one) + (two + three)

    seg_row = segment.reshape(1, tok)
    part, tails, k, v, wq = call(
        functools.partial(lowrank_kernel, send),
        [
            ((2 * RANK, tok), F32),
            ((2 * send, HEAD), BF16),
            ((tok, HEAD), BF16),
            ((tok, HEAD), BF16),
            (wq.shape, BF16),
        ],
        [
            pltpu.VMEM((tok, wide), BF16),
            pltpu.VMEM((2 * RANK, wide), BF16),
            pltpu.SemaphoreType.DMA((5,)),
        ],
        limit=FULL,
        in_specs=[pl.BlockSpec(memory_space=pltpu.HBM)] * 5,
    )(x, a.T, k, v, wq)
    seg_rows = jnp.broadcast_to(seg_row, (16, tok)).astype(BF16)
    pack = jnp.concatenate([tails, seg_rows], axis=0)
    wv = wv * SCALE
    start = seq_index * tok
    base = start.reshape(1).astype(jnp.int32)
    freqs = ROPE_BASE ** (-(2.0 * jnp.arange(HALF, dtype=F32)) / HEAD)
    positions = (start - halo + jnp.arange(keys, dtype=jnp.int32)).astype(F32)
    angles = positions[:, None] * freqs[None, :]
    cos, sin = jnp.cos(angles), jnp.sin(angles)
    packs = jnp.stack([shift(pack, d) for d in range(blocks, 0, -1)])
    low = sum_fsdp(part)
    low, cos, sin, wv = lax.optimization_barrier((low, cos, sin, wv))
    low_v = low[RANK:].astype(BF16)
    if direct:
        far = inner(low_v, True)
    else:
        lows = jnp.stack([shift(low_v, d) for d in range(blocks, 0, -1)])
    count = heads if blocks == 1 else 1
    qr, kt, s, dp, cos_t, sin_t = call(
        functools.partial(project_kernel, count, heads),
        [
            ((heads * tok, HEAD), BF16),
            ((HEAD, tok), BF16),
            ((tok, heads * tok), F32),
            ((tok, heads * tok), F32),
            ((HALF, tok), F32),
            ((HALF, tok), F32),
        ],
        cost=3 << 20,
    )(low, q, k, v, o, seg_rows, cos[halo:], sin[halo:], wq, wv)
    specs = [pl.BlockSpec(memory_space=pltpu.VMEM)] * 9
    specs[5] = pl.BlockSpec(memory_space=pltpu.SMEM)
    w, kt_far, dv, codes_v = call(
        functools.partial(softmax_kernel, count, send, blocks, heads),
        [
            ((keys, heads * tok), F32),
            ((HEAD, halo), BF16),
            ((keys, HEAD), F32),
            (((blocks + 1) * RANK, tok), F32),
        ],
        in_specs=specs,
        cost=5 << 20,
    )(qr, s, o, seg_rows, packs, base, cos[:halo], sin[:halo], wv)
    if direct:
        w, far = lax.optimization_barrier((w, far))
        mine = (seq_index == 2) == (lax.axis_index("fsdp") % 2 == 1)
        lows = jnp.where(mine, far, swap(far, "fsdp", 1))[None]
    code_v = codes_v[:RANK]
    if direct:
        above, below = swap(codes_v[RANK:], "seq", 1), inner(codes_v[RANK:], False)
        backs = jnp.where(seq_index % 2 == 0, above, jnp.where(seq_index == 1, below, 0.0))
    code_q, up = call(
        functools.partial(grads_kernel, count, send, blocks, heads),
        [((RANK, tok), F32), ((RANK, (heads + 1) * HEAD), BF16 if direct else F32)],
        [pltpu.VMEM((heads * HEAD, tok), BF16)],
        cost=24 << 20,
    )(low, lows, packs, o, w, dp, kt, kt_far, dv, cos_t, sin_t, wq, wv)
    if not direct:
        for b, d in enumerate(range(blocks, 0, -1)):
            code_v = code_v + shift(codes_v[(b + 1) * RANK : (b + 2) * RANK], -d)
        dlow = sum_fsdp(jnp.concatenate([code_q, code_v], axis=0)).astype(BF16)
        (down,) = call(down_kernel, [((2 * RANK, wide), F32)])(dlow, x)
        down, up = lax.psum((down, up), "seq")
        return down.T, up[:, : heads * HEAD], up[:, heads * HEAD :]

    codes = jnp.concatenate([code_q, code_v + backs], axis=0)
    dlow = sum_fsdp(codes).astype(BF16)
    half = -(-(heads + 1) // 2) * HEAD
    (mine,) = call(partial_kernel, [((2 * RANK, wide + half), BF16)])(dlow, x, up)
    three, two, one = [swap(mine, "seq", bit) for bit in (3, 2, 1)]
    down, up_q, up_v = call(
        final_kernel,
        [((2 * RANK, wide), F32), ((RANK, heads * HEAD), F32), ((RANK, HEAD), F32)],
    )(mine, three, two, one)
    return down.T, up_q, up_v


def solution(mesh):
    rows = ("groups", "seq")
    in_specs = (
        P(rows, "fsdp"),
        P(rows, "fsdp"),
        P(rows, "fsdp"),
        P(rows, "fsdp"),
        P(rows, "fsdp"),
        P(rows),
        P("fsdp", None),
        P(None, "fsdp"),
        P(None, "fsdp"),
    )
    out_specs = (P(("groups", "fsdp"), None), P("groups", "fsdp"), P("groups", "fsdp"))
    return jax.shard_map(body, mesh=mesh, in_specs=in_specs, out_specs=out_specs, check_vma=False)
```

```python
import functools
import math

import jax
import jax.numpy as jnp
from jax import lax
from jax.experimental import pallas as pl
from jax.experimental.pallas import tpu as pltpu
from jax.sharding import PartitionSpec as P

HEAD = 128
HALF = HEAD // 2
RANK = 16
SCALE = 2.0
ROPE_BASE = 500000.0
NEG_FILL = -1e30
INV_ROOT = 1.0 / math.sqrt(HEAD)
F32 = jnp.float32
BF16 = jnp.bfloat16
LIMIT = 40 * 1024 * 1024
FULL = 55080 * 1024


def dot(left, right, left_dim, right_dim):
    return lax.dot_general(
        left,
        right,
        (((left_dim,), (right_dim,)), ((), ())),
        preferred_element_type=F32,
    )


def call(kernel, out_shapes, scratch=(), limit=LIMIT, cost=1, **specs):
    return pl.pallas_call(
        kernel,
        out_shape=[jax.ShapeDtypeStruct(s, d) for s, d in out_shapes],
        **specs,
        scratch_shapes=list(scratch),
        compiler_params=pltpu.CompilerParams(vmem_limit_bytes=limit),
        cost_estimate=pl.CostEstimate(flops=cost, bytes_accessed=cost, transcendentals=0),
    )


def lowrank_kernel(send, *refs):
    sources, (part_ref, tails_ref, k_ref, v_ref, wq_ref) = refs[:5], refs[5:10]
    x_ref, a_ref, sems = refs[10:]
    targets = (x_ref, a_ref, k_ref, v_ref, wq_ref)
    copies = []
    for i, (source, target) in enumerate(zip(sources, targets)):
        copies.append(pltpu.make_async_copy(source, target, sems.at[i]))
        copies[-1].start()
    for copy in copies:
        copy.wait()
    part_ref[...] = dot(a_ref[...], x_ref[...], 1, 1)
    tok = k_ref.shape[0]
    tails_ref[0:send] = k_ref[tok - send :]
    tails_ref[send:] = v_ref[tok - send :]


def rotate_rows(u, cos, sin):
    return u * cos + pltpu.roll(u, HALF, 1) * sin


def wide_tables(cos, sin):
    return jnp.concatenate([cos, cos], axis=1), jnp.concatenate([-sin, sin], axis=1)


def column(row, tok):
    return jnp.broadcast_to(row, (tok, tok)).T


def lanes(array, count):
    return jnp.concatenate([array] * count, axis=1)


def head_rows(ref, first, count):
    parts = [ref[:, h * HEAD : (h + 1) * HEAD] for h in range(first, first + count)]
    return jnp.concatenate(parts, axis=0)


def split_dot(left, right, left_dim, right_dim):
    high = right.astype(BF16)
    rest = (right - high.astype(F32)).astype(BF16)
    return dot(left, high, left_dim, right_dim) + dot(left, rest, left_dim, right_dim)


def by_token(array, send, tok):
    if send == tok:
        return array
    gap = jnp.zeros((tok - send, array.shape[1]), array.dtype)
    return jnp.concatenate([array[:tok], gap, array[tok:]], axis=0)


def project_kernel(
    count, heads,
    low_ref, q_ref, k_ref, v_ref, o_ref, seg_ref, cos_ref, sin_ref, wq_ref, wv_ref,
    qr_ref, kt_ref, s_ref, dp_ref, cost_ref, sint_ref,
):
    tok = q_ref.shape[0]
    low = low_ref[...].astype(BF16)
    cost_ref[...] = cos_ref[...].T
    sint_ref[...] = sin_ref[...].T
    cos, sin = wide_tables(cos_ref[...], sin_ref[...])
    keys = rotate_rows(k_ref[...].astype(F32), cos, sin)
    kt_ref[...] = keys.T.astype(BF16)
    keys = keys.astype(BF16)
    vals = (v_ref[...].astype(F32) + dot(low[RANK:], wv_ref[...], 0, 0)).astype(BF16)
    seg_here = seg_ref[...].astype(F32)[0:1]
    key = lax.broadcasted_iota(jnp.int32, (tok, tok), 0)
    query = lax.broadcasted_iota(jnp.int32, (tok, tok), 1)
    allowed = (key <= query) & (column(seg_here, tok) == seg_here)
    bias = lanes(jnp.where(allowed, 0.0, NEG_FILL), count)
    q0 = q_ref[...].astype(F32) + SCALE * dot(low[:RANK], wq_ref[...], 0, 0)
    for g in range(0, heads, count):
        cut = slice(g * tok, (g + count) * tok)
        parts = [q0[:, h * HEAD : (h + 1) * HEAD] for h in range(g, g + count)]
        qr = jnp.concatenate([rotate_rows(u, cos, sin).astype(BF16) for u in parts], axis=0)
        qr_ref[cut] = qr
        s_ref[:, cut] = dot(keys, qr, 1, 1) * INV_ROOT + bias
        dp_ref[:, cut] = dot(vals, head_rows(o_ref, g, count), 1, 1)


def softmax_kernel(
    count, send, blocks, heads,
    qr_ref, s_ref, o_ref, seg_ref, pack_ref, base_ref, cos_ref, sin_ref, wv_ref,
    w_ref, kt_ref, dv_ref, code_ref,
):
    tok = o_ref.shape[0]
    halo = send * blocks
    cos, sin = wide_tables(cos_ref[...], sin_ref[...])
    keys = jnp.concatenate([pack_ref[b, 0:send] for b in range(blocks)], axis=0)
    keys = rotate_rows(keys.astype(F32), cos, sin)
    kt_ref[...] = keys.T.astype(BF16)
    keys = keys.astype(BF16)
    seg_here = seg_ref[...].astype(F32)[0:1]
    cols = []
    for b in range(blocks):
        row = pack_ref[b, 2 * send :].astype(F32)[0:1]
        cols.append(column(row, tok)[tok - send :])
    seg_col = jnp.concatenate(cols, axis=0)
    offset = lax.broadcasted_iota(jnp.int32, (halo, tok), 0)
    allowed = (offset + base_ref[0] >= halo) & (seg_col == seg_here)
    bias = lanes(jnp.where(allowed, 0.0, NEG_FILL), count)
    dv = jnp.zeros((tok + halo, HEAD), F32)
    for g in range(0, heads, count):
        cut = slice(g * tok, (g + count) * tok)
        far = dot(keys, qr_ref[cut], 1, 1) * INV_ROOT + bias
        s = jnp.concatenate([s_ref[:, cut], far], axis=0)
        e = jnp.exp(s - jnp.max(s, axis=0, keepdims=True))
        w = e * (1.0 / jnp.sum(e, axis=0, keepdims=True))
        w_ref[:, cut] = w
        dv = dv + dot(w.astype(BF16), head_rows(o_ref, g, count), 1, 0)
    dv_ref[...] = dv
    codes = split_dot(wv_ref[...], by_token(dv, send, tok), 1, 1)
    for b in range(blocks + 1):
        code_ref[b * RANK : (b + 1) * RANK] = codes[:, b * tok : (b + 1) * tok]


def grads_kernel(
    count, send, blocks, heads,
    low_ref, far_ref, pack_ref, o_ref, w_ref, dp_ref, kt_ref, kth_ref, dv_ref, cost_ref, sint_ref, wq_ref, wv_ref,
    code_ref, up_ref, qg_ref,
):
    tok = o_ref.shape[0]
    low = low_ref[...].astype(BF16)
    wv = wv_ref[...]
    vals = []
    for b in range(blocks):
        rows = pack_ref[b, send : 2 * send].astype(F32)
        add = dot(far_ref[b], wv, 0, 0)[tok - send :]
        vals.append((rows + add).astype(BF16))
    vals = jnp.concatenate(vals, axis=0)
    kt = jnp.concatenate([kt_ref[...], kth_ref[...]], axis=1)
    cos, sin = lanes(cost_ref[...], count), lanes(sint_ref[...], count)
    for g in range(0, heads, count):
        cut = slice(g * tok, (g + count) * tok)
        far = dot(vals, head_rows(o_ref, g, count), 1, 1)
        dp = jnp.concatenate([dp_ref[:, cut], far], axis=0)
        w = w_ref[:, cut]
        delta = jnp.sum(w * dp, axis=0, keepdims=True)
        ds = (w * (dp - delta) * INV_ROOT).astype(BF16)
        dq = dot(kt, ds, 1, 0)
        first, second = dq[:HALF], dq[HALF:]
        first, second = first * cos + second * sin, second * cos - first * sin
        turned = jnp.concatenate([first.astype(BF16), second.astype(BF16)], axis=0)
        for h in range(count):
            qg_ref[(g + h) * HEAD : (g + h + 1) * HEAD] = turned[:, h * tok : (h + 1) * tok]
    qg = qg_ref[...]
    code_ref[...] = SCALE * dot(wq_ref[...], qg, 1, 0)
    up_ref[:, : heads * HEAD] = (SCALE * dot(low[:RANK], qg, 1, 1)).astype(up_ref.dtype)
    codes = jnp.concatenate([low[RANK:]] + [far_ref[b] for b in range(blocks)], axis=1)
    up_v = SCALE * split_dot(codes, by_token(dv_ref[...], send, tok), 1, 0)
    up_ref[:, heads * HEAD :] = up_v.astype(up_ref.dtype)


def down_kernel(dl_ref, x_ref, part_ref):
    part_ref[...] = dot(dl_ref[...], x_ref[...], 1, 0)


def partial_kernel(own_ref, x_ref, up_ref, near_ref, part_ref, both_ref):
    part = dot(own_ref[...], x_ref[...], 1, 0).astype(BF16)
    wide = part.shape[1]
    part_ref[...] = part
    both_ref[:, :wide] = part[:RANK]
    both_ref[:, wide : 2 * wide] = part[RANK:]
    both_ref[:, 2 * wide :] = (up_ref[...].astype(F32) + near_ref[...].astype(F32)).astype(BF16)


def final_kernel(mine_ref, three_ref, two_ref, one_ref, down_ref, upq_ref, upv_ref):
    wide, size = down_ref.shape[1], upq_ref.shape[1]
    for i in range(2):
        rows, cut = slice(i * RANK, (i + 1) * RANK), slice(i * wide, (i + 1) * wide)
        near = mine_ref[:, cut].astype(F32) + one_ref[rows].astype(F32)
        far = two_ref[:, cut].astype(F32) + three_ref[rows].astype(F32)
        down_ref[rows] = near + far
    up = mine_ref[:, 2 * wide :].astype(F32) + two_ref[:, 2 * wide :].astype(F32)
    upq_ref[...] = up[:, :size]
    upv_ref[...] = up[:, size:]


def body(x, q, k, v, o, segment, a, wq, wv):
    tok, wide = x.shape
    seq_count = lax.axis_size("seq")
    fsdp_count = lax.axis_size("fsdp")
    seq_index = lax.axis_index("seq")
    heads = q.shape[1] // HEAD
    longest = tok * seq_count // 8
    blocks = -(-longest // tok)
    send = longest if blocks == 1 else tok
    halo = blocks * send
    keys = halo + tok
    direct = seq_count == 4 and fsdp_count == 4

    def swap(array, axis, bit):
        size = lax.axis_size(axis)
        return lax.ppermute(array, axis, [(i, i ^ bit) for i in range(size)])

    def shift(array, by):
        moves = [(i, (i + by) % seq_count) for i in range(seq_count)]
        return lax.ppermute(array, "seq", moves)

    def inner(array, even):
        moves = []
        for i in range(seq_count):
            for f in range(fsdp_count):
                if even and f % 2 == 0:
                    to, flip = i ^ 1, 0
                elif i in (1, 2):
                    to, flip = 3 - i, 0
                else:
                    to, flip = i, 2
                moves.append((i * fsdp_count + f, to * fsdp_count + (f ^ flip)))
        return lax.ppermute(array, ("seq", "fsdp"), moves)

    def sum_fsdp(array):
        if fsdp_count != 4:
            return lax.psum(array, "fsdp")
        one, two, three = [swap(array, "fsdp", bit) for bit in (1, 2, 3)]
        return (array + one) + (two + three)

    seg_row = segment.reshape(1, tok)
    part, tails, k, v, wq = call(
        functools.partial(lowrank_kernel, send),
        [
            ((2 * RANK, tok), F32),
            ((2 * send, HEAD), BF16),
            ((tok, HEAD), BF16),
            ((tok, HEAD), BF16),
            (wq.shape, BF16),
        ],
        [
            pltpu.VMEM((tok, wide), BF16),
            pltpu.VMEM((2 * RANK, wide), BF16),
            pltpu.SemaphoreType.DMA((5,)),
        ],
        limit=FULL,
        in_specs=[pl.BlockSpec(memory_space=pltpu.HBM)] * 5,
    )(x, a.T, k, v, wq)
    seg_rows = jnp.broadcast_to(seg_row, (16, tok)).astype(BF16)
    pack = jnp.concatenate([tails, seg_rows], axis=0)
    wv = wv * SCALE
    start = seq_index * tok
    base = start.reshape(1).astype(jnp.int32)
    freqs = ROPE_BASE ** (-(2.0 * jnp.arange(HALF, dtype=F32)) / HEAD)
    positions = (start - halo + jnp.arange(keys, dtype=jnp.int32)).astype(F32)
    angles = positions[:, None] * freqs[None, :]
    cos, sin = jnp.cos(angles), jnp.sin(angles)
    packs = jnp.stack([shift(pack, d) for d in range(blocks, 0, -1)])
    low = sum_fsdp(part)
    low, cos, sin, wv = lax.optimization_barrier((low, cos, sin, wv))
    low_v = low[RANK:].astype(BF16)
    if direct:
        far = inner(low_v, True)
    else:
        lows = jnp.stack([shift(low_v, d) for d in range(blocks, 0, -1)])
    count = heads if blocks == 1 else 1
    qr, kt, s, dp, cos_t, sin_t = call(
        functools.partial(project_kernel, count, heads),
        [
            ((heads * tok, HEAD), BF16),
            ((HEAD, tok), BF16),
            ((tok, heads * tok), F32),
            ((tok, heads * tok), F32),
            ((HALF, tok), F32),
            ((HALF, tok), F32),
        ],
        cost=3 << 20,
    )(low, q, k, v, o, seg_rows, cos[halo:], sin[halo:], wq, wv)
    specs = [pl.BlockSpec(memory_space=pltpu.VMEM)] * 9
    specs[5] = pl.BlockSpec(memory_space=pltpu.SMEM)
    w, kt_far, dv, codes_v = call(
        functools.partial(softmax_kernel, count, send, blocks, heads),
        [
            ((keys, heads * tok), F32),
            ((HEAD, halo), BF16),
            ((keys, HEAD), F32),
            (((blocks + 1) * RANK, tok), F32),
        ],
        in_specs=specs,
        cost=5 << 20,
    )(qr, s, o, seg_rows, packs, base, cos[:halo], sin[:halo], wv)
    if direct:
        w, far = lax.optimization_barrier((w, far))
        mine = (seq_index == 2) == (lax.axis_index("fsdp") % 2 == 1)
        lows = jnp.where(mine, far, swap(far, "fsdp", 1))[None]
    code_v = codes_v[:RANK]
    if direct:
        above, below = swap(codes_v[RANK:], "seq", 1), inner(codes_v[RANK:], False)
        backs = jnp.where(seq_index % 2 == 0, above, jnp.where(seq_index == 1, below, 0.0))
    code_q, up = call(
        functools.partial(grads_kernel, count, send, blocks, heads),
        [((RANK, tok), F32), ((RANK, (heads + 1) * HEAD), BF16 if direct else F32)],
        [pltpu.VMEM((heads * HEAD, tok), BF16)],
        cost=24 << 20,
    )(low, lows, packs, o, w, dp, kt, kt_far, dv, cos_t, sin_t, wq, wv)
    if not direct:
        for b, d in enumerate(range(blocks, 0, -1)):
            code_v = code_v + shift(codes_v[(b + 1) * RANK : (b + 2) * RANK], -d)
        dlow = sum_fsdp(jnp.concatenate([code_q, code_v], axis=0)).astype(BF16)
        (down,) = call(down_kernel, [((2 * RANK, wide), F32)])(dlow, x)
        down, up = lax.psum((down, up), "seq")
        return down.T, up[:, : heads * HEAD], up[:, heads * HEAD :]

    codes = jnp.concatenate([code_q, code_v + backs], axis=0)
    dlow, near_up = lax.optimization_barrier((sum_fsdp(codes), swap(up, "seq", 1)))
    part, both = call(
        partial_kernel,
        [((2 * RANK, wide), BF16), ((RANK, 2 * wide + (heads + 1) * HEAD), BF16)],
    )(dlow.astype(BF16), x, up, near_up)
    three, two, one = swap(part, "seq", 3), swap(both, "seq", 2), swap(part, "seq", 1)
    down, up_q, up_v = call(
        final_kernel,
        [((2 * RANK, wide), F32), ((RANK, heads * HEAD), F32), ((RANK, HEAD), F32)],
    )(both, three, two, one)
    return down.T, up_q, up_v


def solution(mesh):
    rows = ("groups", "seq")
    in_specs = (
        P(rows, "fsdp"),
        P(rows, "fsdp"),
        P(rows, "fsdp"),
        P(rows, "fsdp"),
        P(rows, "fsdp"),
        P(rows),
        P("fsdp", None),
        P(None, "fsdp"),
        P(None, "fsdp"),
    )
    out_specs = (P(("groups", "fsdp"), None), P("groups", "fsdp"), P("groups", "fsdp"))
    return jax.shard_map(body, mesh=mesh, in_specs=in_specs, out_specs=out_specs, check_vma=False)
```

```python
import functools
import math

import jax
import jax.numpy as jnp
from jax import lax
from jax.experimental import pallas as pl
from jax.experimental.pallas import tpu as pltpu
from jax.sharding import PartitionSpec as P

HEAD = 128
HALF = HEAD // 2
RANK = 16
SCALE = 2.0
ROPE_BASE = 500000.0
NEG_FILL = -1e30
INV_ROOT = 1.0 / math.sqrt(HEAD)
F32 = jnp.float32
BF16 = jnp.bfloat16
LIMIT = 40 * 1024 * 1024
FULL = 55080 * 1024


def dot(left, right, left_dim, right_dim):
    return lax.dot_general(
        left,
        right,
        (((left_dim,), (right_dim,)), ((), ())),
        preferred_element_type=F32,
    )


def call(kernel, out_shapes, scratch=(), limit=LIMIT, cost=1, **specs):
    return pl.pallas_call(
        kernel,
        out_shape=[jax.ShapeDtypeStruct(s, d) for s, d in out_shapes],
        **specs,
        scratch_shapes=list(scratch),
        compiler_params=pltpu.CompilerParams(vmem_limit_bytes=limit),
        cost_estimate=pl.CostEstimate(flops=cost, bytes_accessed=cost, transcendentals=0),
    )


def lowrank_kernel(send, *refs):
    sources, (part_ref, tails_ref, k_ref, v_ref, wq_ref) = refs[:5], refs[5:10]
    x_ref, a_ref, sems = refs[10:]
    targets = (x_ref, a_ref, k_ref, v_ref, wq_ref)
    copies = []
    for i, (source, target) in enumerate(zip(sources, targets)):
        copies.append(pltpu.make_async_copy(source, target, sems.at[i]))
        copies[-1].start()
    for copy in copies:
        copy.wait()
    part_ref[...] = dot(a_ref[...], x_ref[...], 1, 1)
    tok = k_ref.shape[0]
    tails_ref[0:send] = k_ref[tok - send :]
    tails_ref[send:] = v_ref[tok - send :]


def rotate_rows(u, cos, sin):
    return u * cos + pltpu.roll(u, HALF, 1) * sin


def wide_tables(cos, sin):
    return jnp.concatenate([cos, cos], axis=1), jnp.concatenate([-sin, sin], axis=1)


def column(row, tok):
    return jnp.broadcast_to(row, (tok, tok)).T


def lanes(array, count):
    return jnp.concatenate([array] * count, axis=1)


def head_rows(ref, first, count):
    parts = [ref[:, h * HEAD : (h + 1) * HEAD] for h in range(first, first + count)]
    return jnp.concatenate(parts, axis=0)


def split_dot(left, right, left_dim, right_dim):
    high = right.astype(BF16)
    rest = (right - high.astype(F32)).astype(BF16)
    return dot(left, high, left_dim, right_dim) + dot(left, rest, left_dim, right_dim)


def by_token(array, send, tok):
    if send == tok:
        return array
    gap = jnp.zeros((tok - send, array.shape[1]), array.dtype)
    return jnp.concatenate([array[:tok], gap, array[tok:]], axis=0)


def project_kernel(
    count, heads,
    low_ref, q_ref, k_ref, v_ref, o_ref, seg_ref, cos_ref, sin_ref, wq_ref, wv_ref,
    qr_ref, kt_ref, s_ref, dp_ref, cost_ref, sint_ref,
):
    tok = q_ref.shape[0]
    low = low_ref[...].astype(BF16)
    cost_ref[...] = cos_ref[...].T
    sint_ref[...] = sin_ref[...].T
    cos, sin = wide_tables(cos_ref[...], sin_ref[...])
    keys = rotate_rows(k_ref[...].astype(F32), cos, sin)
    kt_ref[...] = keys.T.astype(BF16)
    keys = keys.astype(BF16)
    vals = (v_ref[...].astype(F32) + dot(low[RANK:], wv_ref[...], 0, 0)).astype(BF16)
    seg_here = seg_ref[...].astype(F32)[0:1]
    key = lax.broadcasted_iota(jnp.int32, (tok, tok), 0)
    query = lax.broadcasted_iota(jnp.int32, (tok, tok), 1)
    allowed = (key <= query) & (column(seg_here, tok) == seg_here)
    bias = lanes(jnp.where(allowed, 0.0, NEG_FILL), count)
    q0 = q_ref[...].astype(F32) + SCALE * dot(low[:RANK], wq_ref[...], 0, 0)
    for g in range(0, heads, count):
        cut = slice(g * tok, (g + count) * tok)
        parts = [q0[:, h * HEAD : (h + 1) * HEAD] for h in range(g, g + count)]
        qr = jnp.concatenate([rotate_rows(u, cos, sin).astype(BF16) for u in parts], axis=0)
        qr_ref[cut] = qr
        s_ref[:, cut] = dot(keys, qr, 1, 1) * INV_ROOT + bias
        dp_ref[:, cut] = dot(vals, head_rows(o_ref, g, count), 1, 1)


def softmax_kernel(
    count, send, blocks, heads,
    qr_ref, s_ref, o_ref, seg_ref, pack_ref, base_ref, cos_ref, sin_ref, wv_ref,
    w_ref, kt_ref, dv_ref, code_ref,
):
    tok = o_ref.shape[0]
    halo = send * blocks
    cos, sin = wide_tables(cos_ref[...], sin_ref[...])
    keys = jnp.concatenate([pack_ref[b, 0:send] for b in range(blocks)], axis=0)
    keys = rotate_rows(keys.astype(F32), cos, sin)
    kt_ref[...] = keys.T.astype(BF16)
    keys = keys.astype(BF16)
    seg_here = seg_ref[...].astype(F32)[0:1]
    cols = []
    for b in range(blocks):
        row = pack_ref[b, 2 * send :].astype(F32)[0:1]
        cols.append(column(row, tok)[tok - send :])
    seg_col = jnp.concatenate(cols, axis=0)
    offset = lax.broadcasted_iota(jnp.int32, (halo, tok), 0)
    allowed = (offset + base_ref[0] >= halo) & (seg_col == seg_here)
    bias = lanes(jnp.where(allowed, 0.0, NEG_FILL), count)
    dv = jnp.zeros((tok + halo, HEAD), F32)
    for g in range(0, heads, count):
        cut = slice(g * tok, (g + count) * tok)
        far = dot(keys, qr_ref[cut], 1, 1) * INV_ROOT + bias
        s = jnp.concatenate([s_ref[:, cut], far], axis=0)
        e = jnp.exp(s - jnp.max(s, axis=0, keepdims=True))
        w = e * (1.0 / jnp.sum(e, axis=0, keepdims=True))
        w_ref[:, cut] = w
        dv = dv + dot(w.astype(BF16), head_rows(o_ref, g, count), 1, 0)
    dv_ref[...] = dv
    codes = split_dot(wv_ref[...], by_token(dv, send, tok), 1, 1)
    for b in range(blocks + 1):
        code_ref[b * RANK : (b + 1) * RANK] = codes[:, b * tok : (b + 1) * tok]


def grads_kernel(
    count, send, blocks, heads,
    low_ref, far_ref, pack_ref, o_ref, w_ref, dp_ref, kt_ref, kth_ref, dv_ref, cost_ref, sint_ref, wq_ref, wv_ref,
    code_ref, up_ref, qg_ref,
):
    tok = o_ref.shape[0]
    low = low_ref[...].astype(BF16)
    wv = wv_ref[...]
    vals = []
    for b in range(blocks):
        rows = pack_ref[b, send : 2 * send].astype(F32)
        add = dot(far_ref[b], wv, 0, 0)[tok - send :]
        vals.append((rows + add).astype(BF16))
    vals = jnp.concatenate(vals, axis=0)
    kt = jnp.concatenate([kt_ref[...], kth_ref[...]], axis=1)
    cos, sin = lanes(cost_ref[...], count), lanes(sint_ref[...], count)
    for g in range(0, heads, count):
        cut = slice(g * tok, (g + count) * tok)
        far = dot(vals, head_rows(o_ref, g, count), 1, 1)
        dp = jnp.concatenate([dp_ref[:, cut], far], axis=0)
        w = w_ref[:, cut]
        delta = jnp.sum(w * dp, axis=0, keepdims=True)
        ds = (w * (dp - delta) * INV_ROOT).astype(BF16)
        dq = dot(kt, ds, 1, 0)
        first, second = dq[:HALF], dq[HALF:]
        first, second = first * cos + second * sin, second * cos - first * sin
        turned = jnp.concatenate([first.astype(BF16), second.astype(BF16)], axis=0)
        for h in range(count):
            qg_ref[(g + h) * HEAD : (g + h + 1) * HEAD] = turned[:, h * tok : (h + 1) * tok]
    qg = qg_ref[...]
    code_ref[...] = SCALE * dot(wq_ref[...], qg, 1, 0)
    up_ref[:, : heads * HEAD] = (SCALE * dot(low[:RANK], qg, 1, 1)).astype(up_ref.dtype)
    codes = jnp.concatenate([low[RANK:]] + [far_ref[b] for b in range(blocks)], axis=1)
    up_v = SCALE * split_dot(codes, by_token(dv_ref[...], send, tok), 1, 0)
    up_ref[:, heads * HEAD :] = up_v.astype(up_ref.dtype)


def down_kernel(dl_ref, x_ref, part_ref):
    part_ref[...] = dot(dl_ref[...], x_ref[...], 1, 0)


def partial_kernel(own_ref, x_ref, both_ref, query_ref, value_ref):
    part = dot(own_ref[...], x_ref[...], 1, 0).astype(BF16)
    both_ref[...] = part
    query_ref[...] = part[:RANK]
    value_ref[...] = part[RANK:]


def combine_kernel(query_ref, up_ref, near_ref, send_ref):
    wide = query_ref.shape[1]
    send_ref[:, :wide] = query_ref[...]
    send_ref[:, wide:] = (up_ref[...].astype(F32) + near_ref[...].astype(F32)).astype(BF16)


def final_kernel(
    mine_ref, one_ref, query_ref, query_two_ref, query_three_ref, value_two_ref, value_three_ref,
    down_ref, upq_ref, upv_ref,
):
    wide, size = down_ref.shape[1], upq_ref.shape[1]
    near = mine_ref[...].astype(F32) + one_ref[...].astype(F32)
    far = query_two_ref[:, :wide].astype(F32) + query_three_ref[...].astype(F32)
    down_ref[:RANK] = near[:RANK] + far
    far = value_two_ref[...].astype(F32) + value_three_ref[...].astype(F32)
    down_ref[RANK:] = near[RANK:] + far
    up = query_ref[:, wide:].astype(F32) + query_two_ref[:, wide:].astype(F32)
    upq_ref[...] = up[:, :size]
    upv_ref[...] = up[:, size:]


def body(x, q, k, v, o, segment, a, wq, wv):
    tok, wide = x.shape
    seq_count = lax.axis_size("seq")
    fsdp_count = lax.axis_size("fsdp")
    seq_index = lax.axis_index("seq")
    heads = q.shape[1] // HEAD
    longest = tok * seq_count // 8
    blocks = -(-longest // tok)
    send = longest if blocks == 1 else tok
    halo = blocks * send
    keys = halo + tok
    direct = seq_count == 4 and fsdp_count == 4

    def swap(array, axis, bit):
        size = lax.axis_size(axis)
        return lax.ppermute(array, axis, [(i, i ^ bit) for i in range(size)])

    def shift(array, by):
        moves = [(i, (i + by) % seq_count) for i in range(seq_count)]
        return lax.ppermute(array, "seq", moves)

    def inner(array, even):
        moves = []
        for i in range(seq_count):
            for f in range(fsdp_count):
                if even and f % 2 == 0:
                    to, flip = i ^ 1, 0
                elif i in (1, 2):
                    to, flip = 3 - i, 0
                else:
                    to, flip = i, 2
                moves.append((i * fsdp_count + f, to * fsdp_count + (f ^ flip)))
        return lax.ppermute(array, ("seq", "fsdp"), moves)

    def sum_fsdp(array):
        if fsdp_count != 4:
            return lax.psum(array, "fsdp")
        one, two, three = [swap(array, "fsdp", bit) for bit in (1, 2, 3)]
        return (array + one) + (two + three)

    seg_row = segment.reshape(1, tok)
    part, tails, k, v, wq = call(
        functools.partial(lowrank_kernel, send),
        [
            ((2 * RANK, tok), F32),
            ((2 * send, HEAD), BF16),
            ((tok, HEAD), BF16),
            ((tok, HEAD), BF16),
            (wq.shape, BF16),
        ],
        [
            pltpu.VMEM((tok, wide), BF16),
            pltpu.VMEM((2 * RANK, wide), BF16),
            pltpu.SemaphoreType.DMA((5,)),
        ],
        limit=FULL,
        in_specs=[pl.BlockSpec(memory_space=pltpu.HBM)] * 5,
    )(x, a.T, k, v, wq)
    seg_rows = jnp.broadcast_to(seg_row, (16, tok)).astype(BF16)
    pack = jnp.concatenate([tails, seg_rows], axis=0)
    wv = wv * SCALE
    start = seq_index * tok
    base = start.reshape(1).astype(jnp.int32)
    freqs = ROPE_BASE ** (-(2.0 * jnp.arange(HALF, dtype=F32)) / HEAD)
    positions = (start - halo + jnp.arange(keys, dtype=jnp.int32)).astype(F32)
    angles = positions[:, None] * freqs[None, :]
    cos, sin = jnp.cos(angles), jnp.sin(angles)
    packs = jnp.stack([shift(pack, d) for d in range(blocks, 0, -1)])
    low = sum_fsdp(part)
    low, cos, sin, wv = lax.optimization_barrier((low, cos, sin, wv))
    low_v = low[RANK:].astype(BF16)
    if direct:
        far = inner(low_v, True)
    else:
        lows = jnp.stack([shift(low_v, d) for d in range(blocks, 0, -1)])
    count = heads if blocks == 1 else 1
    qr, kt, s, dp, cos_t, sin_t = call(
        functools.partial(project_kernel, count, heads),
        [
            ((heads * tok, HEAD), BF16),
            ((HEAD, tok), BF16),
            ((tok, heads * tok), F32),
            ((tok, heads * tok), F32),
            ((HALF, tok), F32),
            ((HALF, tok), F32),
        ],
        cost=3 << 20,
    )(low, q, k, v, o, seg_rows, cos[halo:], sin[halo:], wq, wv)
    specs = [pl.BlockSpec(memory_space=pltpu.VMEM)] * 9
    specs[5] = pl.BlockSpec(memory_space=pltpu.SMEM)
    w, kt_far, dv, codes_v = call(
        functools.partial(softmax_kernel, count, send, blocks, heads),
        [
            ((keys, heads * tok), F32),
            ((HEAD, halo), BF16),
            ((keys, HEAD), F32),
            (((blocks + 1) * RANK, tok), F32),
        ],
        in_specs=specs,
        cost=5 << 20,
    )(qr, s, o, seg_rows, packs, base, cos[:halo], sin[:halo], wv)
    if direct:
        w, far = lax.optimization_barrier((w, far))
        mine = (seq_index == 2) == (lax.axis_index("fsdp") % 2 == 1)
        lows = jnp.where(mine, far, swap(far, "fsdp", 1))[None]
    code_v = codes_v[:RANK]
    if direct:
        above, below = swap(codes_v[RANK:], "seq", 1), inner(codes_v[RANK:], False)
        backs = jnp.where(seq_index % 2 == 0, above, jnp.where(seq_index == 1, below, 0.0))
    code_q, up = call(
        functools.partial(grads_kernel, count, send, blocks, heads),
        [((RANK, tok), F32), ((RANK, (heads + 1) * HEAD), BF16 if direct else F32)],
        [pltpu.VMEM((heads * HEAD, tok), BF16)],
        cost=24 << 20,
    )(low, lows, packs, o, w, dp, kt, kt_far, dv, cos_t, sin_t, wq, wv)
    if not direct:
        for b, d in enumerate(range(blocks, 0, -1)):
            code_v = code_v + shift(codes_v[(b + 1) * RANK : (b + 2) * RANK], -d)
        dlow = sum_fsdp(jnp.concatenate([code_q, code_v], axis=0)).astype(BF16)
        (down,) = call(down_kernel, [((2 * RANK, wide), F32)])(dlow, x)
        down, up = lax.psum((down, up), "seq")
        return down.T, up[:, : heads * HEAD], up[:, heads * HEAD :]

    codes = jnp.concatenate([code_q, code_v + backs], axis=0)
    near_up = swap(up, "seq", 1)
    both, part_q, part_v = call(
        partial_kernel, [((2 * RANK, wide), BF16), ((RANK, wide), BF16), ((RANK, wide), BF16)]
    )(sum_fsdp(codes).astype(BF16), x)
    (send_q,) = call(combine_kernel, [((RANK, wide + up.shape[1]), BF16)])(part_q, up, near_up)
    value_two = swap(part_v, "seq", 2)
    value_three = swap(value_two, "seq", 1)
    query_two, query_three = swap(send_q, "seq", 2), swap(part_q, "seq", 3)
    one = swap(both, "seq", 1)
    down, up_q, up_v = call(
        final_kernel,
        [((2 * RANK, wide), F32), ((RANK, heads * HEAD), F32), ((RANK, HEAD), F32)],
    )(both, one, send_q, query_two, query_three, value_two, value_three)
    return down.T, up_q, up_v


def solution(mesh):
    rows = ("groups", "seq")
    in_specs = (
        P(rows, "fsdp"),
        P(rows, "fsdp"),
        P(rows, "fsdp"),
        P(rows, "fsdp"),
        P(rows, "fsdp"),
        P(rows),
        P("fsdp", None),
        P(None, "fsdp"),
        P(None, "fsdp"),
    )
    out_specs = (P(("groups", "fsdp"), None), P("groups", "fsdp"), P("groups", "fsdp"))
    return jax.shard_map(body, mesh=mesh, in_specs=in_specs, out_specs=out_specs, check_vma=False)
```

```python
import functools
import math

import jax
import jax.numpy as jnp
from jax import lax
from jax.experimental import pallas as pl
from jax.experimental.pallas import tpu as pltpu
from jax.sharding import PartitionSpec as P

HEAD = 128
HALF = HEAD // 2
RANK = 16
SCALE = 2.0
ROPE_BASE = 500000.0
NEG_FILL = -1e30
INV_ROOT = 1.0 / math.sqrt(HEAD)
F32 = jnp.float32
BF16 = jnp.bfloat16
LIMIT = 40 * 1024 * 1024
FULL = 55080 * 1024


def dot(left, right, left_dim, right_dim):
    return lax.dot_general(
        left,
        right,
        (((left_dim,), (right_dim,)), ((), ())),
        preferred_element_type=F32,
    )


def call(kernel, out_shapes, scratch=(), limit=LIMIT, cost=1, **specs):
    return pl.pallas_call(
        kernel,
        out_shape=[jax.ShapeDtypeStruct(s, d) for s, d in out_shapes],
        **specs,
        scratch_shapes=list(scratch),
        compiler_params=pltpu.CompilerParams(vmem_limit_bytes=limit),
        cost_estimate=pl.CostEstimate(flops=cost, bytes_accessed=cost, transcendentals=0),
    )


def lowrank_kernel(send, *refs):
    sources, (part_ref, tails_ref, k_ref, v_ref, wq_ref) = refs[:5], refs[5:10]
    x_ref, a_ref, sems = refs[10:]
    targets = (x_ref, a_ref, k_ref, v_ref, wq_ref)
    copies = []
    for i, (source, target) in enumerate(zip(sources, targets)):
        copies.append(pltpu.make_async_copy(source, target, sems.at[i]))
        copies[-1].start()
    for copy in copies:
        copy.wait()
    part_ref[...] = dot(a_ref[...], x_ref[...], 1, 1)
    tok = k_ref.shape[0]
    tails_ref[0:send] = k_ref[tok - send :]
    tails_ref[send:] = v_ref[tok - send :]


def rotate_rows(u, cos, sin):
    return u * cos + pltpu.roll(u, HALF, 1) * sin


def wide_tables(cos, sin):
    return jnp.concatenate([cos, cos], axis=1), jnp.concatenate([-sin, sin], axis=1)


def column(row, tok):
    return jnp.broadcast_to(row, (tok, tok)).T


def lanes(array, count):
    return jnp.concatenate([array] * count, axis=1)


def head_rows(ref, first, count):
    parts = [ref[:, h * HEAD : (h + 1) * HEAD] for h in range(first, first + count)]
    return jnp.concatenate(parts, axis=0)


def split_dot(left, right, left_dim, right_dim):
    high = right.astype(BF16)
    rest = (right - high.astype(F32)).astype(BF16)
    return dot(left, high, left_dim, right_dim) + dot(left, rest, left_dim, right_dim)


def by_token(array, send, tok):
    if send == tok:
        return array
    gap = jnp.zeros((tok - send, array.shape[1]), array.dtype)
    return jnp.concatenate([array[:tok], gap, array[tok:]], axis=0)


def project_kernel(
    count, heads,
    low_ref, q_ref, k_ref, v_ref, o_ref, seg_ref, cos_ref, sin_ref, wq_ref, wv_ref,
    qr_ref, kt_ref, s_ref, dp_ref, cost_ref, sint_ref,
):
    tok = q_ref.shape[0]
    low = low_ref[...].astype(BF16)
    cost_ref[...] = cos_ref[...].T
    sint_ref[...] = sin_ref[...].T
    cos, sin = wide_tables(cos_ref[...], sin_ref[...])
    keys = rotate_rows(k_ref[...].astype(F32), cos, sin)
    kt_ref[...] = keys.T.astype(BF16)
    keys = keys.astype(BF16)
    vals = (v_ref[...].astype(F32) + dot(low[RANK:], wv_ref[...], 0, 0)).astype(BF16)
    seg_here = seg_ref[...].astype(F32)[0:1]
    key = lax.broadcasted_iota(jnp.int32, (tok, tok), 0)
    query = lax.broadcasted_iota(jnp.int32, (tok, tok), 1)
    allowed = (key <= query) & (column(seg_here, tok) == seg_here)
    bias = lanes(jnp.where(allowed, 0.0, NEG_FILL), count)
    q0 = q_ref[...].astype(F32) + SCALE * dot(low[:RANK], wq_ref[...], 0, 0)
    for g in range(0, heads, count):
        cut = slice(g * tok, (g + count) * tok)
        parts = [q0[:, h * HEAD : (h + 1) * HEAD] for h in range(g, g + count)]
        qr = jnp.concatenate([rotate_rows(u, cos, sin).astype(BF16) for u in parts], axis=0)
        qr_ref[cut] = qr
        s_ref[:, cut] = dot(keys, qr, 1, 1) * INV_ROOT + bias
        dp_ref[:, cut] = dot(vals, head_rows(o_ref, g, count), 1, 1)


def softmax_kernel(
    count, send, blocks, heads,
    qr_ref, s_ref, o_ref, seg_ref, pack_ref, base_ref, cos_ref, sin_ref, wv_ref,
    w_ref, kt_ref, dv_ref, code_ref,
):
    tok = o_ref.shape[0]
    halo = send * blocks
    cos, sin = wide_tables(cos_ref[...], sin_ref[...])
    keys = jnp.concatenate([pack_ref[b, 0:send] for b in range(blocks)], axis=0)
    keys = rotate_rows(keys.astype(F32), cos, sin)
    kt_ref[...] = keys.T.astype(BF16)
    keys = keys.astype(BF16)
    seg_here = seg_ref[...].astype(F32)[0:1]
    cols = []
    for b in range(blocks):
        row = pack_ref[b, 2 * send :].astype(F32)[0:1]
        cols.append(column(row, tok)[tok - send :])
    seg_col = jnp.concatenate(cols, axis=0)
    offset = lax.broadcasted_iota(jnp.int32, (halo, tok), 0)
    allowed = (offset + base_ref[0] >= halo) & (seg_col == seg_here)
    bias = lanes(jnp.where(allowed, 0.0, NEG_FILL), count)
    dv = jnp.zeros((tok + halo, HEAD), F32)
    for g in range(0, heads, count):
        cut = slice(g * tok, (g + count) * tok)
        far = dot(keys, qr_ref[cut], 1, 1) * INV_ROOT + bias
        s = jnp.concatenate([s_ref[:, cut], far], axis=0)
        e = jnp.exp(s - jnp.max(s, axis=0, keepdims=True))
        w = e * (1.0 / jnp.sum(e, axis=0, keepdims=True))
        w_ref[:, cut] = w
        dv = dv + dot(w.astype(BF16), head_rows(o_ref, g, count), 1, 0)
    dv_ref[...] = dv
    codes = split_dot(wv_ref[...], by_token(dv, send, tok), 1, 1)
    for b in range(blocks + 1):
        code_ref[b * RANK : (b + 1) * RANK] = codes[:, b * tok : (b + 1) * tok]


def grads_kernel(
    count, send, blocks, heads,
    low_ref, far_ref, pack_ref, o_ref, w_ref, dp_ref, kt_ref, kth_ref, dv_ref, cost_ref, sint_ref, wq_ref, wv_ref,
    code_ref, up_ref, qg_ref,
):
    tok = o_ref.shape[0]
    low = low_ref[...].astype(BF16)
    wv = wv_ref[...]
    vals = []
    for b in range(blocks):
        rows = pack_ref[b, send : 2 * send].astype(F32)
        add = dot(far_ref[b], wv, 0, 0)[tok - send :]
        vals.append((rows + add).astype(BF16))
    vals = jnp.concatenate(vals, axis=0)
    kt = jnp.concatenate([kt_ref[...], kth_ref[...]], axis=1)
    cos, sin = lanes(cost_ref[...], count), lanes(sint_ref[...], count)
    for g in range(0, heads, count):
        cut = slice(g * tok, (g + count) * tok)
        far = dot(vals, head_rows(o_ref, g, count), 1, 1)
        dp = jnp.concatenate([dp_ref[:, cut], far], axis=0)
        w = w_ref[:, cut]
        delta = jnp.sum(w * dp, axis=0, keepdims=True)
        ds = (w * (dp - delta) * INV_ROOT).astype(BF16)
        dq = dot(kt, ds, 1, 0)
        first, second = dq[:HALF], dq[HALF:]
        first, second = first * cos + second * sin, second * cos - first * sin
        turned = jnp.concatenate([first.astype(BF16), second.astype(BF16)], axis=0)
        for h in range(count):
            qg_ref[(g + h) * HEAD : (g + h + 1) * HEAD] = turned[:, h * tok : (h + 1) * tok]
    qg = qg_ref[...]
    code_ref[...] = SCALE * dot(wq_ref[...], qg, 1, 0)
    up_ref[:, : heads * HEAD] = (SCALE * dot(low[:RANK], qg, 1, 1)).astype(up_ref.dtype)
    codes = jnp.concatenate([low[RANK:]] + [far_ref[b] for b in range(blocks)], axis=1)
    up_v = SCALE * split_dot(codes, by_token(dv_ref[...], send, tok), 1, 0)
    up_ref[:, heads * HEAD :] = up_v.astype(up_ref.dtype)


def down_kernel(dl_ref, x_ref, part_ref):
    part_ref[...] = dot(dl_ref[...], x_ref[...], 1, 0)


def partial_kernel(own_ref, x_ref, up_ref, both_ref, relay_ref, rest_ref):
    part = dot(own_ref[...], x_ref[...], 1, 0).astype(BF16)
    wide, up = part.shape[1], up_ref[...]
    cut = wide - rest_ref.shape[1]
    both_ref[:, :wide] = part[:RANK]
    both_ref[:, wide : 2 * wide] = part[RANK:]
    both_ref[:, 2 * wide :] = up
    relay_ref[:, :cut] = part[:RANK, :cut]
    relay_ref[:, cut : cut + wide] = part[RANK:]
    relay_ref[:, cut + wide :] = up
    rest_ref[...] = part[:RANK, cut:]


def final_kernel(
    mine_ref, one_ref, rest_two_ref, rest_three_ref, relay_two_ref, first_three_ref, second_three_ref,
    down_ref, upq_ref, upv_ref,
):
    wide, size = down_ref.shape[1], upq_ref.shape[1]
    cut = wide - rest_three_ref.shape[1]
    near = mine_ref[...].astype(F32) + one_ref[...].astype(F32)
    relay = jnp.concatenate([first_three_ref[...], second_three_ref[...]], axis=1)
    relay = relay_two_ref[...].astype(F32) + relay.astype(F32)
    down_ref[:RANK, :cut] = near[:, :cut] + relay[:, :cut]
    rest = rest_two_ref[...].astype(F32) + rest_three_ref[...].astype(F32)
    down_ref[:RANK, cut:] = near[:, cut:wide] + rest
    others = near[:, wide:] + relay[:, cut:]
    down_ref[RANK:] = others[:, :wide]
    upq_ref[...] = others[:, wide : wide + size]
    upv_ref[...] = others[:, wide + size :]


def body(x, q, k, v, o, segment, a, wq, wv):
    tok, wide = x.shape
    seq_count = lax.axis_size("seq")
    fsdp_count = lax.axis_size("fsdp")
    seq_index = lax.axis_index("seq")
    heads = q.shape[1] // HEAD
    longest = tok * seq_count // 8
    blocks = -(-longest // tok)
    send = longest if blocks == 1 else tok
    halo = blocks * send
    keys = halo + tok
    direct = seq_count == 4 and fsdp_count == 4

    def swap(array, axis, bit):
        size = lax.axis_size(axis)
        return lax.ppermute(array, axis, [(i, i ^ bit) for i in range(size)])

    def shift(array, by):
        moves = [(i, (i + by) % seq_count) for i in range(seq_count)]
        return lax.ppermute(array, "seq", moves)

    def inner(array, even):
        moves = []
        for i in range(seq_count):
            for f in range(fsdp_count):
                if even and f % 2 == 0:
                    to, flip = i ^ 1, 0
                elif i in (1, 2):
                    to, flip = 3 - i, 0
                else:
                    to, flip = i, 2
                moves.append((i * fsdp_count + f, to * fsdp_count + (f ^ flip)))
        return lax.ppermute(array, ("seq", "fsdp"), moves)

    def sum_fsdp(array):
        if fsdp_count != 4:
            return lax.psum(array, "fsdp")
        one, two, three = [swap(array, "fsdp", bit) for bit in (1, 2, 3)]
        return (array + one) + (two + three)

    seg_row = segment.reshape(1, tok)
    part, tails, k, v, wq = call(
        functools.partial(lowrank_kernel, send),
        [
            ((2 * RANK, tok), F32),
            ((2 * send, HEAD), BF16),
            ((tok, HEAD), BF16),
            ((tok, HEAD), BF16),
            (wq.shape, BF16),
        ],
        [
            pltpu.VMEM((tok, wide), BF16),
            pltpu.VMEM((2 * RANK, wide), BF16),
            pltpu.SemaphoreType.DMA((5,)),
        ],
        limit=FULL,
        in_specs=[pl.BlockSpec(memory_space=pltpu.HBM)] * 5,
    )(x, a.T, k, v, wq)
    seg_rows = jnp.broadcast_to(seg_row, (16, tok)).astype(BF16)
    pack = jnp.concatenate([tails, seg_rows], axis=0)
    wv = wv * SCALE
    start = seq_index * tok
    base = start.reshape(1).astype(jnp.int32)
    freqs = ROPE_BASE ** (-(2.0 * jnp.arange(HALF, dtype=F32)) / HEAD)
    positions = (start - halo + jnp.arange(keys, dtype=jnp.int32)).astype(F32)
    angles = positions[:, None] * freqs[None, :]
    cos, sin = jnp.cos(angles), jnp.sin(angles)
    packs = jnp.stack([shift(pack, d) for d in range(blocks, 0, -1)])
    low = sum_fsdp(part)
    low, cos, sin, wv = lax.optimization_barrier((low, cos, sin, wv))
    low_v = low[RANK:].astype(BF16)
    if direct:
        far = inner(low_v, True)
    else:
        lows = jnp.stack([shift(low_v, d) for d in range(blocks, 0, -1)])
    count = heads if blocks == 1 else 1
    qr, kt, s, dp, cos_t, sin_t = call(
        functools.partial(project_kernel, count, heads),
        [
            ((heads * tok, HEAD), BF16),
            ((HEAD, tok), BF16),
            ((tok, heads * tok), F32),
            ((tok, heads * tok), F32),
            ((HALF, tok), F32),
            ((HALF, tok), F32),
        ],
        cost=3 << 20,
    )(low, q, k, v, o, seg_rows, cos[halo:], sin[halo:], wq, wv)
    specs = [pl.BlockSpec(memory_space=pltpu.VMEM)] * 9
    specs[5] = pl.BlockSpec(memory_space=pltpu.SMEM)
    w, kt_far, dv, codes_v = call(
        functools.partial(softmax_kernel, count, send, blocks, heads),
        [
            ((keys, heads * tok), F32),
            ((HEAD, halo), BF16),
            ((keys, HEAD), F32),
            (((blocks + 1) * RANK, tok), F32),
        ],
        in_specs=specs,
        cost=5 << 20,
    )(qr, s, o, seg_rows, packs, base, cos[:halo], sin[:halo], wv)
    if direct:
        w, far = lax.optimization_barrier((w, far))
        mine = (seq_index == 2) == (lax.axis_index("fsdp") % 2 == 1)
        lows = jnp.where(mine, far, swap(far, "fsdp", 1))[None]
    code_v = codes_v[:RANK]
    if direct:
        above, below = swap(codes_v[RANK:], "seq", 1), inner(codes_v[RANK:], False)
        backs = jnp.where(seq_index % 2 == 0, above, jnp.where(seq_index == 1, below, 0.0))
    code_q, up = call(
        functools.partial(grads_kernel, count, send, blocks, heads),
        [((RANK, tok), F32), ((RANK, (heads + 1) * HEAD), BF16 if direct else F32)],
        [pltpu.VMEM((heads * HEAD, tok), BF16)],
        cost=24 << 20,
    )(low, lows, packs, o, w, dp, kt, kt_far, dv, cos_t, sin_t, wq, wv)
    if not direct:
        for b, d in enumerate(range(blocks, 0, -1)):
            code_v = code_v + shift(codes_v[(b + 1) * RANK : (b + 2) * RANK], -d)
        dlow = sum_fsdp(jnp.concatenate([code_q, code_v], axis=0)).astype(BF16)
        (down,) = call(down_kernel, [((2 * RANK, wide), F32)])(dlow, x)
        down, up = lax.psum((down, up), "seq")
        return down.T, up[:, : heads * HEAD], up[:, heads * HEAD :]

    codes = jnp.concatenate([code_q, code_v + backs], axis=0)
    cut, size = HEAD, (heads + 1) * HEAD
    half = (cut + wide + size) // 2 // HEAD * HEAD
    both, relay, rest = call(
        partial_kernel,
        [((RANK, 2 * wide + size), BF16), ((RANK, cut + wide + size), BF16), ((RANK, wide - cut), BF16)],
    )(sum_fsdp(codes).astype(BF16), x, up)
    relay_two = swap(relay, "seq", 2)
    relay_three = [swap(part, "seq", 1) for part in (relay_two[:, :half], relay_two[:, half:])]
    rest_two, rest_three = swap(rest, "seq", 2), swap(rest, "seq", 3)
    one = swap(both, "seq", 1)
    down, up_q, up_v = call(
        final_kernel,
        [((2 * RANK, wide), F32), ((RANK, heads * HEAD), F32), ((RANK, HEAD), F32)],
    )(both, one, rest_two, rest_three, relay_two, *relay_three)
    return down.T, up_q, up_v


def solution(mesh):
    rows = ("groups", "seq")
    in_specs = (
        P(rows, "fsdp"),
        P(rows, "fsdp"),
        P(rows, "fsdp"),
        P(rows, "fsdp"),
        P(rows, "fsdp"),
        P(rows),
        P("fsdp", None),
        P(None, "fsdp"),
        P(None, "fsdp"),
    )
    out_specs = (P(("groups", "fsdp"), None), P("groups", "fsdp"), P("groups", "fsdp"))
    return jax.shard_map(body, mesh=mesh, in_specs=in_specs, out_specs=out_specs, check_vma=False)
```

```python
import functools
import math

import jax
import jax.numpy as jnp
from jax import lax
from jax.experimental import pallas as pl
from jax.experimental.pallas import tpu as pltpu
from jax.sharding import PartitionSpec as P

HEAD = 128
HALF = HEAD // 2
RANK = 16
SCALE = 2.0
ROPE_BASE = 500000.0
NEG_FILL = -1e30
INV_ROOT = 1.0 / math.sqrt(HEAD)
F32 = jnp.float32
BF16 = jnp.bfloat16
LIMIT = 40 * 1024 * 1024
FULL = 55080 * 1024


def dot(left, right, left_dim, right_dim):
    return lax.dot_general(
        left,
        right,
        (((left_dim,), (right_dim,)), ((), ())),
        preferred_element_type=F32,
    )


def call(kernel, out_shapes, scratch=(), limit=LIMIT, cost=1, **specs):
    return pl.pallas_call(
        kernel,
        out_shape=[jax.ShapeDtypeStruct(s, d) for s, d in out_shapes],
        **specs,
        scratch_shapes=list(scratch),
        compiler_params=pltpu.CompilerParams(vmem_limit_bytes=limit),
        cost_estimate=pl.CostEstimate(flops=cost, bytes_accessed=cost, transcendentals=0),
    )


def lowrank_kernel(send, *refs):
    sources, (part_ref, tails_ref, k_ref, v_ref, wq_ref) = refs[:5], refs[5:10]
    x_ref, a_ref, sems = refs[10:]
    targets = (x_ref, a_ref, k_ref, v_ref, wq_ref)
    copies = []
    for i, (source, target) in enumerate(zip(sources, targets)):
        copies.append(pltpu.make_async_copy(source, target, sems.at[i]))
        copies[-1].start()
    for copy in copies:
        copy.wait()
    part_ref[...] = dot(a_ref[...], x_ref[...], 1, 1)
    tok = k_ref.shape[0]
    tails_ref[0:send] = k_ref[tok - send :]
    tails_ref[send:] = v_ref[tok - send :]


def rotate_rows(u, cos, sin):
    return u * cos + pltpu.roll(u, HALF, 1) * sin


def wide_tables(cos, sin):
    return jnp.concatenate([cos, cos], axis=1), jnp.concatenate([-sin, sin], axis=1)


def column(row, tok):
    return jnp.broadcast_to(row, (tok, tok)).T


def lanes(array, count):
    return jnp.concatenate([array] * count, axis=1)


def head_rows(ref, first, count):
    parts = [ref[:, h * HEAD : (h + 1) * HEAD] for h in range(first, first + count)]
    return jnp.concatenate(parts, axis=0)


def split_dot(left, right, left_dim, right_dim):
    high = right.astype(BF16)
    rest = (right - high.astype(F32)).astype(BF16)
    return dot(left, high, left_dim, right_dim) + dot(left, rest, left_dim, right_dim)


def by_token(array, send, tok):
    if send == tok:
        return array
    gap = jnp.zeros((tok - send, array.shape[1]), array.dtype)
    return jnp.concatenate([array[:tok], gap, array[tok:]], axis=0)


def project_kernel(
    count, heads,
    low_ref, q_ref, k_ref, v_ref, o_ref, seg_ref, cos_ref, sin_ref, wq_ref, wv_ref,
    qr_ref, kt_ref, s_ref, dp_ref, cost_ref, sint_ref,
):
    tok = q_ref.shape[0]
    low = low_ref[...].astype(BF16)
    cost_ref[...] = cos_ref[...].T
    sint_ref[...] = sin_ref[...].T
    cos, sin = wide_tables(cos_ref[...], sin_ref[...])
    keys = rotate_rows(k_ref[...].astype(F32), cos, sin)
    kt_ref[...] = keys.T.astype(BF16)
    keys = keys.astype(BF16)
    vals = (v_ref[...].astype(F32) + dot(low[RANK:], wv_ref[...], 0, 0)).astype(BF16)
    seg_here = seg_ref[...].astype(F32)[0:1]
    key = lax.broadcasted_iota(jnp.int32, (tok, tok), 0)
    query = lax.broadcasted_iota(jnp.int32, (tok, tok), 1)
    allowed = (key <= query) & (column(seg_here, tok) == seg_here)
    bias = lanes(jnp.where(allowed, 0.0, NEG_FILL), count)
    q0 = q_ref[...].astype(F32) + SCALE * dot(low[:RANK], wq_ref[...], 0, 0)
    for g in range(0, heads, count):
        cut = slice(g * tok, (g + count) * tok)
        parts = [q0[:, h * HEAD : (h + 1) * HEAD] for h in range(g, g + count)]
        qr = jnp.concatenate([rotate_rows(u, cos, sin).astype(BF16) for u in parts], axis=0)
        qr_ref[cut] = qr
        s_ref[:, cut] = dot(keys, qr, 1, 1) * INV_ROOT + bias
        dp_ref[:, cut] = dot(vals, head_rows(o_ref, g, count), 1, 1)


def softmax_kernel(
    count, send, blocks, heads,
    qr_ref, s_ref, o_ref, seg_ref, pack_ref, base_ref, cos_ref, sin_ref, wv_ref,
    w_ref, kt_ref, dv_ref, code_ref,
):
    tok = o_ref.shape[0]
    halo = send * blocks
    cos, sin = wide_tables(cos_ref[...], sin_ref[...])
    keys = jnp.concatenate([pack_ref[b, 0:send] for b in range(blocks)], axis=0)
    keys = rotate_rows(keys.astype(F32), cos, sin)
    kt_ref[...] = keys.T.astype(BF16)
    keys = keys.astype(BF16)
    seg_here = seg_ref[...].astype(F32)[0:1]
    cols = []
    for b in range(blocks):
        row = pack_ref[b, 2 * send :].astype(F32)[0:1]
        cols.append(column(row, tok)[tok - send :])
    seg_col = jnp.concatenate(cols, axis=0)
    offset = lax.broadcasted_iota(jnp.int32, (halo, tok), 0)
    allowed = (offset + base_ref[0] >= halo) & (seg_col == seg_here)
    bias = lanes(jnp.where(allowed, 0.0, NEG_FILL), count)
    dv = jnp.zeros((tok + halo, HEAD), F32)
    for g in range(0, heads, count):
        cut = slice(g * tok, (g + count) * tok)
        far = dot(keys, qr_ref[cut], 1, 1) * INV_ROOT + bias
        s = jnp.concatenate([s_ref[:, cut], far], axis=0)
        e = jnp.exp(s - jnp.max(s, axis=0, keepdims=True))
        w = e * (1.0 / jnp.sum(e, axis=0, keepdims=True))
        w_ref[:, cut] = w
        dv = dv + dot(w.astype(BF16), head_rows(o_ref, g, count), 1, 0)
    dv_ref[...] = dv
    codes = split_dot(wv_ref[...], by_token(dv, send, tok), 1, 1)
    for b in range(blocks + 1):
        code_ref[b * RANK : (b + 1) * RANK] = codes[:, b * tok : (b + 1) * tok]


def grads_kernel(
    count, send, blocks, heads,
    low_ref, far_ref, pack_ref, o_ref, w_ref, dp_ref, kt_ref, kth_ref, dv_ref, cost_ref, sint_ref, wq_ref, wv_ref,
    code_ref, up_ref, qg_ref,
):
    tok = o_ref.shape[0]
    low = low_ref[...].astype(BF16)
    wv = wv_ref[...]
    vals = []
    for b in range(blocks):
        rows = pack_ref[b, send : 2 * send].astype(F32)
        add = dot(far_ref[b], wv, 0, 0)[tok - send :]
        vals.append((rows + add).astype(BF16))
    vals = jnp.concatenate(vals, axis=0)
    kt = jnp.concatenate([kt_ref[...], kth_ref[...]], axis=1)
    cos, sin = lanes(cost_ref[...], count), lanes(sint_ref[...], count)
    for g in range(0, heads, count):
        cut = slice(g * tok, (g + count) * tok)
        far = dot(vals, head_rows(o_ref, g, count), 1, 1)
        dp = jnp.concatenate([dp_ref[:, cut], far], axis=0)
        w = w_ref[:, cut]
        delta = jnp.sum(w * dp, axis=0, keepdims=True)
        ds = (w * (dp - delta) * INV_ROOT).astype(BF16)
        dq = dot(kt, ds, 1, 0)
        first, second = dq[:HALF], dq[HALF:]
        first, second = first * cos + second * sin, second * cos - first * sin
        turned = jnp.concatenate([first.astype(BF16), second.astype(BF16)], axis=0)
        for h in range(count):
            qg_ref[(g + h) * HEAD : (g + h + 1) * HEAD] = turned[:, h * tok : (h + 1) * tok]
    qg = qg_ref[...]
    code_ref[...] = SCALE * dot(wq_ref[...], qg, 1, 0)
    up_ref[:, : heads * HEAD] = (SCALE * dot(low[:RANK], qg, 1, 1)).astype(up_ref.dtype)
    codes = jnp.concatenate([low[RANK:]] + [far_ref[b] for b in range(blocks)], axis=1)
    up_v = SCALE * split_dot(codes, by_token(dv_ref[...], send, tok), 1, 0)
    up_ref[:, heads * HEAD :] = up_v.astype(up_ref.dtype)


def down_kernel(dl_ref, x_ref, part_ref):
    part_ref[...] = dot(dl_ref[...], x_ref[...], 1, 0)


def partial_kernel(own_ref, x_ref, both_ref, query_ref, value_ref):
    part = dot(own_ref[...], x_ref[...], 1, 0).astype(BF16)
    both_ref[...] = part
    query_ref[...] = part[:RANK]
    value_ref[...] = part[RANK:]


def combine_kernel(query_ref, up_ref, near_ref, send_ref):
    wide = query_ref.shape[1]
    send_ref[:, :wide] = query_ref[...]
    send_ref[:, wide:] = (up_ref[...].astype(F32) + near_ref[...].astype(F32)).astype(BF16)


def final_kernel(
    mine_ref, one_ref, query_ref, query_two_ref, query_three_ref, value_two_ref, value_three_ref,
    down_ref, upq_ref, upv_ref,
):
    wide, size = down_ref.shape[1], upq_ref.shape[1]
    near = mine_ref[...].astype(F32) + one_ref[...].astype(F32)
    far = query_two_ref[:, :wide].astype(F32) + query_three_ref[...].astype(F32)
    down_ref[:RANK] = near[:RANK] + far
    far = value_two_ref[...].astype(F32) + value_three_ref[...].astype(F32)
    down_ref[RANK:] = near[RANK:] + far
    up = query_ref[:, wide:].astype(F32) + query_two_ref[:, wide:].astype(F32)
    upq_ref[...] = up[:, :size]
    upv_ref[...] = up[:, size:]


def body(x, q, k, v, o, segment, a, wq, wv):
    tok, wide = x.shape
    seq_count = lax.axis_size("seq")
    fsdp_count = lax.axis_size("fsdp")
    seq_index = lax.axis_index("seq")
    heads = q.shape[1] // HEAD
    longest = tok * seq_count // 8
    blocks = -(-longest // tok)
    send = longest if blocks == 1 else tok
    halo = blocks * send
    keys = halo + tok
    direct = seq_count == 4 and fsdp_count == 4

    def swap(array, axis, bit):
        size = lax.axis_size(axis)
        return lax.ppermute(array, axis, [(i, i ^ bit) for i in range(size)])

    def shift(array, by):
        moves = [(i, (i + by) % seq_count) for i in range(seq_count)]
        return lax.ppermute(array, "seq", moves)

    def inner(array, bit):
        moves = []
        for i in range(seq_count):
            for f in range(fsdp_count):
                if f % 2 == 0:
                    source = (i ^ 1, f ^ bit)
                elif i in (1, 2):
                    source = (3 - i, f ^ bit)
                else:
                    source = (i, f ^ bit if bit % 2 else f ^ 2)
                moves.append((source[0] * fsdp_count + source[1], i * fsdp_count + f))
        return lax.ppermute(array, ("seq", "fsdp"), moves)

    def sum_fsdp(array):
        if fsdp_count != 4:
            return lax.psum(array, "fsdp")
        one, two, three = [swap(array, "fsdp", bit) for bit in (1, 2, 3)]
        return (array + one) + (two + three)

    seg_row = segment.reshape(1, tok)
    part, tails, k, v, wq = call(
        functools.partial(lowrank_kernel, send),
        [
            ((2 * RANK, tok), F32),
            ((2 * send, HEAD), BF16),
            ((tok, HEAD), BF16),
            ((tok, HEAD), BF16),
            (wq.shape, BF16),
        ],
        [
            pltpu.VMEM((tok, wide), BF16),
            pltpu.VMEM((2 * RANK, wide), BF16),
            pltpu.SemaphoreType.DMA((5,)),
        ],
        limit=FULL,
        in_specs=[pl.BlockSpec(memory_space=pltpu.HBM)] * 5,
    )(x, a.T, k, v, wq)
    seg_rows = jnp.broadcast_to(seg_row, (16, tok)).astype(BF16)
    pack = jnp.concatenate([tails, seg_rows], axis=0)
    wv = wv * SCALE
    start = seq_index * tok
    base = start.reshape(1).astype(jnp.int32)
    freqs = ROPE_BASE ** (-(2.0 * jnp.arange(HALF, dtype=F32)) / HEAD)
    positions = (start - halo + jnp.arange(keys, dtype=jnp.int32)).astype(F32)
    angles = positions[:, None] * freqs[None, :]
    cos, sin = jnp.cos(angles), jnp.sin(angles)
    packs = jnp.stack([shift(pack, d) for d in range(blocks, 0, -1)])
    low = sum_fsdp(part)
    low, cos, sin, wv = lax.optimization_barrier((low, cos, sin, wv))
    low_v = low[RANK:].astype(BF16)
    if direct:
        far = inner(low_v, 0)
    else:
        lows = jnp.stack([shift(low_v, d) for d in range(blocks, 0, -1)])
    count = heads if blocks == 1 else 1
    qr, kt, s, dp, cos_t, sin_t = call(
        functools.partial(project_kernel, count, heads),
        [
            ((heads * tok, HEAD), BF16),
            ((HEAD, tok), BF16),
            ((tok, heads * tok), F32),
            ((tok, heads * tok), F32),
            ((HALF, tok), F32),
            ((HALF, tok), F32),
        ],
        cost=3 << 20,
    )(low, q, k, v, o, seg_rows, cos[halo:], sin[halo:], wq, wv)
    specs = [pl.BlockSpec(memory_space=pltpu.VMEM)] * 9
    specs[5] = pl.BlockSpec(memory_space=pltpu.SMEM)
    w, kt_far, dv, codes_v = call(
        functools.partial(softmax_kernel, count, send, blocks, heads),
        [
            ((keys, heads * tok), F32),
            ((HEAD, halo), BF16),
            ((keys, HEAD), F32),
            (((blocks + 1) * RANK, tok), F32),
        ],
        in_specs=specs,
        cost=5 << 20,
    )(qr, s, o, seg_rows, packs, base, cos[:halo], sin[:halo], wv)
    if direct:
        w, far = lax.optimization_barrier((w, far))
        mine = (seq_index == 2) == (lax.axis_index("fsdp") % 2 == 1)
        lows = jnp.where(mine, far, swap(far, "fsdp", 1))[None]
    code_v = codes_v[:RANK]
    if direct:
        parts = [inner(codes_v[RANK:], bit) for bit in range(4)]
        back = (parts[0] + parts[1]) + (parts[2] + parts[3])
        even = lax.axis_index("fsdp") % 2 == 0
        mine = even == (seq_index % 2 == 0)
        back = jnp.where(mine, back, swap(back, "fsdp", 1))
        back = jnp.where(seq_index < seq_count - 1, back, 0.0)
    code_q, up = call(
        functools.partial(grads_kernel, count, send, blocks, heads),
        [((RANK, tok), F32), ((RANK, (heads + 1) * HEAD), BF16 if direct else F32)],
        [pltpu.VMEM((heads * HEAD, tok), BF16)],
        cost=24 << 20,
    )(low, lows, packs, o, w, dp, kt, kt_far, dv, cos_t, sin_t, wq, wv)
    if not direct:
        for b, d in enumerate(range(blocks, 0, -1)):
            code_v = code_v + shift(codes_v[(b + 1) * RANK : (b + 2) * RANK], -d)
        dlow = sum_fsdp(jnp.concatenate([code_q, code_v], axis=0)).astype(BF16)
        (down,) = call(down_kernel, [((2 * RANK, wide), F32)])(dlow, x)
        down, up = lax.psum((down, up), "seq")
        return down.T, up[:, : heads * HEAD], up[:, heads * HEAD :]

    codes = sum_fsdp(jnp.concatenate([code_q, code_v], axis=0))
    dlow = jnp.concatenate([codes[:RANK], codes[RANK:] + back], axis=0).astype(BF16)
    near_up = swap(up, "seq", 1)
    both, part_q, part_v = call(
        partial_kernel, [((2 * RANK, wide), BF16), ((RANK, wide), BF16), ((RANK, wide), BF16)]
    )(dlow, x)
    (send_q,) = call(combine_kernel, [((RANK, wide + up.shape[1]), BF16)])(part_q, up, near_up)
    value_two = swap(part_v, "seq", 2)
    value_three = swap(value_two, "seq", 1)
    query_two, query_three = swap(send_q, "seq", 2), swap(part_q, "seq", 3)
    one = swap(both, "seq", 1)
    down, up_q, up_v = call(
        final_kernel,
        [((2 * RANK, wide), F32), ((RANK, heads * HEAD), F32), ((RANK, HEAD), F32)],
    )(both, one, send_q, query_two, query_three, value_two, value_three)
    return down.T, up_q, up_v


def solution(mesh):
    rows = ("groups", "seq")
    in_specs = (
        P(rows, "fsdp"),
        P(rows, "fsdp"),
        P(rows, "fsdp"),
        P(rows, "fsdp"),
        P(rows, "fsdp"),
        P(rows),
        P("fsdp", None),
        P(None, "fsdp"),
        P(None, "fsdp"),
    )
    out_specs = (P(("groups", "fsdp"), None), P("groups", "fsdp"), P("groups", "fsdp"))
    return jax.shard_map(body, mesh=mesh, in_specs=in_specs, out_specs=out_specs, check_vma=False)
```

```python
import functools
import math

import jax
import jax.numpy as jnp
from jax import lax
from jax.experimental import pallas as pl
from jax.experimental.pallas import tpu as pltpu
from jax.sharding import PartitionSpec as P

HEAD = 128
HALF = HEAD // 2
RANK = 16
SCALE = 2.0
ROPE_BASE = 500000.0
NEG_FILL = -1e30
INV_ROOT = 1.0 / math.sqrt(HEAD)
F32 = jnp.float32
BF16 = jnp.bfloat16
LIMIT = 40 * 1024 * 1024
FULL = 55080 * 1024


def dot(left, right, left_dim, right_dim):
    return lax.dot_general(
        left,
        right,
        (((left_dim,), (right_dim,)), ((), ())),
        preferred_element_type=F32,
    )


def call(kernel, out_shapes, scratch=(), limit=LIMIT, cost=1, **specs):
    return pl.pallas_call(
        kernel,
        out_shape=[jax.ShapeDtypeStruct(s, d) for s, d in out_shapes],
        **specs,
        scratch_shapes=list(scratch),
        compiler_params=pltpu.CompilerParams(vmem_limit_bytes=limit),
        cost_estimate=pl.CostEstimate(flops=cost, bytes_accessed=cost, transcendentals=0),
    )


def lowrank_kernel(send, *refs):
    sources, (part_ref, tails_ref, k_ref, v_ref, wq_ref) = refs[:5], refs[5:10]
    x_ref, a_ref, sems = refs[10:]
    targets = (x_ref, a_ref, k_ref, v_ref, wq_ref)
    copies = []
    for i, (source, target) in enumerate(zip(sources, targets)):
        copies.append(pltpu.make_async_copy(source, target, sems.at[i]))
        copies[-1].start()
    for copy in copies:
        copy.wait()
    part_ref[...] = dot(a_ref[...], x_ref[...], 1, 1)
    tok = k_ref.shape[0]
    tails_ref[0:send] = k_ref[tok - send :]
    tails_ref[send:] = v_ref[tok - send :]


def rotate_rows(u, cos, sin):
    return u * cos + pltpu.roll(u, HALF, 1) * sin


def wide_tables(cos, sin):
    return jnp.concatenate([cos, cos], axis=1), jnp.concatenate([-sin, sin], axis=1)


def column(row, tok):
    return jnp.broadcast_to(row, (tok, tok)).T


def lanes(array, count):
    return jnp.concatenate([array] * count, axis=1)


def head_rows(ref, first, count):
    parts = [ref[:, h * HEAD : (h + 1) * HEAD] for h in range(first, first + count)]
    return jnp.concatenate(parts, axis=0)


def split_dot(left, right, left_dim, right_dim):
    high = right.astype(BF16)
    rest = (right - high.astype(F32)).astype(BF16)
    return dot(left, high, left_dim, right_dim) + dot(left, rest, left_dim, right_dim)


def by_token(array, send, tok):
    if send == tok:
        return array
    gap = jnp.zeros((tok - send, array.shape[1]), array.dtype)
    return jnp.concatenate([array[:tok], gap, array[tok:]], axis=0)


def project_kernel(
    count, heads,
    low_ref, q_ref, k_ref, seg_ref, cos_ref, sin_ref, wq_ref,
    qr_ref, kt_ref, s_ref, cost_ref, sint_ref,
):
    tok = q_ref.shape[0]
    low = low_ref[...].astype(BF16)
    cost_ref[...] = cos_ref[...].T
    sint_ref[...] = sin_ref[...].T
    cos, sin = wide_tables(cos_ref[...], sin_ref[...])
    keys = rotate_rows(k_ref[...].astype(F32), cos, sin)
    kt_ref[...] = keys.T.astype(BF16)
    keys = keys.astype(BF16)
    seg_here = seg_ref[...].astype(F32)[0:1]
    key = lax.broadcasted_iota(jnp.int32, (tok, tok), 0)
    query = lax.broadcasted_iota(jnp.int32, (tok, tok), 1)
    allowed = (key <= query) & (column(seg_here, tok) == seg_here)
    bias = lanes(jnp.where(allowed, 0.0, NEG_FILL), count)
    q0 = q_ref[...].astype(F32) + SCALE * dot(low[:RANK], wq_ref[...], 0, 0)
    for g in range(0, heads, count):
        cut = slice(g * tok, (g + count) * tok)
        parts = [q0[:, h * HEAD : (h + 1) * HEAD] for h in range(g, g + count)]
        qr = jnp.concatenate([rotate_rows(u, cos, sin).astype(BF16) for u in parts], axis=0)
        qr_ref[cut] = qr
        s_ref[:, cut] = dot(keys, qr, 1, 1) * INV_ROOT + bias


def own_kernel(count, heads, low_ref, v_ref, o_ref, wv_ref, dp_ref):
    low_v = low_ref[RANK:].astype(BF16)
    vals = (v_ref[...].astype(F32) + dot(low_v, wv_ref[...], 0, 0)).astype(BF16)
    tok = o_ref.shape[0]
    for g in range(0, heads, count):
        cut = slice(g * tok, (g + count) * tok)
        dp_ref[:, cut] = dot(vals, head_rows(o_ref, g, count), 1, 1)


def softmax_kernel(
    count, send, blocks, heads,
    qr_ref, s_ref, o_ref, seg_ref, pack_ref, base_ref, cos_ref, sin_ref, wv_ref, low_ref,
    w_ref, kt_ref, dv_ref, code_ref,
):
    tok = o_ref.shape[0]
    halo = send * blocks
    cos, sin = wide_tables(cos_ref[...], sin_ref[...])
    keys = jnp.concatenate([pack_ref[b, 0:send] for b in range(blocks)], axis=0)
    keys = rotate_rows(keys.astype(F32), cos, sin)
    kt_ref[...] = keys.T.astype(BF16)
    keys = keys.astype(BF16)
    seg_here = seg_ref[...].astype(F32)[0:1]
    cols = []
    for b in range(blocks):
        row = pack_ref[b, 2 * send :].astype(F32)[0:1]
        cols.append(column(row, tok)[tok - send :])
    seg_col = jnp.concatenate(cols, axis=0)
    offset = lax.broadcasted_iota(jnp.int32, (halo, tok), 0)
    allowed = (offset + base_ref[0] >= halo) & (seg_col == seg_here)
    bias = lanes(jnp.where(allowed, 0.0, NEG_FILL), count)
    dv = jnp.zeros((tok + halo, HEAD), F32)
    for g in range(0, heads, count):
        cut = slice(g * tok, (g + count) * tok)
        far = dot(keys, qr_ref[cut], 1, 1) * INV_ROOT + bias
        s = jnp.concatenate([s_ref[:, cut], far], axis=0)
        e = jnp.exp(s - jnp.max(s, axis=0, keepdims=True))
        w = e * (1.0 / jnp.sum(e, axis=0, keepdims=True))
        w_ref[:, cut] = w
        dv = dv + dot(w.astype(BF16), head_rows(o_ref, g, count), 1, 0)
    dv_ref[...] = dv
    codes = split_dot(wv_ref[...], by_token(dv, send, tok), 1, 1)
    for b in range(blocks + 1):
        code_ref[b * RANK : (b + 1) * RANK] = codes[:, b * tok : (b + 1) * tok]
    code_ref[(blocks + 1) * RANK :] = low_ref[RANK:].astype(BF16).astype(F32)


def grads_kernel(
    count, send, blocks, heads,
    low_ref, far_ref, pack_ref, o_ref, w_ref, dp_ref, kt_ref, kth_ref, dv_ref, cost_ref, sint_ref, wq_ref, wv_ref,
    code_ref, up_ref, qg_ref,
):
    tok = o_ref.shape[0]
    low = low_ref[...].astype(BF16)
    wv = wv_ref[...]
    vals = []
    for b in range(blocks):
        rows = pack_ref[b, send : 2 * send].astype(F32)
        add = dot(far_ref[b], wv, 0, 0)[tok - send :]
        vals.append((rows + add).astype(BF16))
    vals = jnp.concatenate(vals, axis=0)
    kt = jnp.concatenate([kt_ref[...], kth_ref[...]], axis=1)
    cos, sin = lanes(cost_ref[...], count), lanes(sint_ref[...], count)
    for g in range(0, heads, count):
        cut = slice(g * tok, (g + count) * tok)
        far = dot(vals, head_rows(o_ref, g, count), 1, 1)
        dp = jnp.concatenate([dp_ref[:, cut], far], axis=0)
        w = w_ref[:, cut]
        delta = jnp.sum(w * dp, axis=0, keepdims=True)
        ds = (w * (dp - delta) * INV_ROOT).astype(BF16)
        dq = dot(kt, ds, 1, 0)
        first, second = dq[:HALF], dq[HALF:]
        first, second = first * cos + second * sin, second * cos - first * sin
        turned = jnp.concatenate([first.astype(BF16), second.astype(BF16)], axis=0)
        for h in range(count):
            qg_ref[(g + h) * HEAD : (g + h + 1) * HEAD] = turned[:, h * tok : (h + 1) * tok]
    qg = qg_ref[...]
    code_ref[...] = SCALE * dot(wq_ref[...], qg, 1, 0)
    up_ref[:, : heads * HEAD] = (SCALE * dot(low[:RANK], qg, 1, 1)).astype(up_ref.dtype)
    codes = jnp.concatenate([low[RANK:]] + [far_ref[b] for b in range(blocks)], axis=1)
    up_v = SCALE * split_dot(codes, by_token(dv_ref[...], send, tok), 1, 0)
    up_ref[:, heads * HEAD :] = up_v.astype(up_ref.dtype)


def down_kernel(dl_ref, x_ref, part_ref):
    part_ref[...] = dot(dl_ref[...], x_ref[...], 1, 0)


def partial_kernel(own_ref, x_ref, both_ref, query_ref, value_ref):
    part = dot(own_ref[...], x_ref[...], 1, 0).astype(BF16)
    both_ref[...] = part
    query_ref[...] = part[:RANK]
    value_ref[...] = part[RANK:]


def combine_kernel(query_ref, up_ref, near_ref, send_ref):
    wide = query_ref.shape[1]
    send_ref[:, :wide] = query_ref[...]
    send_ref[:, wide:] = (up_ref[...].astype(F32) + near_ref[...].astype(F32)).astype(BF16)


def final_kernel(
    mine_ref, one_ref, query_ref, query_two_ref, query_three_ref, value_two_ref, value_three_ref,
    down_ref, upq_ref, upv_ref,
):
    wide, size = down_ref.shape[1], upq_ref.shape[1]
    near = mine_ref[...].astype(F32) + one_ref[...].astype(F32)
    far = query_two_ref[:, :wide].astype(F32) + query_three_ref[...].astype(F32)
    down_ref[:RANK] = near[:RANK] + far
    far = value_two_ref[...].astype(F32) + value_three_ref[...].astype(F32)
    down_ref[RANK:] = near[RANK:] + far
    up = query_ref[:, wide:].astype(F32) + query_two_ref[:, wide:].astype(F32)
    upq_ref[...] = up[:, :size]
    upv_ref[...] = up[:, size:]


def body(x, q, k, v, o, segment, a, wq, wv):
    tok, wide = x.shape
    seq_count = lax.axis_size("seq")
    fsdp_count = lax.axis_size("fsdp")
    seq_index = lax.axis_index("seq")
    heads = q.shape[1] // HEAD
    longest = tok * seq_count // 8
    blocks = -(-longest // tok)
    send = longest if blocks == 1 else tok
    halo = blocks * send
    keys = halo + tok
    direct = seq_count == 4 and fsdp_count == 4

    def swap(array, axis, bit):
        size = lax.axis_size(axis)
        return lax.ppermute(array, axis, [(i, i ^ bit) for i in range(size)])

    def shift(array, by):
        moves = [(i, (i + by) % seq_count) for i in range(seq_count)]
        return lax.ppermute(array, "seq", moves)

    def inner(array):
        moves = []
        for i in range(seq_count):
            for f in range(fsdp_count):
                to, flip = (3 - i, 0) if i in (1, 2) else (i, 2)
                moves.append((i * fsdp_count + f, to * fsdp_count + (f ^ flip)))
        return lax.ppermute(array, ("seq", "fsdp"), moves)

    def sum_fsdp(array):
        if fsdp_count != 4:
            return lax.psum(array, "fsdp")
        one, two, three = [swap(array, "fsdp", bit) for bit in (1, 2, 3)]
        return (array + one) + (two + three)

    seg_row = segment.reshape(1, tok)
    part, tails, k, v, wq = call(
        functools.partial(lowrank_kernel, send),
        [
            ((2 * RANK, tok), F32),
            ((2 * send, HEAD), BF16),
            ((tok, HEAD), BF16),
            ((tok, HEAD), BF16),
            (wq.shape, BF16),
        ],
        [
            pltpu.VMEM((tok, wide), BF16),
            pltpu.VMEM((2 * RANK, wide), BF16),
            pltpu.SemaphoreType.DMA((5,)),
        ],
        limit=FULL,
        in_specs=[pl.BlockSpec(memory_space=pltpu.HBM)] * 5,
    )(x, a.T, k, v, wq)
    seg_rows = jnp.broadcast_to(seg_row, (16, tok)).astype(BF16)
    pack = jnp.concatenate([tails, seg_rows], axis=0)
    wv = wv * SCALE
    start = seq_index * tok
    base = start.reshape(1).astype(jnp.int32)
    freqs = ROPE_BASE ** (-(2.0 * jnp.arange(HALF, dtype=F32)) / HEAD)
    positions = (start - halo + jnp.arange(keys, dtype=jnp.int32)).astype(F32)
    angles = positions[:, None] * freqs[None, :]
    cos, sin = jnp.cos(angles), jnp.sin(angles)
    packs = jnp.stack([shift(pack, d) for d in range(blocks, 0, -1)])
    low = sum_fsdp(part)
    low, cos, sin, wv = lax.optimization_barrier((low, cos, sin, wv))
    count = heads if blocks == 1 else 1
    qr, kt, s, cos_t, sin_t = call(
        functools.partial(project_kernel, count, heads),
        [
            ((heads * tok, HEAD), BF16),
            ((HEAD, tok), BF16),
            ((tok, heads * tok), F32),
            ((HALF, tok), F32),
            ((HALF, tok), F32),
        ],
        cost=3 << 20,
    )(low, q, k, seg_rows, cos[halo:], sin[halo:], wq)
    specs = [pl.BlockSpec(memory_space=pltpu.VMEM)] * 10
    specs[5] = pl.BlockSpec(memory_space=pltpu.SMEM)
    w, kt_far, dv, codes_v = call(
        functools.partial(softmax_kernel, count, send, blocks, heads),
        [
            ((keys, heads * tok), F32),
            ((HEAD, halo), BF16),
            ((keys, HEAD), F32),
            (((blocks + 2) * RANK, tok), F32),
        ],
        in_specs=specs,
        cost=5 << 20,
    )(qr, s, o, seg_rows, packs, base, cos[:halo], sin[:halo], wv, low)
    code_v = codes_v[:RANK]
    low_v, dv = lax.optimization_barrier((low, dv))
    (dp,) = call(
        functools.partial(own_kernel, count, heads), [((tok, heads * tok), F32)], cost=24 << 20
    )(low_v, v, o, wv)
    if direct:
        outer, middle = swap(codes_v[RANK:], "seq", 1), inner(codes_v[RANK:])
        lows = jnp.where(seq_index == 2, middle[RANK:], outer[RANK:]).astype(BF16)[None]
        back = jnp.where(seq_index == 1, middle[:RANK], 0.0)
        code_v = code_v + jnp.where(seq_index % 2 == 0, outer[:RANK], back)
    else:
        low_v = low[RANK:].astype(BF16)
        lows = jnp.stack([shift(low_v, d) for d in range(blocks, 0, -1)])
        for b, d in enumerate(range(blocks, 0, -1)):
            code_v = code_v + shift(codes_v[(b + 1) * RANK : (b + 2) * RANK], -d)
    code_q, up = call(
        functools.partial(grads_kernel, count, send, blocks, heads),
        [((RANK, tok), F32), ((RANK, (heads + 1) * HEAD), BF16 if direct else F32)],
        [pltpu.VMEM((heads * HEAD, tok), BF16)],
        cost=24 << 20,
    )(low, lows, packs, o, w, dp, kt, kt_far, dv, cos_t, sin_t, wq, wv)
    if not direct:
        dlow = sum_fsdp(jnp.concatenate([code_q, code_v], axis=0)).astype(BF16)
        (down,) = call(down_kernel, [((2 * RANK, wide), F32)])(dlow, x)
        down, up = lax.psum((down, up), "seq")
        return down.T, up[:, : heads * HEAD], up[:, heads * HEAD :]

    codes = jnp.concatenate([code_q, code_v], axis=0)
    near_up = swap(up, "seq", 1)
    both, part_q, part_v = call(
        partial_kernel, [((2 * RANK, wide), BF16), ((RANK, wide), BF16), ((RANK, wide), BF16)]
    )(sum_fsdp(codes).astype(BF16), x)
    (send_q,) = call(combine_kernel, [((RANK, wide + up.shape[1]), BF16)])(part_q, up, near_up)
    value_two = swap(part_v, "seq", 2)
    value_three = swap(value_two, "seq", 1)
    query_two, query_three = swap(send_q, "seq", 2), swap(part_q, "seq", 3)
    one = swap(both, "seq", 1)
    down, up_q, up_v = call(
        final_kernel,
        [((2 * RANK, wide), F32), ((RANK, heads * HEAD), F32), ((RANK, HEAD), F32)],
    )(both, one, send_q, query_two, query_three, value_two, value_three)
    return down.T, up_q, up_v


def solution(mesh):
    rows = ("groups", "seq")
    in_specs = (
        P(rows, "fsdp"),
        P(rows, "fsdp"),
        P(rows, "fsdp"),
        P(rows, "fsdp"),
        P(rows, "fsdp"),
        P(rows),
        P("fsdp", None),
        P(None, "fsdp"),
        P(None, "fsdp"),
    )
    out_specs = (P(("groups", "fsdp"), None), P("groups", "fsdp"), P("groups", "fsdp"))
    return jax.shard_map(body, mesh=mesh, in_specs=in_specs, out_specs=out_specs, check_vma=False)
```

```python
import functools
import math

import jax
import jax.numpy as jnp
from jax import lax
from jax.experimental import pallas as pl
from jax.experimental.pallas import tpu as pltpu
from jax.sharding import PartitionSpec as P

HEAD = 128
HALF = HEAD // 2
RANK = 16
SCALE = 2.0
ROPE_BASE = 500000.0
NEG_FILL = -1e30
INV_ROOT = 1.0 / math.sqrt(HEAD)
F32 = jnp.float32
BF16 = jnp.bfloat16
LIMIT = 40 * 1024 * 1024
FULL = 55080 * 1024


def dot(left, right, left_dim, right_dim):
    return lax.dot_general(
        left,
        right,
        (((left_dim,), (right_dim,)), ((), ())),
        preferred_element_type=F32,
    )


def call(kernel, out_shapes, scratch=(), limit=LIMIT, cost=1, **specs):
    return pl.pallas_call(
        kernel,
        out_shape=[jax.ShapeDtypeStruct(s, d) for s, d in out_shapes],
        **specs,
        scratch_shapes=list(scratch),
        compiler_params=pltpu.CompilerParams(vmem_limit_bytes=limit),
        cost_estimate=pl.CostEstimate(flops=cost, bytes_accessed=cost, transcendentals=0),
    )


def lowrank_kernel(send, *refs):
    sources, (part_ref, tails_ref, k_ref, v_ref, wq_ref) = refs[:5], refs[5:10]
    x_ref, a_ref, sems = refs[10:]
    targets = (x_ref, a_ref, k_ref, v_ref, wq_ref)
    copies = []
    for i, (source, target) in enumerate(zip(sources, targets)):
        copies.append(pltpu.make_async_copy(source, target, sems.at[i]))
        copies[-1].start()
    for copy in copies:
        copy.wait()
    part_ref[...] = dot(a_ref[...], x_ref[...], 1, 1)
    tok = k_ref.shape[0]
    tails_ref[0:send] = k_ref[tok - send :]
    tails_ref[send:] = v_ref[tok - send :]


def rotate_rows(u, cos, sin):
    return u * cos + pltpu.roll(u, HALF, 1) * sin


def wide_tables(cos, sin):
    return jnp.concatenate([cos, cos], axis=1), jnp.concatenate([-sin, sin], axis=1)


def column(row, tok):
    return jnp.broadcast_to(row, (tok, tok)).T


def lanes(array, count):
    return jnp.concatenate([array] * count, axis=1)


def head_rows(ref, first, count):
    parts = [ref[:, h * HEAD : (h + 1) * HEAD] for h in range(first, first + count)]
    return jnp.concatenate(parts, axis=0)


def split_dot(left, right, left_dim, right_dim):
    high = right.astype(BF16)
    rest = (right - high.astype(F32)).astype(BF16)
    return dot(left, high, left_dim, right_dim) + dot(left, rest, left_dim, right_dim)


def by_token(array, send, tok):
    if send == tok:
        return array
    gap = jnp.zeros((tok - send, array.shape[1]), array.dtype)
    return jnp.concatenate([array[:tok], gap, array[tok:]], axis=0)


def project_kernel(
    count, heads,
    low_ref, q_ref, k_ref, seg_ref, cos_ref, sin_ref, wq_ref,
    qr_ref, kt_ref, s_ref, cost_ref, sint_ref,
):
    tok = q_ref.shape[0]
    low = low_ref[...].astype(BF16)
    cost_ref[...] = cos_ref[...].T
    sint_ref[...] = sin_ref[...].T
    cos, sin = wide_tables(cos_ref[...], sin_ref[...])
    keys = rotate_rows(k_ref[...].astype(F32), cos, sin)
    kt_ref[...] = keys.T.astype(BF16)
    keys = keys.astype(BF16)
    seg_here = seg_ref[...].astype(F32)[0:1]
    key = lax.broadcasted_iota(jnp.int32, (tok, tok), 0)
    query = lax.broadcasted_iota(jnp.int32, (tok, tok), 1)
    allowed = (key <= query) & (column(seg_here, tok) == seg_here)
    bias = lanes(jnp.where(allowed, 0.0, NEG_FILL), count)
    q0 = q_ref[...].astype(F32) + SCALE * dot(low[:RANK], wq_ref[...], 0, 0)
    for g in range(0, heads, count):
        cut = slice(g * tok, (g + count) * tok)
        parts = [q0[:, h * HEAD : (h + 1) * HEAD] for h in range(g, g + count)]
        qr = jnp.concatenate([rotate_rows(u, cos, sin).astype(BF16) for u in parts], axis=0)
        qr_ref[cut] = qr
        s_ref[:, cut] = dot(keys, qr, 1, 1) * INV_ROOT + bias


def own_kernel(count, heads, low_ref, v_ref, o_ref, wv_ref, dp_ref):
    low_v = low_ref[RANK:].astype(BF16)
    vals = (v_ref[...].astype(F32) + dot(low_v, wv_ref[...], 0, 0)).astype(BF16)
    tok = o_ref.shape[0]
    for g in range(0, heads, count):
        cut = slice(g * tok, (g + count) * tok)
        dp_ref[:, cut] = dot(vals, head_rows(o_ref, g, count), 1, 1)


def softmax_kernel(
    count, send, blocks, heads,
    qr_ref, s_ref, o_ref, seg_ref, pack_ref, base_ref, cos_ref, sin_ref, wv_ref, low_ref,
    w_ref, kt_ref, dv_ref, code_ref,
):
    tok = o_ref.shape[0]
    halo = send * blocks
    cos, sin = wide_tables(cos_ref[...], sin_ref[...])
    keys = jnp.concatenate([pack_ref[b, 0:send] for b in range(blocks)], axis=0)
    keys = rotate_rows(keys.astype(F32), cos, sin)
    kt_ref[...] = keys.T.astype(BF16)
    keys = keys.astype(BF16)
    seg_here = seg_ref[...].astype(F32)[0:1]
    cols = []
    for b in range(blocks):
        row = pack_ref[b, 2 * send :].astype(F32)[0:1]
        cols.append(column(row, tok)[tok - send :])
    seg_col = jnp.concatenate(cols, axis=0)
    offset = lax.broadcasted_iota(jnp.int32, (halo, tok), 0)
    allowed = (offset + base_ref[0] >= halo) & (seg_col == seg_here)
    bias = lanes(jnp.where(allowed, 0.0, NEG_FILL), count)
    dv = jnp.zeros((tok + halo, HEAD), F32)
    for g in range(0, heads, count):
        cut = slice(g * tok, (g + count) * tok)
        far = dot(keys, qr_ref[cut], 1, 1) * INV_ROOT + bias
        s = jnp.concatenate([s_ref[:, cut], far], axis=0)
        e = jnp.exp(s - jnp.max(s, axis=0, keepdims=True))
        w = e * (1.0 / jnp.sum(e, axis=0, keepdims=True))
        w_ref[:, cut] = w
        dv = dv + dot(w.astype(BF16), head_rows(o_ref, g, count), 1, 0)
    dv_ref[...] = dv
    codes = split_dot(wv_ref[...], by_token(dv, send, tok), 1, 1)
    for b in range(blocks + 1):
        code_ref[b * RANK : (b + 1) * RANK] = codes[:, b * tok : (b + 1) * tok]
    code_ref[(blocks + 1) * RANK :] = low_ref[RANK:].astype(BF16).astype(F32)


def grads_kernel(
    count, send, blocks, heads,
    low_ref, far_ref, pack_ref, o_ref, w_ref, dp_ref, kt_ref, kth_ref, dv_ref, cost_ref, sint_ref, wq_ref, wv_ref,
    code_ref, up_ref, qg_ref,
):
    tok = o_ref.shape[0]
    low = low_ref[...].astype(BF16)
    wv = wv_ref[...]
    vals = []
    for b in range(blocks):
        rows = pack_ref[b, send : 2 * send].astype(F32)
        add = dot(far_ref[b], wv, 0, 0)[tok - send :]
        vals.append((rows + add).astype(BF16))
    vals = jnp.concatenate(vals, axis=0)
    kt = jnp.concatenate([kt_ref[...], kth_ref[...]], axis=1)
    cos, sin = lanes(cost_ref[...], count), lanes(sint_ref[...], count)
    for g in range(0, heads, count):
        cut = slice(g * tok, (g + count) * tok)
        far = dot(vals, head_rows(o_ref, g, count), 1, 1)
        dp = jnp.concatenate([dp_ref[:, cut], far], axis=0)
        w = w_ref[:, cut]
        delta = jnp.sum(w * dp, axis=0, keepdims=True)
        ds = (w * (dp - delta) * INV_ROOT).astype(BF16)
        dq = dot(kt, ds, 1, 0)
        first, second = dq[:HALF], dq[HALF:]
        first, second = first * cos + second * sin, second * cos - first * sin
        turned = jnp.concatenate([first.astype(BF16), second.astype(BF16)], axis=0)
        for h in range(count):
            qg_ref[(g + h) * HEAD : (g + h + 1) * HEAD] = turned[:, h * tok : (h + 1) * tok]
    qg = qg_ref[...]
    code_ref[...] = SCALE * dot(wq_ref[...], qg, 1, 0)
    up_ref[:, : heads * HEAD] = (SCALE * dot(low[:RANK], qg, 1, 1)).astype(up_ref.dtype)
    codes = jnp.concatenate([low[RANK:]] + [far_ref[b] for b in range(blocks)], axis=1)
    up_v = SCALE * split_dot(codes, by_token(dv_ref[...], send, tok), 1, 0)
    up_ref[:, heads * HEAD :] = up_v.astype(up_ref.dtype)


def down_kernel(dl_ref, x_ref, part_ref):
    part_ref[...] = dot(dl_ref[...], x_ref[...], 1, 0)


def partial_kernel(own_ref, x_ref, both_ref, query_ref, value_ref):
    part = dot(own_ref[...], x_ref[...], 1, 0).astype(BF16)
    both_ref[...] = part
    query_ref[...] = part[:RANK]
    value_ref[...] = part[RANK:]


def combine_kernel(query_ref, up_ref, near_ref, send_ref):
    wide = query_ref.shape[1]
    send_ref[:, :wide] = query_ref[...]
    send_ref[:, wide:] = (up_ref[...].astype(F32) + near_ref[...].astype(F32)).astype(BF16)


def final_kernel(
    mine_ref, query_ref, query_two_ref, query_three_ref, value_two_ref, value_three_ref, query_one_ref, value_one_ref,
    down_ref, upq_ref, upv_ref,
):
    wide, size = down_ref.shape[1], upq_ref.shape[1]
    one = jnp.concatenate([query_one_ref[...], value_one_ref[...]], axis=0)
    near = mine_ref[...].astype(F32) + one.astype(F32)
    far = query_two_ref[:, :wide].astype(F32) + query_three_ref[...].astype(F32)
    down_ref[:RANK] = near[:RANK] + far
    far = value_two_ref[...].astype(F32) + value_three_ref[...].astype(F32)
    down_ref[RANK:] = near[RANK:] + far
    up = query_ref[:, wide:].astype(F32) + query_two_ref[:, wide:].astype(F32)
    upq_ref[...] = up[:, :size]
    upv_ref[...] = up[:, size:]


def body(x, q, k, v, o, segment, a, wq, wv):
    tok, wide = x.shape
    seq_count = lax.axis_size("seq")
    fsdp_count = lax.axis_size("fsdp")
    seq_index = lax.axis_index("seq")
    heads = q.shape[1] // HEAD
    longest = tok * seq_count // 8
    blocks = -(-longest // tok)
    send = longest if blocks == 1 else tok
    halo = blocks * send
    keys = halo + tok
    direct = seq_count == 4 and fsdp_count == 4

    def swap(array, axis, bit):
        size = lax.axis_size(axis)
        return lax.ppermute(array, axis, [(i, i ^ bit) for i in range(size)])

    def shift(array, by):
        moves = [(i, (i + by) % seq_count) for i in range(seq_count)]
        return lax.ppermute(array, "seq", moves)

    def inner(array):
        moves = []
        for i in range(seq_count):
            for f in range(fsdp_count):
                to, flip = (3 - i, 0) if i in (1, 2) else (i, 2)
                moves.append((i * fsdp_count + f, to * fsdp_count + (f ^ flip)))
        return lax.ppermute(array, ("seq", "fsdp"), moves)

    def sum_fsdp(array):
        if fsdp_count != 4:
            return lax.psum(array, "fsdp")
        one, two, three = [swap(array, "fsdp", bit) for bit in (1, 2, 3)]
        return (array + one) + (two + three)

    seg_row = segment.reshape(1, tok)
    part, tails, k, v, wq = call(
        functools.partial(lowrank_kernel, send),
        [
            ((2 * RANK, tok), F32),
            ((2 * send, HEAD), BF16),
            ((tok, HEAD), BF16),
            ((tok, HEAD), BF16),
            (wq.shape, BF16),
        ],
        [
            pltpu.VMEM((tok, wide), BF16),
            pltpu.VMEM((2 * RANK, wide), BF16),
            pltpu.SemaphoreType.DMA((5,)),
        ],
        limit=FULL,
        in_specs=[pl.BlockSpec(memory_space=pltpu.HBM)] * 5,
    )(x, a.T, k, v, wq)
    seg_rows = jnp.broadcast_to(seg_row, (16, tok)).astype(BF16)
    pack = jnp.concatenate([tails, seg_rows], axis=0)
    wv = wv * SCALE
    start = seq_index * tok
    base = start.reshape(1).astype(jnp.int32)
    freqs = ROPE_BASE ** (-(2.0 * jnp.arange(HALF, dtype=F32)) / HEAD)
    positions = (start - halo + jnp.arange(keys, dtype=jnp.int32)).astype(F32)
    angles = positions[:, None] * freqs[None, :]
    cos, sin = jnp.cos(angles), jnp.sin(angles)
    packs = jnp.stack([shift(pack, d) for d in range(blocks, 0, -1)])
    low = sum_fsdp(part)
    low, cos, sin, wv = lax.optimization_barrier((low, cos, sin, wv))
    count = heads if blocks == 1 else 1
    qr, kt, s, cos_t, sin_t = call(
        functools.partial(project_kernel, count, heads),
        [
            ((heads * tok, HEAD), BF16),
            ((HEAD, tok), BF16),
            ((tok, heads * tok), F32),
            ((HALF, tok), F32),
            ((HALF, tok), F32),
        ],
        cost=3 << 20,
    )(low, q, k, seg_rows, cos[halo:], sin[halo:], wq)
    specs = [pl.BlockSpec(memory_space=pltpu.VMEM)] * 10
    specs[5] = pl.BlockSpec(memory_space=pltpu.SMEM)
    w, kt_far, dv, codes_v = call(
        functools.partial(softmax_kernel, count, send, blocks, heads),
        [
            ((keys, heads * tok), F32),
            ((HEAD, halo), BF16),
            ((keys, HEAD), F32),
            (((blocks + 2) * RANK, tok), F32),
        ],
        in_specs=specs,
        cost=5 << 20,
    )(qr, s, o, seg_rows, packs, base, cos[:halo], sin[:halo], wv, low)
    code_v = codes_v[:RANK]
    low_v, dv = lax.optimization_barrier((low, dv))
    (dp,) = call(
        functools.partial(own_kernel, count, heads), [((tok, heads * tok), F32)], cost=24 << 20
    )(low_v, v, o, wv)
    if direct:
        outer, middle = swap(codes_v[RANK:], "seq", 1), inner(codes_v[RANK:])
        lows = jnp.where(seq_index == 2, middle[RANK:], outer[RANK:]).astype(BF16)[None]
        back = jnp.where(seq_index == 1, middle[:RANK], 0.0)
        code_v = code_v + jnp.where(seq_index % 2 == 0, outer[:RANK], back)
    else:
        low_v = low[RANK:].astype(BF16)
        lows = jnp.stack([shift(low_v, d) for d in range(blocks, 0, -1)])
        for b, d in enumerate(range(blocks, 0, -1)):
            code_v = code_v + shift(codes_v[(b + 1) * RANK : (b + 2) * RANK], -d)
    code_q, up = call(
        functools.partial(grads_kernel, count, send, blocks, heads),
        [((RANK, tok), F32), ((RANK, (heads + 1) * HEAD), BF16 if direct else F32)],
        [pltpu.VMEM((heads * HEAD, tok), BF16)],
        cost=24 << 20,
    )(low, lows, packs, o, w, dp, kt, kt_far, dv, cos_t, sin_t, wq, wv)
    if not direct:
        dlow = sum_fsdp(jnp.concatenate([code_q, code_v], axis=0)).astype(BF16)
        (down,) = call(down_kernel, [((2 * RANK, wide), F32)])(dlow, x)
        down, up = lax.psum((down, up), "seq")
        return down.T, up[:, : heads * HEAD], up[:, heads * HEAD :]

    codes = jnp.concatenate([code_q, code_v], axis=0)
    near_up = swap(up, "seq", 1)
    both, part_q, part_v = call(
        partial_kernel, [((2 * RANK, wide), BF16), ((RANK, wide), BF16), ((RANK, wide), BF16)]
    )(sum_fsdp(codes).astype(BF16), x)
    (send_q,) = call(combine_kernel, [((RANK, wide + up.shape[1]), BF16)])(part_q, up, near_up)
    send_q, late = lax.optimization_barrier((send_q, both))
    value_two = swap(part_v, "seq", 2)
    value_three = swap(value_two, "seq", 1)
    query_two, query_three = swap(send_q, "seq", 2), swap(part_q, "seq", 3)
    ones = [swap(late[i * RANK : (i + 1) * RANK], "seq", 1) for i in range(2)]
    down, up_q, up_v = call(
        final_kernel,
        [((2 * RANK, wide), F32), ((RANK, heads * HEAD), F32), ((RANK, HEAD), F32)],
    )(both, send_q, query_two, query_three, value_two, value_three, *ones)
    return down.T, up_q, up_v


def solution(mesh):
    rows = ("groups", "seq")
    in_specs = (
        P(rows, "fsdp"),
        P(rows, "fsdp"),
        P(rows, "fsdp"),
        P(rows, "fsdp"),
        P(rows, "fsdp"),
        P(rows),
        P("fsdp", None),
        P(None, "fsdp"),
        P(None, "fsdp"),
    )
    out_specs = (P(("groups", "fsdp"), None), P("groups", "fsdp"), P("groups", "fsdp"))
    return jax.shard_map(body, mesh=mesh, in_specs=in_specs, out_specs=out_specs, check_vma=False)
```

```python
import functools
import math

import jax
import jax.numpy as jnp
from jax import lax
from jax.experimental import pallas as pl
from jax.experimental.pallas import tpu as pltpu
from jax.sharding import PartitionSpec as P

HEAD = 128
HALF = HEAD // 2
RANK = 16
SCALE = 2.0
ROPE_BASE = 500000.0
NEG_FILL = -1e30
INV_ROOT = 1.0 / math.sqrt(HEAD)
F32 = jnp.float32
BF16 = jnp.bfloat16
LIMIT = 40 * 1024 * 1024
FULL = 55080 * 1024


def dot(left, right, left_dim, right_dim):
    return lax.dot_general(
        left,
        right,
        (((left_dim,), (right_dim,)), ((), ())),
        preferred_element_type=F32,
    )


def call(kernel, out_shapes, scratch=(), limit=LIMIT, cost=1, **specs):
    return pl.pallas_call(
        kernel,
        out_shape=[jax.ShapeDtypeStruct(s, d) for s, d in out_shapes],
        **specs,
        scratch_shapes=list(scratch),
        compiler_params=pltpu.CompilerParams(vmem_limit_bytes=limit),
        cost_estimate=pl.CostEstimate(flops=cost, bytes_accessed=cost, transcendentals=0),
    )


def lowrank_kernel(send, *refs):
    sources, (part_ref, tails_ref, k_ref, v_ref, wq_ref) = refs[:5], refs[5:10]
    x_ref, a_ref, sems = refs[10:]
    targets = (x_ref, a_ref, k_ref, v_ref, wq_ref)
    copies = []
    for i, (source, target) in enumerate(zip(sources, targets)):
        copies.append(pltpu.make_async_copy(source, target, sems.at[i]))
        copies[-1].start()
    for copy in copies:
        copy.wait()
    part_ref[...] = dot(a_ref[...], x_ref[...], 1, 1)
    tok = k_ref.shape[0]
    tails_ref[0:send] = k_ref[tok - send :]
    tails_ref[send:] = v_ref[tok - send :]


def rotate_rows(u, cos, sin):
    return u * cos + pltpu.roll(u, HALF, 1) * sin


def wide_tables(cos, sin):
    return jnp.concatenate([cos, cos], axis=1), jnp.concatenate([-sin, sin], axis=1)


def column(row, tok):
    return jnp.broadcast_to(row, (tok, tok)).T


def lanes(array, count):
    return jnp.concatenate([array] * count, axis=1)


def head_rows(ref, first, count):
    parts = [ref[:, h * HEAD : (h + 1) * HEAD] for h in range(first, first + count)]
    return jnp.concatenate(parts, axis=0)


def split_dot(left, right, left_dim, right_dim):
    high = right.astype(BF16)
    rest = (right - high.astype(F32)).astype(BF16)
    return dot(left, high, left_dim, right_dim) + dot(left, rest, left_dim, right_dim)


def by_token(array, send, tok):
    if send == tok:
        return array
    gap = jnp.zeros((tok - send, array.shape[1]), array.dtype)
    return jnp.concatenate([array[:tok], gap, array[tok:]], axis=0)


def project_kernel(
    count, heads,
    low_ref, q_ref, k_ref, seg_ref, cos_ref, sin_ref, wq_ref,
    qr_ref, kt_ref, s_ref, cost_ref, sint_ref,
):
    tok = q_ref.shape[0]
    low = low_ref[...].astype(BF16)
    cost_ref[...] = cos_ref[...].T
    sint_ref[...] = sin_ref[...].T
    cos, sin = wide_tables(cos_ref[...], sin_ref[...])
    keys = rotate_rows(k_ref[...].astype(F32), cos, sin)
    kt_ref[...] = keys.T.astype(BF16)
    keys = keys.astype(BF16)
    seg_here = seg_ref[...].astype(F32)[0:1]
    key = lax.broadcasted_iota(jnp.int32, (tok, tok), 0)
    query = lax.broadcasted_iota(jnp.int32, (tok, tok), 1)
    allowed = (key <= query) & (column(seg_here, tok) == seg_here)
    bias = lanes(jnp.where(allowed, 0.0, NEG_FILL), count)
    q0 = q_ref[...].astype(F32) + SCALE * dot(low[:RANK], wq_ref[...], 0, 0)
    for g in range(0, heads, count):
        cut = slice(g * tok, (g + count) * tok)
        parts = [q0[:, h * HEAD : (h + 1) * HEAD] for h in range(g, g + count)]
        qr = jnp.concatenate([rotate_rows(u, cos, sin).astype(BF16) for u in parts], axis=0)
        qr_ref[cut] = qr
        s_ref[:, cut] = dot(keys, qr, 1, 1) * INV_ROOT + bias


def own_kernel(count, heads, low_ref, v_ref, o_ref, wv_ref, dp_ref):
    low_v = low_ref[RANK:].astype(BF16)
    vals = (v_ref[...].astype(F32) + dot(low_v, wv_ref[...], 0, 0)).astype(BF16)
    tok = o_ref.shape[0]
    for g in range(0, heads, count):
        cut = slice(g * tok, (g + count) * tok)
        dp_ref[:, cut] = dot(vals, head_rows(o_ref, g, count), 1, 1)


def softmax_kernel(
    count, send, blocks, heads,
    qr_ref, s_ref, o_ref, seg_ref, pack_ref, base_ref, cos_ref, sin_ref, wv_ref, low_ref,
    w_ref, kt_ref, dv_ref, code_ref,
):
    tok = o_ref.shape[0]
    halo = send * blocks
    cos, sin = wide_tables(cos_ref[...], sin_ref[...])
    keys = jnp.concatenate([pack_ref[b, 0:send] for b in range(blocks)], axis=0)
    keys = rotate_rows(keys.astype(F32), cos, sin)
    kt_ref[...] = keys.T.astype(BF16)
    keys = keys.astype(BF16)
    seg_here = seg_ref[...].astype(F32)[0:1]
    cols = []
    for b in range(blocks):
        row = pack_ref[b, 2 * send :].astype(F32)[0:1]
        cols.append(column(row, tok)[tok - send :])
    seg_col = jnp.concatenate(cols, axis=0)
    offset = lax.broadcasted_iota(jnp.int32, (halo, tok), 0)
    allowed = (offset + base_ref[0] >= halo) & (seg_col == seg_here)
    bias = lanes(jnp.where(allowed, 0.0, NEG_FILL), count)
    dv = jnp.zeros((tok + halo, HEAD), F32)
    for g in range(0, heads, count):
        cut = slice(g * tok, (g + count) * tok)
        far = dot(keys, qr_ref[cut], 1, 1) * INV_ROOT + bias
        s = jnp.concatenate([s_ref[:, cut], far], axis=0)
        e = jnp.exp(s - jnp.max(s, axis=0, keepdims=True))
        w = e * (1.0 / jnp.sum(e, axis=0, keepdims=True))
        w_ref[:, cut] = w
        dv = dv + dot(w.astype(BF16), head_rows(o_ref, g, count), 1, 0)
    dv_ref[...] = dv
    codes = split_dot(wv_ref[...], by_token(dv, send, tok), 1, 1)
    for b in range(blocks + 1):
        code_ref[b * RANK : (b + 1) * RANK] = codes[:, b * tok : (b + 1) * tok]
    code_ref[(blocks + 1) * RANK :] = low_ref[RANK:].astype(BF16).astype(F32)


def grads_kernel(
    count, send, blocks, heads,
    low_ref, far_ref, pack_ref, o_ref, w_ref, dp_ref, kt_ref, kth_ref, dv_ref, cost_ref, sint_ref, wq_ref, wv_ref,
    code_ref, up_ref, qg_ref,
):
    tok = o_ref.shape[0]
    low = low_ref[...].astype(BF16)
    wv = wv_ref[...]
    vals = []
    for b in range(blocks):
        rows = pack_ref[b, send : 2 * send].astype(F32)
        add = dot(far_ref[b], wv, 0, 0)[tok - send :]
        vals.append((rows + add).astype(BF16))
    vals = jnp.concatenate(vals, axis=0)
    kt = jnp.concatenate([kt_ref[...], kth_ref[...]], axis=1)
    cos, sin = lanes(cost_ref[...], count), lanes(sint_ref[...], count)
    for g in range(0, heads, count):
        cut = slice(g * tok, (g + count) * tok)
        far = dot(vals, head_rows(o_ref, g, count), 1, 1)
        dp = jnp.concatenate([dp_ref[:, cut], far], axis=0)
        w = w_ref[:, cut]
        delta = jnp.sum(w * dp, axis=0, keepdims=True)
        ds = (w * (dp - delta) * INV_ROOT).astype(BF16)
        dq = dot(kt, ds, 1, 0)
        first, second = dq[:HALF], dq[HALF:]
        first, second = first * cos + second * sin, second * cos - first * sin
        turned = jnp.concatenate([first.astype(BF16), second.astype(BF16)], axis=0)
        for h in range(count):
            qg_ref[(g + h) * HEAD : (g + h + 1) * HEAD] = turned[:, h * tok : (h + 1) * tok]
    qg = qg_ref[...]
    code_ref[...] = SCALE * dot(wq_ref[...], qg, 1, 0)
    up_ref[:, : heads * HEAD] = (SCALE * dot(low[:RANK], qg, 1, 1)).astype(up_ref.dtype)
    codes = jnp.concatenate([low[RANK:]] + [far_ref[b] for b in range(blocks)], axis=1)
    up_v = SCALE * split_dot(codes, by_token(dv_ref[...], send, tok), 1, 0)
    up_ref[:, heads * HEAD :] = up_v.astype(up_ref.dtype)


def down_kernel(dl_ref, x_ref, part_ref):
    part_ref[...] = dot(dl_ref[...], x_ref[...], 1, 0)


def partial_kernel(own_ref, x_ref, both_ref, query_ref, value_ref):
    part = dot(own_ref[...], x_ref[...], 1, 0).astype(BF16)
    both_ref[...] = part
    query_ref[...] = part[:RANK]
    value_ref[...] = part[RANK:]


def combine_kernel(query_ref, up_ref, near_ref, send_ref):
    wide = query_ref.shape[1]
    send_ref[:, :wide] = query_ref[...]
    send_ref[:, wide:] = (up_ref[...].astype(F32) + near_ref[...].astype(F32)).astype(BF16)


def final_kernel(
    mine_ref, query_ref, query_two_ref, query_three_ref, value_two_ref, value_three_ref, query_one_ref, value_one_ref,
    down_ref, upq_ref, upv_ref,
):
    wide, size = down_ref.shape[1], upq_ref.shape[1]
    one = jnp.concatenate([query_one_ref[...], value_one_ref[...]], axis=0)
    near = mine_ref[...].astype(F32) + one.astype(F32)
    far = query_two_ref[:, :wide].astype(F32) + query_three_ref[...].astype(F32)
    down_ref[:RANK] = near[:RANK] + far
    far = value_two_ref[...].astype(F32) + value_three_ref[...].astype(F32)
    down_ref[RANK:] = near[RANK:] + far
    up = query_ref[:, wide:].astype(F32) + query_two_ref[:, wide:].astype(F32)
    upq_ref[...] = up[:, :size]
    upv_ref[...] = up[:, size:]


def body(x, q, k, v, o, segment, a, wq, wv):
    tok, wide = x.shape
    seq_count = lax.axis_size("seq")
    fsdp_count = lax.axis_size("fsdp")
    seq_index = lax.axis_index("seq")
    heads = q.shape[1] // HEAD
    longest = tok * seq_count // 8
    blocks = -(-longest // tok)
    send = longest if blocks == 1 else tok
    halo = blocks * send
    keys = halo + tok
    direct = seq_count == 4 and fsdp_count == 4

    def swap(array, axis, bit):
        size = lax.axis_size(axis)
        return lax.ppermute(array, axis, [(i, i ^ bit) for i in range(size)])

    def shift(array, by):
        moves = [(i, (i + by) % seq_count) for i in range(seq_count)]
        return lax.ppermute(array, "seq", moves)

    def inner(array):
        moves = []
        for i in range(seq_count):
            for f in range(fsdp_count):
                to, flip = (3 - i, 0) if i in (1, 2) else (i, 2)
                moves.append((i * fsdp_count + f, to * fsdp_count + (f ^ flip)))
        return lax.ppermute(array, ("seq", "fsdp"), moves)

    def sum_fsdp(array):
        if fsdp_count != 4:
            return lax.psum(array, "fsdp")
        one, two, three = [swap(array, "fsdp", bit) for bit in (1, 2, 3)]
        return (array + one) + (two + three)

    seg_row = segment.reshape(1, tok)
    part, tails, k, v, wq = call(
        functools.partial(lowrank_kernel, send),
        [
            ((2 * RANK, tok), F32),
            ((2 * send, HEAD), BF16),
            ((tok, HEAD), BF16),
            ((tok, HEAD), BF16),
            (wq.shape, BF16),
        ],
        [
            pltpu.VMEM((tok, wide), BF16),
            pltpu.VMEM((2 * RANK, wide), BF16),
            pltpu.SemaphoreType.DMA((5,)),
        ],
        limit=FULL,
        in_specs=[pl.BlockSpec(memory_space=pltpu.HBM)] * 5,
    )(x, a.T, k, v, wq)
    seg_rows = jnp.broadcast_to(seg_row, (16, tok)).astype(BF16)
    pack = jnp.concatenate([tails, seg_rows], axis=0)
    wv = wv * SCALE
    start = seq_index * tok
    base = start.reshape(1).astype(jnp.int32)
    freqs = ROPE_BASE ** (-(2.0 * jnp.arange(HALF, dtype=F32)) / HEAD)
    positions = (start - halo + jnp.arange(keys, dtype=jnp.int32)).astype(F32)
    angles = positions[:, None] * freqs[None, :]
    cos, sin = jnp.cos(angles), jnp.sin(angles)
    packs = jnp.stack([shift(pack, d) for d in range(blocks, 0, -1)])
    low = sum_fsdp(part)
    low, cos, sin, wv = lax.optimization_barrier((low, cos, sin, wv))
    count = heads if blocks == 1 else 1
    qr, kt, s, cos_t, sin_t = call(
        functools.partial(project_kernel, count, heads),
        [
            ((heads * tok, HEAD), BF16),
            ((HEAD, tok), BF16),
            ((tok, heads * tok), F32),
            ((HALF, tok), F32),
            ((HALF, tok), F32),
        ],
        cost=3 << 20,
    )(low, q, k, seg_rows, cos[halo:], sin[halo:], wq)
    specs = [pl.BlockSpec(memory_space=pltpu.VMEM)] * 10
    specs[5] = pl.BlockSpec(memory_space=pltpu.SMEM)
    w, kt_far, dv, codes_v = call(
        functools.partial(softmax_kernel, count, send, blocks, heads),
        [
            ((keys, heads * tok), F32),
            ((HEAD, halo), BF16),
            ((keys, HEAD), F32),
            (((blocks + 2) * RANK, tok), F32),
        ],
        in_specs=specs,
        cost=5 << 20,
    )(qr, s, o, seg_rows, packs, base, cos[:halo], sin[:halo], wv, low)
    code_v = codes_v[:RANK]
    low_v, dv = lax.optimization_barrier((low, dv))
    (dp,) = call(
        functools.partial(own_kernel, count, heads), [((tok, heads * tok), F32)], cost=24 << 20
    )(low_v, v, o, wv)
    if direct:
        outer, middle = swap(codes_v[RANK:], "seq", 1), inner(codes_v[RANK:])
        lows = jnp.where(seq_index == 2, middle[RANK:], outer[RANK:]).astype(BF16)[None]
        back = jnp.where(seq_index == 1, middle[:RANK], 0.0)
        code_v = code_v + jnp.where(seq_index % 2 == 0, outer[:RANK], back)
    else:
        low_v = low[RANK:].astype(BF16)
        lows = jnp.stack([shift(low_v, d) for d in range(blocks, 0, -1)])
        for b, d in enumerate(range(blocks, 0, -1)):
            code_v = code_v + shift(codes_v[(b + 1) * RANK : (b + 2) * RANK], -d)
    code_q, up = call(
        functools.partial(grads_kernel, count, send, blocks, heads),
        [((RANK, tok), F32), ((RANK, (heads + 1) * HEAD), BF16 if direct else F32)],
        [pltpu.VMEM((heads * HEAD, tok), BF16)],
        cost=24 << 20,
    )(low, lows, packs, o, w, dp, kt, kt_far, dv, cos_t, sin_t, wq, wv)
    if not direct:
        dlow = sum_fsdp(jnp.concatenate([code_q, code_v], axis=0)).astype(BF16)
        (down,) = call(down_kernel, [((2 * RANK, wide), F32)])(dlow, x)
        down, up = lax.psum((down, up), "seq")
        return down.T, up[:, : heads * HEAD], up[:, heads * HEAD :]

    codes = jnp.concatenate([code_q, code_v], axis=0)
    near_up = swap(up, "seq", 1)
    both, part_q, part_v = call(
        partial_kernel, [((2 * RANK, wide), BF16), ((RANK, wide), BF16), ((RANK, wide), BF16)]
    )(sum_fsdp(codes).astype(BF16), x)
    (send_q,) = call(combine_kernel, [((RANK, wide + up.shape[1]), BF16)])(part_q, up, near_up)
    value_two = swap(part_v, "seq", 2)
    value_two, late = lax.optimization_barrier((value_two, both))
    value_three = swap(value_two, "seq", 1)
    query_two, query_three = swap(send_q, "seq", 2), swap(part_q, "seq", 3)
    ones = [swap(late[i * RANK : (i + 1) * RANK], "seq", 1) for i in range(2)]
    down, up_q, up_v = call(
        final_kernel,
        [((2 * RANK, wide), F32), ((RANK, heads * HEAD), F32), ((RANK, HEAD), F32)],
    )(both, send_q, query_two, query_three, value_two, value_three, *ones)
    return down.T, up_q, up_v


def solution(mesh):
    rows = ("groups", "seq")
    in_specs = (
        P(rows, "fsdp"),
        P(rows, "fsdp"),
        P(rows, "fsdp"),
        P(rows, "fsdp"),
        P(rows, "fsdp"),
        P(rows),
        P("fsdp", None),
        P(None, "fsdp"),
        P(None, "fsdp"),
    )
    out_specs = (P(("groups", "fsdp"), None), P("groups", "fsdp"), P("groups", "fsdp"))
    return jax.shard_map(body, mesh=mesh, in_specs=in_specs, out_specs=out_specs, check_vma=False)
```
